32 devices in a mesh: dp: 8 (over z, x), height: 4 (over y, core).
Axes of the slice: x: 2, y: 2, z: 4, core: 2. Of those that a mesh axis runs over, the one named last changes fastest.
Arguments:
- images: bfloat16 [48, 32, 32, 512], P('dp', 'height'), may hold values from -6 to 6
- size_group: int32 [48], P('dp'), may hold values from 0 to 2
- cotangent: bfloat16 [48, 16, 16, 1024], P('dp', 'height'), may hold values from -6 to 6
- reduce_one: bfloat16 [131072], P(('dp', 'height')), may hold values from -0.25 to 0.25
- split_one: bfloat16 [589824], P(('dp', 'height')), may hold values from -0.1875 to 0.1875
- squeeze_one: bfloat16 [32768], P(('dp', 'height')), may hold values from -0.375 to 0.375
- expand_one: bfloat16 [65536], P(('dp', 'height')), may hold values from -0.5 to 0.5
- output_one: bfloat16 [262144], P(('dp', 'height')), may hold values from -0.375 to 0.375
- shortcut: bfloat16 [524288], P(('dp', 'height')), may hold values from -0.25 to 0.25
- reduce_two: bfloat16 [262144], P(('dp', 'height')), may hold values from -0.1875 to 0.1875
- split_two: bfloat16 [589824], P(('dp', 'height')), may hold values from -0.1875 to 0.1875
- squeeze_two: bfloat16 [32768], P(('dp', 'height')), may hold values from -0.375 to 0.375
- expand_two: bfloat16 [65536], P(('dp', 'height')), may hold values from -0.5 to 0.5
- output_two: bfloat16 [262144], P(('dp', 'height')), may hold values from -0.375 to 0.375
- norm_gains: bfloat16 [4864], P(('dp', 'height')), may hold values from 0.099609375 to 1.8984375
- norm_shifts: bfloat16 [5888], P(('dp', 'height')), may hold values from -3 to 3
Outputs:
- layer_one: bfloat16 [48, 16, 16, 1024], P('dp', 'height')
- layer_two: bfloat16 [48, 16, 16, 1024], P('dp', 'height')
- grad_images: bfloat16 [48, 32, 32, 512], P('dp', 'height')
- grad_reduce_one: float32 [131072], P(('dp', 'height'))
- grad_split_one: float32 [589824], P(('dp', 'height'))
- grad_squeeze_one: float32 [32768], P(('dp', 'height'))
- grad_expand_one: float32 [65536], P(('dp', 'height'))
- grad_output_one: float32 [262144], P(('dp', 'height'))
- grad_shortcut: float32 [524288], P(('dp', 'height'))
- grad_reduce_two: float32 [262144], P(('dp', 'height'))
- grad_split_two: float32 [589824], P(('dp', 'height'))
- grad_squeeze_two: float32 [32768], P(('dp', 'height'))
- grad_expand_two: float32 [65536], P(('dp', 'height'))
- grad_output_two: float32 [262144], P(('dp', 'height'))
- grad_gains: float32 [4864], P(('dp', 'height'))
- grad_shifts: float32 [5888], P(('dp', 'height'))
The draws below stay inside these ranges and needn't reach their ends.
Inputs may be any that keep to these rules, and one draw needn't show every extreme that they name: `size_group`: size group of each image: its valid grid is 32 - 4 * (2 - group) cells on a side, in the top-left corner; the other cells are ignored.
All inputs are finite; a program needn't handle non-finite values.
Results may differ from the reference program's by a relative error of at most 0.019.
Values may be sent and summed in bfloat16 or wider, within the bound.
A program may use at most 128 MiB of HBM per device.

```python
from functools import partial
import jax
import jax.numpy as jnp
from jax import lax

C_IN = 512
C_MID = 256
C_ATT = 128
C_OUT = 1024
H = 32
STEP = 4
MICRO = 2
MB = 3
IMAGES = 48
GAIN_LEN = 4864
SHIFT_LEN = 5888
N_DP = 8


def touch_ends(values, stream_key, least, largest):
    longest = values.shape.index(max(values.shape))
    spots = []
    for shift in (0, 1):
        where = [jax.random.randint(jax.random.fold_in(stream_key, axis), (), 0, length) for axis, length in enumerate(values.shape)]
        where[longest] = (where[longest] + shift) % values.shape[longest]
        spots.append(tuple(where))
    return values.at[spots[0]].set(least).at[spots[1]].set(largest)


def level_of(key, dims, cuts, least, high):
    loudness = 1.0
    for axis_at, blocks in cuts:
        draws = jax.random.uniform(jax.random.fold_in(jax.random.fold_in(key, 6), axis_at), (blocks,), jnp.float32, least / len(cuts), high / len(cuts))
        loudness = loudness * jnp.repeat(jnp.exp(draws), dims[axis_at] // blocks).reshape((-1,) + (1,) * (len(dims) - 1 - axis_at))
    return loudness


def normal_values(stream_key, shape, width, limit, shards=(), kind=jnp.bfloat16):
    result = jax.random.normal(stream_key, shape, jnp.float32) * width
    if len(shards) > 0:
        result = level_of(stream_key, shape, shards, -0.22, 0.18) * result
    return jnp.clip(result, min=-limit, max=limit).astype(kind)


def setup_inputs(seed: int = 0) -> dict:
    keys = jax.random.split(jax.random.key(seed), 17)
    return {
        "images": normal_values(keys[0], (IMAGES, H, H, C_IN), 1.0, 6.0, ((0, 8), (1, 4))),
        "size_group": touch_ends(jax.random.randint(keys[1], (IMAGES,), 0, 3), jax.random.fold_in(keys[1], 1), 0, 2).astype(jnp.int32),
        "cotangent": normal_values(keys[2], (IMAGES, H // 2, H // 2, C_OUT), 1.0, 6.0, ((0, 8), (1, 4))),
        "reduce_one": normal_values(keys[3], (C_IN * C_MID,), C_IN ** -0.5, 0.25, ((0, 32),)),
        "split_one": normal_values(keys[4], (9 * C_MID * C_MID,), (9 * C_MID // 2) ** -0.5, 0.1875, ((0, 32),)),
        "squeeze_one": normal_values(keys[5], (C_MID * C_ATT,), C_MID ** -0.5, 0.375, ((0, 32),)),
        "expand_one": normal_values(keys[6], (2 * C_ATT * C_MID,), C_ATT ** -0.5, 0.5, ((0, 32),)),
        "output_one": normal_values(keys[7], (C_MID * C_OUT,), C_MID ** -0.5, 0.375, ((0, 32),)),
        "shortcut": normal_values(keys[8], (C_IN * C_OUT,), C_IN ** -0.5, 0.25, ((0, 32),)),
        "reduce_two": normal_values(keys[9], (C_OUT * C_MID,), C_OUT ** -0.5, 0.1875, ((0, 32),)),
        "split_two": normal_values(keys[10], (9 * C_MID * C_MID,), (9 * C_MID // 2) ** -0.5, 0.1875, ((0, 32),)),
        "squeeze_two": normal_values(keys[11], (C_MID * C_ATT,), C_MID ** -0.5, 0.375, ((0, 32),)),
        "expand_two": normal_values(keys[12], (2 * C_ATT * C_MID,), C_ATT ** -0.5, 0.5, ((0, 32),)),
        "output_two": normal_values(keys[13], (C_MID * C_OUT,), C_MID ** -0.5, 0.375, ((0, 32),)),
        "norm_gains": jnp.clip(1.0 + 0.18 * jax.random.normal(keys[14], (GAIN_LEN,), jnp.float32), 0.099609375, 1.8984375).astype(jnp.bfloat16),
        "norm_shifts": normal_values(keys[15], (SHIFT_LEN,), 0.5, 3.0, ((0, 32),)),
    }


EPSILON = 1e-05
HIGHEST = lax.Precision.HIGHEST

@jax.custom_vjp
def low(v):
    return lax.optimization_barrier(v.astype(jnp.bfloat16)).astype(jnp.float32)

@jax.custom_vjp
def low_back(v):
    return v

def low_keep(v):
    return (low(v), None)

def low_pass(kept, grad):
    return (grad,)

def back_keep(v):
    return (v, None)

def back_low(kept, grad):
    return (low(grad),)
low.defvjp(low_keep, low_pass)
low_back.defvjp(back_keep, back_low)

def offsets():
    first = {'reduce': 0, 'split': C_MID, 'attend': 3 * C_MID, 'output': 3 * C_MID + C_ATT, 'shortcut': 3 * C_MID + C_ATT + C_OUT}
    base = 3 * C_MID + C_ATT + 2 * C_OUT
    second = {'reduce': base, 'split': base + C_MID, 'attend': base + 3 * C_MID, 'output': base + 3 * C_MID + C_ATT}
    total = base + 3 * C_MID + C_ATT + C_OUT
    first['bias'] = total
    second['bias'] = total + 2 * C_MID
    return (first, second)

def segment(vector, start, length):
    return lax.slice_in_dim(vector, start, start + length)

def make_mask(valid_size, extent):
    coords = jnp.arange(extent, dtype=jnp.int32)
    inside = (coords[None, :, None] < valid_size[:, None, None]) & (coords[None, None, :] < valid_size[:, None, None])
    return inside.astype(jnp.float32)[..., None]

def batch_norm(values, weight_mask, gain, shift):
    count_sum = jnp.sum(weight_mask)
    centre = lax.optimization_barrier(jnp.sum(values * weight_mask, axis=(0, 1, 2))) / count_sum
    scaled = lax.rsqrt(lax.optimization_barrier(jnp.sum(values * values * weight_mask, axis=(0, 1, 2))) / count_sum - centre * centre + EPSILON)
    return gain * ((values - centre) * scaled) + shift

def image_norm(values, gain, shift):
    centre = lax.optimization_barrier(jnp.mean(values, axis=0))
    scaled = lax.rsqrt(lax.optimization_barrier(jnp.mean(values * values, axis=0)) - centre * centre + EPSILON)
    return gain * ((values - centre) * scaled) + shift

def project(values, matrix, inner, outer):
    return jnp.einsum('...i,ij->...j', values, matrix.reshape(inner, outer), precision=HIGHEST)

def grouped_conv(values, kernel):
    half_width = C_MID // 2
    weights = kernel.reshape(2, 3, 3, half_width, C_MID).transpose(1, 2, 3, 0, 4).reshape(3, 3, half_width, 2 * C_MID)
    return lax.conv_general_dilated(values, weights, (1, 1), ((1, 1), (1, 1)), dimension_numbers=('NHWC', 'HWIO', 'NHWC'), feature_group_count=2, precision=HIGHEST)

def splat(block_in, weight_mask, area, weights, gain_all, shift_all, place):
    reduce_w, split_w, squeeze_w, expand_w = weights
    channels = block_in.shape[-1]
    pre_one = low_back(project(block_in, reduce_w, channels, C_MID))
    act_one = low(jax.nn.silu(batch_norm(pre_one, weight_mask, segment(gain_all, place['reduce'], C_MID), segment(shift_all, place['reduce'], C_MID))) * weight_mask)
    pre_two = low_back(grouped_conv(act_one, split_w))
    splits = jax.nn.silu(batch_norm(pre_two, weight_mask, segment(gain_all, place['split'], 2 * C_MID), segment(shift_all, place['split'], 2 * C_MID))) * weight_mask
    first_split = splits[..., :C_MID]
    second_split = splits[..., C_MID:]
    pooled = lax.optimization_barrier(jnp.sum(first_split + second_split, axis=(1, 2))) / area[:, None]
    pre_att = jnp.dot(pooled, squeeze_w.reshape(C_MID, C_ATT), precision=HIGHEST)
    hidden = jax.nn.silu(image_norm(pre_att, segment(gain_all, place['attend'], C_ATT), segment(shift_all, place['attend'], C_ATT)))
    logits = jnp.dot(hidden, expand_w.reshape(C_ATT, 2 * C_MID), precision=HIGHEST) + segment(shift_all, place['bias'], 2 * C_MID)
    attend = jax.nn.softmax(logits.reshape(-1, 2, C_MID), axis=1)
    return attend[:, 0, None, None, :] * first_split + attend[:, 1, None, None, :] * second_split

def forward(inputs, weights, gain_all, shift_all, inner_mask, outer_mask, inner_area, outer_area, grad_seed):
    reduce_a, split_a, squeeze_a, expand_a, output_a, short_a, reduce_b, split_b, squeeze_b, expand_b, output_b = weights
    first_place, second_place = offsets()
    count_images = inputs.shape[0]
    mixed_one = splat(inputs, inner_mask, inner_area, (reduce_a, split_a, squeeze_a, expand_a), gain_all, shift_all, first_place)
    pooled_one = low(lax.reduce_window(low(mixed_one), 0.0, lax.add, (1, 3, 3, 1), (1, 2, 2, 1), ((0, 0), (1, 1), (1, 1), (0, 0))) / 9.0)
    pre_out = low_back(project(pooled_one, output_a, C_MID, C_OUT))
    normed_out = batch_norm(pre_out, outer_mask, segment(gain_all, first_place['output'], C_OUT), segment(shift_all, first_place['output'], C_OUT))
    short_in = low(lax.optimization_barrier(jnp.mean(inputs.reshape(count_images, H // 2, 2, H // 2, 2, C_IN), axis=(2, 4))))
    pre_short = low_back(project(short_in, short_a, C_IN, C_OUT))
    normed_short = batch_norm(pre_short, outer_mask, segment(gain_all, first_place['shortcut'], C_OUT), segment(shift_all, first_place['shortcut'], C_OUT))
    layer_first = low(jax.nn.silu(normed_out + normed_short) * outer_mask)
    mixed_two = splat(layer_first, outer_mask, outer_area, (reduce_b, split_b, squeeze_b, expand_b), gain_all, shift_all, second_place)
    pre_two = low_back(project(low(mixed_two), output_b, C_MID, C_OUT))
    normed_two = batch_norm(pre_two, outer_mask, segment(gain_all, second_place['output'], C_OUT), segment(shift_all, second_place['output'], C_OUT))
    layer_second = jax.nn.silu(normed_two + layer_first) * outer_mask
    return (jnp.sum(layer_second * grad_seed), (layer_first, layer_second))

def reference(images, size_group, cotangent, reduce_one, split_one, squeeze_one, expand_one, output_one, shortcut, reduce_two, split_two, squeeze_two, expand_two, output_two, norm_gains, norm_shifts):
    weights = tuple((matrix.astype(jnp.float32) for matrix in (reduce_one, split_one, squeeze_one, expand_one, output_one, shortcut, reduce_two, split_two, squeeze_two, expand_two, output_two)))
    gain_all = norm_gains.astype(jnp.float32)
    shift_all = norm_shifts.astype(jnp.float32)
    valid_size = H - STEP * (2 - size_group)
    half_size = valid_size // 2
    inner_mask = make_mask(valid_size, H)
    outer_mask = make_mask(half_size, H // 2)
    inner_area = (valid_size * valid_size).astype(jnp.float32)
    outer_area = (half_size * half_size).astype(jnp.float32)

    def select(array, micro_index):
        grouped = array.reshape((N_DP, MICRO, MB) + array.shape[1:])[:, micro_index]
        return grouped.reshape((N_DP * MB,) + array.shape[1:])
    first_list = []
    second_list = []
    input_list = []
    weight_sums = None
    gain_sum = jnp.zeros(gain_all.shape, jnp.float32)
    shift_sum = jnp.zeros(shift_all.shape, jnp.float32)
    for micro_index in range(MICRO):
        function = partial(forward, inner_mask=select(inner_mask, micro_index), outer_mask=select(outer_mask, micro_index), inner_area=select(inner_area, micro_index), outer_area=select(outer_area, micro_index), grad_seed=select(cotangent, micro_index).astype(jnp.float32))
        loss_value, pullback, outputs = jax.vjp(function, select(images, micro_index).astype(jnp.float32), weights, gain_all, shift_all, has_aux=True)
        grad_inputs, grad_weights, grad_gain, grad_shift = pullback(jnp.ones((), jnp.float32))
        first_list.append(outputs[0])
        second_list.append(outputs[1])
        input_list.append(grad_inputs)
        if weight_sums is None:
            weight_sums = list(grad_weights)
        else:
            weight_sums = [total + extra for total, extra in zip(weight_sums, grad_weights)]
        gain_sum = gain_sum + grad_gain
        shift_sum = shift_sum + grad_shift

    def assemble(pieces):
        tail = pieces[0].shape[1:]
        stacked = jnp.stack([piece.reshape((N_DP, MB) + tail) for piece in pieces], axis=1)
        return stacked.reshape((N_DP * MICRO * MB,) + tail)
    return (assemble(first_list).astype(jnp.bfloat16), assemble(second_list).astype(jnp.bfloat16), assemble(input_list).astype(jnp.bfloat16), weight_sums[0], weight_sums[1], weight_sums[2], weight_sums[3], weight_sums[4], weight_sums[5], weight_sums[6], weight_sums[7], weight_sums[8], weight_sums[9], weight_sums[10], gain_sum, shift_sum)
```

```python
import functools
import types

import jax
import jax.numpy as jnp
from jax import lax
from jax.experimental import pallas as pl
from jax.experimental.pallas import tpu as pltpu
from jax.sharding import PartitionSpec as P

C_IN = 512
C_MID = 256
C_ATT = 128
C_OUT = 1024
H = 32
STEP = 4
MICRO = 2
MB = 3

EPSILON = 1e-05
HIGHEST = lax.Precision.HIGHEST
FLOAT = jnp.float32
BFLOAT = jnp.bfloat16
MESH = pl.DeviceIdType.MESH
LANES = 128
NIM = MICRO * MB
NN = (((1,), (0,)), ((), ()))
NT = (((1,), (1,)), ((), ()))
TN = (((0,), (0,)), ((), ()))


class Names:
    def __getattr__(self, name):
        return name


tag = Names()

SHAPES = dict(
    r1=(C_IN, C_MID),
    s1=(9 * C_MID, C_MID),
    q1=(C_MID, C_ATT),
    e1=(C_ATT, 2 * C_MID),
    o1=(C_MID, C_OUT),
    sh=(C_IN, C_OUT),
    r2=(C_OUT, C_MID),
    s2=(9 * C_MID, C_MID),
    q2=(C_MID, C_ATT),
    e2=(C_ATT, 2 * C_MID),
    o2=(C_MID, C_OUT),
)

HEIGHT, DP, ALL = range(3)
SYNCS = dict(
    n1=(16, C_MID // 2, ALL),
    n2=(8, C_MID, ALL),
    gap=(8, C_MID, HEIGHT),
    na=(8, C_ATT, DP),
    no=(16, C_OUT // 2, ALL),
    n1b=(8, C_MID // 2, ALL),
    n2b=(8, C_MID, ALL),
    gapb=(8, C_MID, HEIGHT),
    nab=(8, C_ATT, DP),
    nob=(8, C_OUT // 2, ALL),
    dnob=(8, C_OUT // 2, ALL),
    dattb=(8, 2 * C_MID, HEIGHT),
    dnab=(8, C_ATT, DP),
    dn2b=(8, C_MID, ALL),
    dn1b=(8, C_MID // 2, ALL),
    dno=(16, C_OUT // 2, ALL),
    datt=(8, 2 * C_MID, HEIGHT),
    dna=(8, C_ATT, DP),
    dn2=(8, C_MID, ALL),
    dn1=(16, C_MID // 2, ALL),
)
SEMAPHORES = 256
SMALL = dict(e2=0, q=16, e1=32)


def offsets():
    first = types.SimpleNamespace(
        reduce=0,
        split=C_MID,
        attend=3 * C_MID,
        output=3 * C_MID + C_ATT,
        shortcut=3 * C_MID + C_ATT + C_OUT,
    )
    base = 3 * C_MID + C_ATT + 2 * C_OUT
    second = types.SimpleNamespace(
        reduce=base,
        split=base + C_MID,
        attend=base + 3 * C_MID,
        output=base + 3 * C_MID + C_ATT,
    )
    total = base + 3 * C_MID + C_ATT + C_OUT
    first.bias = total
    second.bias = total + 2 * C_MID
    return (first, second)


GAIN_LEN = 6 * C_MID + 2 * C_ATT + 3 * C_OUT
SHIFT_LEN = GAIN_LEN + 4 * C_MID
GAIN_ROWS = 48
SHIFT_ROWS = 56


def stage_sizes(kind, nd, nh):
    if kind == HEIGHT:
        return (nh,)
    along = (nd,) if nd <= 8 else (8, nd // 8)
    return along if kind == DP else (nh,) + along


def row_table(per_device):
    table = {}
    at = 0
    parts = dict(
        r1=per_device[tag.r1],
        gs=16,
        s1=per_device[tag.s1],
        q=per_device[tag.q1] + per_device[tag.q2],
        e1=per_device[tag.e1],
        e2=per_device[tag.e2],
        o1=per_device[tag.o1],
        sh=per_device[tag.sh],
        r2=per_device[tag.r2],
        s2=per_device[tag.s2],
        o2=per_device[tag.o2],
    )
    for name, count in parts.items():
        table[name] = (at, count)
        at += count
    return table, at


def dot(left, right, dims=NN):
    return lax.dot_general(left, right, dims, preferred_element_type=FLOAT)


def exact(left, right, dims=NN):
    return lax.dot_general(left, right, dims, preferred_element_type=FLOAT, precision=HIGHEST)


def sigmoid(values):
    return 0.5 * jnp.tanh(0.5 * values) + 0.5


def slope_of(values):
    logistic = sigmoid(values)
    return logistic * (1.0 + values * (1.0 - logistic))


def widen(part, columns):
    return jnp.concatenate([part] * (columns // LANES), axis=1)


def fold(values):
    rows, columns = values.shape
    return jnp.sum(values.reshape(rows // 8, 8, columns), axis=0)


def iota(shape, axis):
    return lax.broadcasted_iota(jnp.int32, shape, axis)


def ones_where(condition, kind=BFLOAT):
    return jnp.where(condition, 1.0, 0.0).astype(FLOAT).astype(kind)


def shuffle(count, rows, blocks, back=False):
    new = iota((count, count), 1 if back else 0)
    old = iota((count, count), 0 if back else 1)
    hit = None
    for block in range(blocks):
        same = old == blocks * new - blocks * block * rows + block
        hit = same if hit is None else hit | same
    return hit


def kernel(cfg, names, *refs):
    R = types.SimpleNamespace(**dict(zip(names, refs)))
    nd, nh, inside = cfg.nd, cfg.nh, cfg.inside
    d, h = lax.axis_index(tag.dp), lax.axis_index(tag.height)
    first, second = offsets()
    used = [0]
    late = []
    share = 1.0 if inside else 1.0 / nh

    def new_sem():
        used[0] += 1
        assert used[0] <= SEMAPHORES
        return R.sem.at[used[0] - 1]

    def remote(source, target, send, receive, device):
        return pltpu.make_async_remote_copy(
            src_ref=source,
            dst_ref=target,
            send_sem=send,
            recv_sem=receive,
            device_id=device,
            device_id_type=MESH,
        )

    def wait_for(ref, sem):
        pltpu.make_async_copy(ref, ref, sem).wait()

    high = nd // 8 if nd > 8 else 1
    dp_low = (nd if nd <= 8 else 8, lax.div(d, high), lambda q: (q * high + lax.rem(d, high), h))
    dp_high = (high, lax.rem(d, high), lambda q: (lax.div(d, high) * high + q, h))
    dims_of = {
        HEIGHT: [(nh, h, lambda q: (d, q))],
        DP: [dp_low] + ([dp_high] if high > 1 else []),
    }
    dims_of[ALL] = dims_of[HEIGHT] + dims_of[DP]

    class Exchange:
        def __init__(self, name):
            self.stages = dims_of[SYNCS[name][2]]
            self.bufs = [getattr(R, "sy_" + name + str(k)) for k in range(len(self.stages))]

        def slot(self):
            return self.bufs[0].at[self.stages[0][1]]

        def send(self, stage):
            count, me, peer = self.stages[stage]
            buf = self.bufs[stage]
            send, self.receive = new_sem(), new_sem()
            for step in range(1, count):
                to = lax.rem(me + step, count)
                remote(buf.at[me], buf.at[me], send, self.receive, peer(to)).start()
            late.append(lambda: wait_for(buf.at[pl.ds(0, count - 1)], send))

        def start(self):
            self.send(0)

        def finish(self):
            total = None
            for stage, (count, me, _) in enumerate(self.stages):
                buf = self.bufs[stage]
                if total is not None:
                    buf[me] = total
                    self.send(stage)
                wait_for(buf.at[pl.ds(0, count - 1)], self.receive)
                total = buf[0]
                for other in range(1, count):
                    total = total + buf[other]
            return total

    def put(exchange, vectors):
        slot = exchange.slot()
        half = vectors[0].shape[1] // 2
        for at, vector in enumerate(vectors):
            slot[2 * at : 2 * at + 1, :] = vector[:, :half]
            slot[2 * at + 1 : 2 * at + 2, :] = vector[:, half:]

    def take(total, at):
        return jnp.concatenate([total[2 * at : 2 * at + 1], total[2 * at + 1 : 2 * at + 2]], axis=1)

    if inside:
        Z, X, Y, C = nd // 2, 2, nh // 2, 2
        z, x = lax.div(d, 2), lax.rem(d, 2)
        y, c = lax.div(h, 2), lax.rem(h, 2)
        table = cfg.table
        G = R.pack

        class Gather:
            def __init__(self, start, stop):
                self.rows = pl.ds(start, stop - start)
                self.phase = -1
                self.sends = []

            def part(self):
                rows = self.rows
                return [
                    G.at[pl.ds(0, Z - 1), x, y, c, rows],
                    G.at[:, x, y, c, rows],
                    G.at[:, :, y, c, rows],
                    G.at[:, :, :, c, rows],
                ][self.phase]

            def step(self):
                if self.phase >= 0:
                    wait_for(self.part(), self.receive)
                self.phase += 1
                if self.phase == 4:
                    return
                send, self.receive = new_sem(), new_sem()
                part = self.part()
                if self.phase == 0:
                    own = G.at[z, x, y, c, self.rows]
                    for step in range(1, Z):
                        to = lax.rem(z + step, Z)
                        remote(own, own, send, self.receive, (to * 2 + x, h)).start()
                else:
                    to = [(z * 2 + 1 - x, h), (d, (1 - y) * 2 + c), (d, y * 2 + 1 - c)][self.phase - 1]
                    remote(part, part, send, self.receive, to).start()
                self.sends.append(lambda: wait_for(part, send))

            def finish(self):
                while self.phase < 4:
                    self.step()

            def sent(self):
                for wait in self.sends:
                    wait()

        class Scatter:
            def __init__(self, start, stop):
                self.rows = pl.ds(start, stop - start)
                self.count = stop - start
                self.phase = -1

            def begin(self, source, target, to):
                send, self.receive = new_sem(), new_sem()
                remote(source, target, send, self.receive, to).start()
                late.append(lambda: wait_for(source, send))

            def step(self):
                rows = self.rows
                self.phase += 1
                if self.phase == 0:
                    self.begin(G.at[:, :, :, 1 - c, rows], R.rc.at[:, :, :, rows], (d, y * 2 + 1 - c))
                elif self.phase == 1:
                    wait_for(R.rc.at[:, :, :, rows], self.receive)

                    def add(zz, _):
                        for xx in range(X):
                            for yy in range(Y):
                                mine = G[zz, xx, yy, c, rows].astype(FLOAT)
                                G[zz, xx, yy, c, rows] = (
                                    mine + R.rc[zz, xx, yy, rows].astype(FLOAT)
                                ).astype(BFLOAT)
                        return 0

                    lax.fori_loop(0, Z, add, 0)
                    self.begin(G.at[:, :, 1 - y, c, rows], R.ry.at[:, :, rows], (d, (1 - y) * 2 + c))
                elif self.phase == 2:
                    wait_for(R.ry.at[:, :, rows], self.receive)

                    def add(zz, _):
                        for xx in range(X):
                            mine = G[zz, xx, y, c, rows].astype(FLOAT)
                            G[zz, xx, y, c, rows] = (mine + R.ry[zz, xx, rows].astype(FLOAT)).astype(
                                BFLOAT
                            )
                        return 0

                    lax.fori_loop(0, Z, add, 0)
                    self.begin(G.at[:, 1 - x, y, c, rows], R.rx.at[:, rows], (z * 2 + 1 - x, h))
                elif self.phase == 3:
                    wait_for(R.rx.at[:, rows], self.receive)

                    def add(zz, _):
                        mine = G[zz, x, y, c, rows].astype(FLOAT)
                        G[zz, x, y, c, rows] = (mine + R.rx[zz, rows].astype(FLOAT)).astype(BFLOAT)
                        return 0

                    lax.fori_loop(0, Z, add, 0)
                    send, self.receive = new_sem(), new_sem()
                    for step in range(1, Z):
                        to = lax.rem(z + step, Z)
                        remote(
                            G.at[to, x, y, c, rows], R.rz.at[z, rows], send, self.receive, (to * 2 + x, h)
                        ).start()
                    late.append(lambda: wait_for(R.rz.at[pl.ds(0, Z - 1), rows], send))
                elif self.phase == 4:
                    wait_for(R.rz.at[pl.ds(0, Z - 1), rows], self.receive)

            def finish(self):
                while self.phase < 4:
                    self.step()

        def scattered(name):
            start, count = table[name]
            rows = pl.ds(start, count)
            total = G[z, x, y, c, rows].astype(FLOAT)
            for step in range(1, Z):
                total = total + R.rz[lax.rem(z + step, Z), rows].astype(FLOAT)
            return total

        def own_rows(name, values):
            start, count = table[name]
            G[z, x, y, c, start : start + count] = values.astype(BFLOAT)

        def per_dev(name):
            return SHAPES[name][0] // (nd * nh)

        def pack_shards():
            for name in (tag.r1, tag.s1, tag.o1, tag.sh, tag.r2, tag.s2, tag.o2):
                rows, blocks = per_dev(name), SHAPES[name][1] // LANES
                order = ones_where(shuffle(rows * blocks, rows, blocks))
                own_rows(name, dot(order, getattr(R, "a_" + name)[...]))
            own_rows(tag.gs, R.gs[...])
            own_rows(
                "q", jnp.concatenate([R.a_q1[...].astype(FLOAT), R.a_q2[...].astype(FLOAT)], axis=0)
            )
            own_rows(tag.e1, R.a_e1[...])
            own_rows(tag.e2, R.a_e2[...])

        def unpack_rows(name):
            rows, blocks = per_dev(name), SHAPES[name][1] // LANES
            start = table[name][0]
            full = getattr(R, "w_" + name)
            for block in range(blocks):
                at = start + block * rows
                full[:, block * LANES : (block + 1) * LANES] = G[
                    :, :, :, :, at : at + rows, :
                ].reshape(nd * nh * rows, LANES)

        def unpack_pairs(name):
            blocks = SHAPES[name][1] // LANES
            start = table[name][0]
            full = getattr(R, "w_" + name)
            for pair in range(blocks // 2):
                at = start + 16 * pair
                both = G[:, :, :, :, at : at + 16, :].astype(FLOAT).reshape(nd * nh, 2, 8, LANES)
                for one in range(2):
                    block = 2 * pair + one
                    full[:, block * LANES : (block + 1) * LANES] = (
                        both[:, one].reshape(nd * nh * 8, LANES).astype(BFLOAT)
                    )

        def unpack_split(name):
            start, count = table[name]
            full = getattr(R, "w_" + name)
            rows = per_dev(name)
            group = nh * rows

            def body(j, _):
                zz, xx = lax.div(j, 2), lax.rem(j, 2)
                part = G[zz, xx, :, :, start : start + count, :].astype(FLOAT)
                part = part.reshape(nh, 2, rows, LANES)
                at = pl.ds(pl.multiple_of(j * group, group), group)
                for block in range(2):
                    full[at, block * LANES : (block + 1) * LANES] = (
                        part[:, block].reshape(group, LANES).astype(BFLOAT)
                    )
                return 0

            lax.fori_loop(0, nd, body, 0)

        def unpack_attention():
            at = table[tag.q][0]
            both = G[:, :, :, :, at : at + 16, :].astype(FLOAT).reshape(nd * nh, 2, 8, LANES)
            R.w_q1[...] = both[:, 0].reshape(C_MID, C_ATT)
            R.w_q2[...] = both[:, 1].reshape(C_MID, C_ATT)
            for name in (tag.e1, tag.e2):
                at = table[name][0]
                part = G[:, :, :, :, at : at + 16, :].reshape(4 * C_ATT, LANES)
                for block in range(4):
                    pick = ones_where(
                        iota((C_ATT, 4 * C_ATT), 1) == 4 * iota((C_ATT, 4 * C_ATT), 0) + block
                    )
                    getattr(R, "w_" + name)[:, block * LANES : (block + 1) * LANES] = dot(pick, part)

        def unpack_gains():
            at = table[tag.gs][0]
            part = G[:, :, :, :, at : at + 16, :].reshape(16 * nd * nh, LANES)
            for full, rows, first_row, length in (
                (R.gains, GAIN_ROWS, 0, GAIN_LEN // (nd * nh)),
                (R.shifts, SHIFT_ROWS, 3, SHIFT_LEN // (nd * nh)),
            ):
                shape = (rows, 16 * nd * nh)
                source = iota(shape, 1)
                row = (source & 15) - first_row
                target = (((source >> 4) * length) >> 7) + row
                hit = (row >= 0) & (row < 3) & (target == iota(shape, 0))
                full[...] = dot(ones_where(hit), part)

        def emit(name, at, values):
            start = table[name][0] if name[0] != "q" else 0
            rows = per_dev(name)
            if rows % 16 == 0:
                for block in range(values.shape[1] // LANES):
                    to = start + (at // LANES + block) * rows
                    part = values[:, block * LANES : (block + 1) * LANES].astype(BFLOAT)
                    G[:, :, :, :, to : to + rows, :] = part.reshape(Z, X, Y, C, rows, LANES)
            elif name[0] == "o":
                for pair in range(values.shape[1] // (2 * LANES)):
                    to = start + (at // LANES + 2 * pair) * 8
                    both = [
                        values[:, (2 * pair + one) * LANES : (2 * pair + one + 1) * LANES].reshape(
                            nd * nh, 8, LANES
                        )
                        for one in range(2)
                    ]
                    part = jnp.concatenate(both, axis=1).astype(BFLOAT)
                    G[:, :, :, :, to : to + 16, :] = part.reshape(Z, X, Y, C, 16, LANES)
            elif name[0] == "e":
                part = None
                for block in range(4):
                    place = ones_where(
                        iota((4 * C_ATT, C_ATT), 0) == 4 * iota((4 * C_ATT, C_ATT), 1) + block, FLOAT
                    )
                    term = exact(place, values[:, block * LANES : (block + 1) * LANES])
                    part = term if part is None else part + term
                at = SMALL[name]
                R.small[:, :, at : at + 16, :] = part.reshape(nd, nh, 16, LANES)
            elif name[0] == "q":
                getattr(R, "g_" + name)[...] = values

        def emit_squeezes():
            both = [part[...].reshape(nd * nh, 8, LANES) for part in (R.g_q1, R.g_q2)]
            part = jnp.concatenate(both, axis=1)
            at = SMALL[tag.q]
            R.small[:, :, at : at + 16, :] = part.reshape(nd, nh, 16, LANES)

        class SmallScatter:
            def __init__(self, start, count):
                self.rows = pl.ds(start, count)

            def start(self):
                send, self.receive = new_sem(), new_sem()
                rows = self.rows
                for step in range(1, nd):
                    to = lax.rem(d + step, nd)
                    source, target = R.small.at[to, h, rows], R.small_in.at[d, rows]
                    remote(source, target, send, self.receive, (to, h)).start()
                late.append(lambda: wait_for(R.small_in.at[pl.ds(0, nd - 1), rows], send))

            def finish(self):
                wait_for(R.small_in.at[pl.ds(0, nd - 1), self.rows], self.receive)
                total = R.small[d, h, self.rows]
                for step in range(1, nd):
                    total = total + R.small_in[lax.rem(d + step, nd), self.rows]
                return total

        def emit_split(name):
            start, count = table[name]
            rows = per_dev(name)
            group = nh * rows

            def body(j, _):
                zz, xx = lax.div(j, 2), lax.rem(j, 2)
                at = pl.ds(pl.multiple_of(j * group, group), group)
                both = [
                    R.grad[at, block * LANES : (block + 1) * LANES].reshape(nh, rows, LANES)
                    for block in range(2)
                ]
                part = jnp.concatenate(both, axis=1).astype(BFLOAT)
                G[zz, xx, :, :, start : start + count, :] = part.reshape(Y, C, count, LANES)
                return 0

            lax.fori_loop(0, nd, body, 0)

        def deliver(name):
            rows, blocks = per_dev(name), SHAPES[name][1] // LANES
            order = ones_where(shuffle(rows * blocks, rows, blocks, back=True), FLOAT)
            getattr(R, "d_" + name)[...] = exact(order, scattered(name))

        def range_of(*parts):
            return (table[parts[0]][0], table[parts[-1]][0] + table[parts[-1]][1])

        gathers = [
            Gather(*range_of(tag.r1, tag.gs)),
            Gather(*range_of(tag.s1)),
            Gather(*range_of(tag.q, tag.sh)),
            Gather(*range_of(tag.r2, tag.o2)),
        ]
        sums = dict(
            o2=Scatter(*range_of(tag.o2)),
            s2=Scatter(*range_of(tag.s2)),
            r2=Scatter(*range_of(tag.r2)),
            mid=Scatter(*range_of(tag.o1, tag.sh)),
            s1=Scatter(*range_of(tag.s1)),
            r1=Scatter(*range_of(tag.r1)),
        )
        small_two, small_one = SmallScatter(0, 16), SmallScatter(16, 32)
    else:

        def emit(name, at, values):
            getattr(R, "d_" + name)[:, at : at + values.shape[1]] = values

        def emit_split(name):
            getattr(R, "d_" + name)[...] = R.grad[...]

    def progress(which, steps=1):
        if inside:
            for _ in range(steps):
                which.step()

    def vector(ref, at, length):
        row = at // LANES
        return jnp.concatenate([ref[row + k : row + k + 1, :] for k in range(length // LANES)], axis=1)

    def store_vector(ref, at, values):
        row = at // LANES
        for k in range(values.shape[1] // LANES):
            ref[row + k : row + k + 1, :] = values[:, k * LANES : (k + 1) * LANES]

    def over_images(body):
        def step(i, _):
            body(i, lax.div(i, MB))
            return 0

        lax.fori_loop(0, NIM, step, 0)

    one = types.SimpleNamespace(
        suffix="", W=H, px=cfg.rows * H, hp=(cfg.rows + 2) * H, place=first, mk=R.mk1, edge=R.edge1, p1=R.p1,
        a3=R.a3, p2=R.p2, s=R.s, dp2=R.dp2, dmix=R.dmix, dy1=R.dmix, c1=R.c_n1, c2=R.c_n2, group=1,
        split=R.w_s1, squeeze=R.w_q1, expand=R.w_e1, att=R.att1, dgap=R.dgap1, count=0, keep=R.keep1, k="1",
    )
    two = types.SimpleNamespace(
        suffix="b", W=H // 2, px=cfg.rows * H // 4, hp=(cfg.rows // 2 + 2) * H // 2, place=second, mk=R.mk2,
        edge=R.edge2, p1=R.p1b, a3=R.a3b, p2=R.p2b, s=R.sb, dp2=R.dp2b, dmix=R.dmixb, dy1=R.dmixb,
        c1=R.c_n1b, c2=R.c_n2b, group=MB, split=R.w_s2, squeeze=R.w_q2, expand=R.w_e2, att=R.att2,
        dgap=R.dgap2, count=2, keep=R.keep2, k="2",
    )
    px1, px2 = one.px, two.px
    edge_rows = H

    def build_masks():
        for at, block in enumerate((one, two)):
            bits = block.W.bit_length() - 1
            shape = (block.hp, LANES)
            pixel = iota(shape, 0)
            column = pixel & (block.W - 1)
            place = iota(block.edge.shape[1:], 0) & (block.W - 1)
            block.edge[0] = ones_where(place != 0, FLOAT)
            block.edge[1] = ones_where(place != block.W - 1, FLOAT)
            row = (pixel >> bits) - 1 + h * (block.px // block.W)
            for i in range(NIM):
                limit = (H - STEP * (2 - R.groups[i])) // (1 if at == 0 else 2)
                inside_grid = (row >= 0) & (row < limit) & (column < limit)
                block.mk[i] = ones_where(inside_grid, FLOAT)

    def clear(ref):
        ref[...] = jnp.zeros(ref.shape, ref.dtype)

    def totals(kinds, columns):
        return [
            jnp.sum(R.acc[m, kind, :, :columns], axis=0, keepdims=True)
            for m in range(MICRO)
            for kind in range(kinds)
        ]

    def clear_acc(kinds, columns):
        for m in range(MICRO):
            for kind in range(kinds):
                R.acc[m, kind, :, :columns] = jnp.zeros((8, columns), FLOAT)

    def chunk_of(columns):
        return 32 if columns <= 512 else 16

    def stat_pass(source, start, px, columns, mk, mask_start):
        chunk = chunk_of(columns)
        clear_acc(2, columns)

        def body(i, m):
            total, square = R.acc[m, 0, :, :columns], R.acc[m, 1, :, :columns]
            for t in range(0, px, chunk):
                v = source[i, start + t : start + t + chunk, :]
                vm = v * widen(mk[i, mask_start + t : mask_start + t + chunk, :], columns)
                total = total + fold(vm)
                square = square + fold(vm * v)
            R.acc[m, 0, :, :columns] = total
            R.acc[m, 1, :, :columns] = square

        over_images(body)
        return totals(2, columns)

    def inverse_count(block, m, columns):
        return widen(R.counts[block.count + m : block.count + m + 1, :], columns)

    def norm_coef(coef, total, at, columns, block, offset):
        gain, shift = vector(R.gains, offset, columns), vector(R.shifts, offset, columns)
        for m in range(MICRO):
            inverse = inverse_count(block, m, columns)
            centre = take(total, at + 2 * m) * inverse
            scaled = lax.rsqrt(take(total, at + 2 * m + 1) * inverse - centre * centre + EPSILON)
            coef[m, 0:1, :] = gain * scaled
            coef[m, 1:2, :] = shift - centre * (gain * scaled)
            coef[m, 2:3, :] = scaled
            coef[m, 3:4, :] = -centre * scaled

    def norm_coef_back(coef, total, pairs, columns, block, offset):
        for m, (at_sum, at_along) in enumerate(pairs):
            inverse = inverse_count(block, m, columns)
            summed, along = take(total, at_sum), take(total, at_along)
            scale = -coef[m, 0:1, :] * inverse
            coef[m, 4:5, :] = scale * (summed + along * coef[m, 3:4, :])
            coef[m, 5:6, :] = scale * along * coef[m, 2:3, :]
        sums_ = [take(total, pair[0]) for pair in pairs]
        alongs = [take(total, pair[1]) for pair in pairs]
        store_vector(R.all_shifts, offset, sums_[0] + sums_[1])
        store_vector(R.all_gains, offset, alongs[0] + alongs[1])

    class Halo:
        def __init__(self, down=None, up=None):
            self.ways = []
            for pair, step in ((down, 1), (up, -1)):
                if pair is not None:
                    sends = h < nh - 1 if step == 1 else h > 0
                    gets = h > 0 if step == 1 else h < nh - 1
                    copy = remote(pair[0], pair[1], new_sem(), new_sem(), (d, h + step))
                    self.ways.append((sends, gets, copy))

        def start(self):
            for sends, _, copy in self.ways:
                pl.when(sends)(copy.start)

        def finish(self):
            for _, gets, copy in self.ways:
                pl.when(gets)(copy.wait_recv)
            late.append(self.sent)

        def sent(self):
            for sends, _, copy in self.ways:
                pl.when(sends)(copy.wait_send)
            self.ways = []

    def activate(block):
        half = C_MID // 2

        def body(i, m):
            mask = block.mk[i]
            for g in range(2):
                cols = slice(g * half, (g + 1) * half)
                value = block.c1[m, 0:1, cols] * block.p1[i, :, cols] + block.c1[m, 1:2, cols]
                value = value * sigmoid(value) * mask
                if block is one:
                    R.a_sum[:, cols] = R.a_sum[:, cols] + fold(value[block.W : block.W + block.px])
                at = 3 * g * half
                left = pltpu.roll(value, 1, 0) * block.edge[0, : block.hp]
                right = pltpu.roll(value, block.hp - 1, 0) * block.edge[1, : block.hp]
                block.a3[i, :, at : at + half] = left.astype(BFLOAT)
                block.a3[i, :, at + half : at + 2 * half] = value.astype(BFLOAT)
                block.a3[i, :, at + 2 * half : at + 3 * half] = right.astype(BFLOAT)

        over_images(body)

    def in_groups(block, body):
        if block.group == 1:
            over_images(lambda i, m: body(i, 1, m))
        else:
            for m in range(MICRO):
                body(m * MB, MB, m)

    def rows_of(ref, i, count, start, rows, cols):
        part = ref[pl.ds(i, count), start : start + rows, cols]
        return part.reshape(count * rows, part.shape[-1])

    def convolve(block):
        half = C_MID // 2

        def body(i, count, m):
            for g in range(2):
                cols = slice(3 * g * half, 3 * (g + 1) * half)
                taps = [rows_of(block.a3, i, count, dy * block.W, block.px, cols) for dy in range(3)]
                matrix = block.split[9 * g * half : 9 * (g + 1) * half, :]
                result = dot(jnp.concatenate(taps, axis=1), matrix)
                block.p2[pl.ds(i, count), :, g * C_MID : (g + 1) * C_MID] = result.reshape(
                    count, block.px, C_MID
                )

        in_groups(block, body)

    def split_activate(block):
        columns = 2 * C_MID

        def body(i, m):
            gap = jnp.zeros((8, C_MID), FLOAT)
            for t in range(0, block.px, 32):
                at = slice(t, t + 32)
                mask = widen(block.mk[i, block.W + t : block.W + t + 32, :], columns)
                value = block.c2[m, 0:1, :] * block.p2[i, at, :] + block.c2[m, 1:2, :]
                value = value * sigmoid(value) * mask
                block.s[i, at, :] = value
                gap = gap + fold(value[:, :C_MID] + value[:, C_MID:])
            R.image_sums[i, :, :C_MID] = gap

        over_images(body)

    def put_image_sums(exchange, columns):
        slot = exchange.slot()
        for i in range(NIM):
            slot[i : i + 1, :] = jnp.sum(R.image_sums[i, :, :columns], axis=0, keepdims=True)
        slot[NIM:8, :] = jnp.zeros((8 - NIM, columns), FLOAT)

    def micro_sums(values):
        row = iota(values.shape, 0)
        return [
            jnp.sum(
                jnp.where((row >= m * MB) & (row < (m + 1) * MB), values, 0.0), axis=0, keepdims=True
            )
            for m in range(MICRO)
        ]

    def micro_pick(vectors, rows=8):
        shape = (rows, vectors[0].shape[1])
        return jnp.where(
            iota(shape, 0) < MB, jnp.broadcast_to(vectors[0], shape), jnp.broadcast_to(vectors[1], shape)
        )

    def inverse_area(block):
        shape = (8, C_MID)
        row = iota(shape, 0)
        side = jnp.ones(shape, FLOAT)
        for i in range(NIM):
            limit = (H - STEP * (2 - R.groups[i])) // (1 if block is one else 2)
            side = jnp.where(row == i, limit.astype(FLOAT), side)
        return 1.0 / (side * side)

    def attend(block, window_gap, window_norm):
        suffix = block.suffix
        gap, norm = Exchange(tag.gap + suffix), Exchange(tag.na + suffix)
        split_activate(block)
        put_image_sums(gap, C_MID)
        gap.start()
        window_gap()
        keep = block.keep
        pooled = gap.finish() * inverse_area(block)
        keep[0, :, :C_MID] = pooled
        before = exact(pooled, block.squeeze[...])
        firsts, seconds = micro_sums(before), micro_sums(before * before)
        slot = norm.slot()
        for m in range(MICRO):
            slot[2 * m : 2 * m + 1, :] = firsts[m]
            slot[2 * m + 1 : 2 * m + 2, :] = seconds[m]
        slot[4:8, :] = jnp.zeros((4, C_ATT), FLOAT)
        norm.start()
        window_norm()
        total = norm.finish()
        count = MB * nd
        centres, scales = [], []
        for m in range(MICRO):
            centre = total[2 * m : 2 * m + 1] / count
            centres.append(centre)
            scales.append(
                lax.rsqrt(total[2 * m + 1 : 2 * m + 2] / count - centre * centre + EPSILON)
            )
        scale = micro_pick(scales)
        normal = (before - micro_pick(centres)) * scale
        gain = vector(R.gains, block.place.attend, C_ATT)
        shift = vector(R.shifts, block.place.attend, C_ATT)
        normed = gain * normal + shift
        hidden = normed * sigmoid(normed)
        keep[1, :, :C_ATT] = normal
        keep[2, :, :C_ATT] = normed
        keep[3, :, :C_ATT] = hidden
        keep[4, :, :C_ATT] = gain * scale
        logits = exact(hidden, block.expand[...]) + vector(R.shifts, block.place.bias, 2 * C_MID)
        gap_logit = logits[:, :C_MID] - logits[:, C_MID:]
        keep[5, :, :] = jnp.concatenate([sigmoid(gap_logit), sigmoid(-gap_logit)], axis=1)
        for i in range(NIM):
            block.att[i] = jnp.broadcast_to(keep[5, i : i + 1, :], (8, 2 * C_MID))

    def mix(block, target, start):
        def body(i, m):
            for t in range(0, block.px, 32):
                at = slice(t, t + 32)
                value = (
                    block.att[i, 0:1, :C_MID] * block.s[i, at, :C_MID]
                    + block.att[i, 0:1, C_MID:] * block.s[i, at, C_MID:]
                )
                target[i, start + t : start + t + 32, :] = value.astype(BFLOAT)

        over_images(body)

    def attend_back(block, window_att, window_norm):
        suffix = block.suffix

        def body(i, m):
            parts = [jnp.zeros((8, C_MID), FLOAT)] * 2
            for t in range(0, block.px, 32):
                at = slice(t, t + 32)
                grad = block.dmix[i, at, :]
                for j in range(2):
                    parts[j] = parts[j] + fold(grad * block.s[i, at, j * C_MID : (j + 1) * C_MID])
            R.image_sums[i] = jnp.concatenate(parts, axis=1)

        over_images(body)
        heights, norm = Exchange(tag.datt + suffix), Exchange(tag.dna + suffix)
        put_image_sums(heights, 2 * C_MID)
        heights.start()
        window_att()
        grad_att = heights.finish()
        keep = block.keep
        att = keep[5]
        weighted = att * grad_att
        both = weighted[:, :C_MID] + weighted[:, C_MID:]
        grad_logits = weighted - att * jnp.concatenate([both, both], axis=1)
        grad_hidden = exact(grad_logits, block.expand[...], NT)
        grad_normed = grad_hidden * slope_of(keep[2, :, :C_ATT])
        normal = keep[1, :, :C_ATT]
        firsts, seconds = micro_sums(grad_normed), micro_sums(grad_normed * normal)
        bias = jnp.sum(grad_logits, axis=0, keepdims=True)
        slot = norm.slot()
        for m in range(MICRO):
            slot[2 * m : 2 * m + 1, :] = firsts[m]
            slot[2 * m + 1 : 2 * m + 2, :] = seconds[m]
        for k in range(4):
            slot[4 + k : 5 + k, :] = bias[:, k * LANES : (k + 1) * LANES]
        norm.start()
        emit(tag.e + block.k, 0, exact(keep[3, :, :C_ATT], grad_logits, TN) * share)
        window_norm()
        total = norm.finish()
        count = MB * nd
        store_vector(R.all_shifts, block.place.attend, total[0:1] + total[2:3])
        store_vector(R.all_gains, block.place.attend, total[1:2] + total[3:4])
        for k in range(4):
            store_vector(R.all_shifts, block.place.bias + k * LANES, total[4 + k : 5 + k])
        summed = micro_pick([total[0:1], total[2:3]])
        along = micro_pick([total[1:2], total[3:4]])
        grad_before = keep[4, :, :C_ATT] * (grad_normed - (summed + normal * along) / count)
        grad_gap = exact(grad_before, block.squeeze[...], NT) * inverse_area(block)
        for i in range(NIM):
            block.dgap[i] = jnp.broadcast_to(grad_gap[i : i + 1, :], (8, C_MID))
        emit(tag.q + block.k, 0, exact(keep[0, :, :C_MID], grad_before, TN) * share)

    def split_back(block):
        clear_acc(2, 2 * C_MID)

        def body(i, m):
            for j in range(2):
                cols = slice(j * C_MID, (j + 1) * C_MID)
                total, along = R.acc[m, 0, :, cols], R.acc[m, 1, :, cols]
                for t in range(0, block.px, 32):
                    at = slice(t, t + 32)
                    mask = widen(block.mk[i, block.W + t : block.W + t + 32, :], C_MID)
                    raw = block.p2[i, at, cols]
                    value = block.c2[m, 0:1, cols] * raw + block.c2[m, 1:2, cols]
                    grad = block.att[i, 0:1, cols] * block.dmix[i, at, :] + block.dgap[i, 0:1, :]
                    grad = grad * slope_of(value) * mask
                    block.s[i, at, cols] = grad
                    total = total + fold(grad)
                    along = along + fold(
                        grad * (block.c2[m, 2:3, cols] * raw + block.c2[m, 3:4, cols])
                    )
                R.acc[m, 0, :, cols] = total
                R.acc[m, 1, :, cols] = along

        over_images(body)

    def norm_back(block_px, grad, coef, raw, raw_start, mk, mask_start, target, start, columns):
        chunk = chunk_of(columns)

        def body(i, m):
            for t in range(0, block_px, chunk):
                mask = widen(mk[i, mask_start + t : mask_start + t + chunk, :], columns)
                value = (
                    coef[m, 0:1, :] * grad[i, t : t + chunk, :]
                    + coef[m, 4:5, :]
                    + coef[m, 5:6, :] * raw[i, raw_start + t : raw_start + t + chunk, :]
                )
                target[i, start + t : start + t + chunk, :] = (value * mask).astype(BFLOAT)

        over_images(body)

    def product_of_means(g):
        half = C_MID // 2
        eye = iota((half, half), 0) == iota((half, half), 1)
        row = jnp.broadcast_to(R.centre[0:1, g * half : (g + 1) * half], (half, half))
        column = jnp.sum(jnp.where(eye, row, 0.0), axis=1, keepdims=True)
        return column * R.grad_sum[0:1, g * C_MID : (g + 1) * C_MID]

    def mean_term():
        half = C_MID // 2
        rows = SHAPES[tag.s1][0] // (nd * nh)
        index = d * nh + h
        low = index * rows < 9 * half
        centre = jnp.where(low, R.centre[0:1, :half], R.centre[0:1, half:])
        sums_ = jnp.where(low, R.grad_sum[1:2, :C_MID], R.grad_sum[1:2, C_MID:])
        shape = (2 * rows, LANES)
        row = iota(shape, 0)
        hit = iota(shape, 1) == ((index * rows + (row >> 1)) & (half - 1))
        column = jnp.sum(
            jnp.where(hit, jnp.broadcast_to(centre, shape), 0.0), axis=1, keepdims=True
        )
        odd = (row & 1) == 1
        return column * jnp.where(
            odd, jnp.broadcast_to(sums_[:, LANES:], shape), jnp.broadcast_to(sums_[:, :LANES], shape)
        )

    def kernel_grad(block, g):
        half = C_MID // 2
        images = MB if block.group == 1 else NIM
        for dy in range(3):
            at = slice(9 * g * half + 3 * dy * half, 9 * g * half + 3 * (dy + 1) * half)
            total = None
            for i in range(0, NIM, images):
                taps = rows_of(
                    block.a3, i, images, dy * block.W, block.px, slice(3 * g * half, 3 * (g + 1) * half)
                )
                grad = rows_of(
                    block.dp2, i, images, block.W, block.px, slice(g * C_MID, (g + 1) * C_MID)
                )
                term = dot(taps, grad, TN)
                total = term if total is None else total + term
            if inside and block is one:
                total = total - jnp.concatenate([product_of_means(g)] * 3, axis=0)
            R.grad[at, :] = total

    def convolve_back(block):
        half = C_MID // 2
        clear_acc(2, C_MID)

        def body(i, count, m):
            rows = count * block.px
            for g in range(2):
                cols = slice(g * half, (g + 1) * half)
                total = None
                for dy in range(3):
                    grad = rows_of(
                        block.dp2, i, count, (2 - dy) * block.W, block.px, slice(g * C_MID, (g + 1) * C_MID)
                    )
                    at = 9 * g * half + 3 * dy * half
                    term = dot(grad, block.split[at : at + 3 * half, :], NT)
                    total = term if total is None else total + term
                value = (
                    total[:, half : 2 * half]
                    + pltpu.roll(total[:, :half], rows - 1, 0) * block.edge[1, :rows]
                    + pltpu.roll(total[:, 2 * half :], 1, 0) * block.edge[0, :rows]
                )
                raw = rows_of(block.p1, i, count, block.W, block.px, cols)
                mask = rows_of(block.mk, i, count, block.W, block.px, slice(0, LANES))
                before = block.c1[m, 0:1, cols] * raw + block.c1[m, 1:2, cols]
                value = value * slope_of(before) * mask
                block.dy1[pl.ds(i, count), :, cols] = value.reshape(count, block.px, half)
                normal = block.c1[m, 2:3, cols] * raw + block.c1[m, 3:4, cols]
                R.acc[m, 0, :, cols] = R.acc[m, 0, :, cols] + fold(value)
                R.acc[m, 1, :, cols] = R.acc[m, 1, :, cols] + fold(value * normal)

        in_groups(block, body)

    def sum_gradients(i, m):
        total = jnp.where(i == 0, 0.0, R.acc[0, 2, :, : 2 * C_MID])
        for t in range(0, one.px, 32):
            total = total + fold(R.dp2[i, one.W + t : one.W + t + 32, :].astype(FLOAT))
        R.acc[0, 2, :, : 2 * C_MID] = total

    def splat_back(block, halo, window_att, window_norm, window_split, window_reduce):
        suffix = block.suffix
        attend_back(block, window_att, window_norm)
        split_back(block)
        exchange = Exchange(tag.dn2 + suffix)
        put(exchange, totals(2, 2 * C_MID))
        exchange.start()
        window_split()
        norm_coef_back(
            block.c2, exchange.finish(), ((0, 1), (2, 3)), 2 * C_MID, block, block.place.split
        )
        norm_back(
            block.px, block.s, block.c2, block.p2, 0, block.mk, block.W, block.dp2, block.W, 2 * C_MID
        )
        halo.start()
        if block is one:
            over_images(sum_gradients)
            R.grad_sum[0:1, :] = jnp.sum(R.acc[0, 2, :, : 2 * C_MID], axis=0, keepdims=True)
        kernel_grad(block, 0)
        halo.finish()
        convolve_back(block)
        exchange = Exchange(tag.dn1 + suffix)
        put(exchange, totals(2, C_MID))
        if block is one:
            slot = exchange.slot()
            for k in range(4):
                slot[8 + k : 9 + k, :] = R.grad_sum[0:1, k * LANES : (k + 1) * LANES]
            slot[12:16, :] = jnp.zeros((4, LANES), FLOAT)
        exchange.start()
        kernel_grad(block, 1)
        emit_split(tag.s + block.k)
        window_reduce()
        total = exchange.finish()
        if block is one:
            for k in range(4):
                R.grad_sum[1:2, k * LANES : (k + 1) * LANES] = total[8 + k : 9 + k]
        norm_coef_back(block.c1, total, ((0, 1), (2, 3)), C_MID, block, block.place.reduce)
        norm_back(
            block.px, block.dy1, block.c1, block.p1, block.W, block.mk, block.W, block.dp1, 0, C_MID
        )

    one.dp1, two.dp1 = R.dp1, R.dp1b
    halo_x = Halo(
        (R.images.at[:, pl.ds(px1 - edge_rows, edge_rows)], R.xh.at[:, pl.ds(0, edge_rows)]),
        (R.images.at[:, pl.ds(0, edge_rows)], R.xh.at[:, pl.ds(one.hp - edge_rows, edge_rows)]),
    )
    load_x = pltpu.make_async_copy(R.images, R.xh.at[:, pl.ds(edge_rows, px1)], new_sem())
    load_cot = pltpu.make_async_copy(R.cotangent, R.cot, new_sem())
    load_x.start()
    load_cot.start()
    for block, refs_ in (
        (one, (R.xh, R.dp2)),
        (two, (R.p1b, R.dp2b)),
    ):
        for ref in refs_:
            shape = (NIM, block.W, ref.shape[-1])
            ref[:, : block.W, :] = jnp.zeros(shape, ref.dtype)
            ref[:, block.hp - block.W :, :] = jnp.zeros(shape, ref.dtype)
    clear(R.a_sum)
    R.v1[:, :edge_rows, :] = jnp.zeros((NIM, edge_rows, C_MID), BFLOAT)
    R.dq[:, px2:, :] = jnp.zeros((NIM, two.W, C_MID), BFLOAT)

    barrier = pltpu.get_barrier_semaphore()
    partners = 0
    for step in range(1, nh):
        to = (d, lax.rem(h + step, nh))
        pl.semaphore_signal(barrier, inc=1, device_id=to, device_id_type=MESH)
        partners += 1
    if high == 1:
        for step in range(1, nd):
            to = (lax.rem(d + step, nd), h)
            pl.semaphore_signal(barrier, inc=1, device_id=to, device_id_type=MESH)
            partners += 1
    else:
        for count, me, peer in dims_of[DP]:
            for step in range(1, count):
                to = peer(lax.rem(me + step, count))
                pl.semaphore_signal(barrier, inc=1, device_id=to, device_id_type=MESH)
                partners += 1
    if inside:
        pack_shards()
    pl.semaphore_wait(barrier, partners)

    if inside:
        gathers[0].step()
    halo_x.start()
    if inside:
        for gather in gathers[1:]:
            gather.step()
    build_masks()

    out_shape = (px2, px1 + edge_rows)
    out_pixel, in_pixel = iota(out_shape, 0), iota(out_shape, 1)
    down = (in_pixel >> 5) - 2 * (out_pixel >> 4)
    along_ = (in_pixel & 31) - 2 * (out_pixel & 15) + 1
    R.pool3[...] = ones_where((down >= 0) & (down < 3) & (along_ >= 0) & (along_ < 3))
    out_shape = (px2, px1)
    out_pixel, in_pixel = iota(out_shape, 0), iota(out_shape, 1)
    cell = ((in_pixel >> 6) == (out_pixel >> 4)) & (((in_pixel & 31) >> 1) == (out_pixel & 15))
    R.pool2[...] = jnp.where(cell, 0.25, 0.0).astype(FLOAT).astype(BFLOAT)
    back_shape = (px1, px2)
    in_pixel, out_pixel = iota(back_shape, 0), iota(back_shape, 1)
    cell = ((in_pixel >> 6) == (out_pixel >> 4)) & (((in_pixel & 31) >> 1) == (out_pixel & 15))
    R.spread2[...] = jnp.where(cell, 0.25, 0.0).astype(FLOAT).astype(BFLOAT)
    back_shape = (px1, px2 + two.W)
    in_pixel, out_pixel = iota(back_shape, 0), iota(back_shape, 1)
    down = (in_pixel >> 5) + 1 - 2 * (out_pixel >> 4)
    along_ = (in_pixel & 31) + 1 - 2 * (out_pixel & 15)
    R.spread3[...] = ones_where((down >= 0) & (down < 3) & (along_ >= 0) & (along_ < 3))

    if inside:
        gathers[0].finish()
        unpack_rows(tag.r1)
        unpack_gains()
    load_x.wait()
    halo_x.finish()

    def body(i, m):
        R.p1[i] = dot(R.xh[i], R.w_r1[...])

    over_images(body)
    if inside:
        gathers[1].step()
    exchange = Exchange(tag.n1)
    put(exchange, stat_pass(R.p1, one.W, px1, C_MID, R.mk1, one.W))
    slot = exchange.slot()
    for m in range(MICRO):
        cells = jnp.zeros((8, LANES), FLOAT)
        for i in range(m * MB, (m + 1) * MB):
            cells = cells + fold(R.mk1[i, one.W : one.W + px1, :])
        slot[8 + m : 9 + m, :] = jnp.sum(cells, axis=0, keepdims=True)
    slot[10:16, :] = jnp.zeros((6, LANES), FLOAT)
    exchange.start()
    if inside:
        gathers[1].step()

    def body(i, m):
        R.t1[i] = dot(R.pool2[...], R.xh[i, edge_rows : edge_rows + px1, :]).astype(BFLOAT)

    over_images(body)
    total = exchange.finish()
    for m in range(MICRO):
        R.counts[m : m + 1, :] = 1.0 / total[8 + m : 9 + m, :]
        R.counts[2 + m : 3 + m, :] = 4.0 / total[8 + m : 9 + m, :]
    norm_coef(R.c_n1, total, 0, C_MID, one, first.reduce)
    if inside:
        gathers[1].step()
        gathers[2].step()
    activate(one)
    if inside:
        gathers[1].finish()
        unpack_split(tag.s1)
    convolve(one)
    exchange = Exchange(tag.n2)
    put(exchange, stat_pass(R.p2, 0, px1, 2 * C_MID, R.mk1, one.W))
    exchange.start()
    if inside:
        gathers[2].step()
        gathers[3].step()
    norm_coef(R.c_n2, exchange.finish(), 0, 2 * C_MID, one, first.split)
    if inside:
        gathers[2].step()

    def window_gap():
        if inside:
            gathers[2].finish()
            unpack_attention()

    def window_norm():
        if inside:
            gathers[3].step()
            unpack_rows(tag.sh)
            unpack_pairs(tag.o1)

    attend(one, window_gap, window_norm)
    mix(one, R.v1, edge_rows)
    halo_v = Halo((R.v1.at[:, pl.ds(px1, edge_rows)], R.v1.at[:, pl.ds(0, edge_rows)]))
    halo_v.start()

    def outer(ref, columns):
        return ref[...].reshape(NIM * px2, columns)

    def product_out(source, inner, matrix, target):
        for at in range(0, C_OUT, 256):
            target[:, :, at : at + 256] = dot(outer(source, inner), matrix[:, at : at + 256]).reshape(
                NIM, px2, 256
            )

    product_out(R.t1, C_IN, R.w_sh, R.csh)
    exchange = Exchange(tag.no)
    stats_short = stat_pass(R.csh, 0, px2, C_OUT, R.mk2, two.W)
    halo_v.finish()

    def body(i, m):
        R.q1[i] = (dot(R.pool3[...], R.v1[i]) * (1.0 / 9.0)).astype(BFLOAT)

    over_images(body)
    product_out(R.q1, C_MID, R.w_o1, R.o1)
    put(exchange, stat_pass(R.o1, 0, px2, C_OUT, R.mk2, two.W) + stats_short)
    exchange.start()
    if inside:
        gathers[3].finish()
        unpack_rows(tag.r2)
        unpack_split(tag.s2)
        unpack_pairs(tag.o2)
    total = exchange.finish()
    norm_coef(R.c_o1, total, 0, C_OUT, two, first.output)
    norm_coef(R.c_sh, total, 4, C_OUT, two, first.shortcut)

    def first_sum(i, m, at, mask_rows):
        return (
            R.c_o1[m, 0:1, :] * R.o1[i, at, :]
            + R.c_sh[m, 0:1, :] * R.csh[i, at, :]
            + (R.c_o1[m, 1:2, :] + R.c_sh[m, 1:2, :])
        )

    def body(i, m):
        for t in range(0, px2, 16):
            at = slice(t, t + 16)
            value = first_sum(i, m, at, None)
            mask = widen(R.mk2[i, two.W + t : two.W + t + 16, :], C_OUT)
            R.l1[i, at, :] = (value * sigmoid(value) * mask).astype(BFLOAT)

    over_images(body)
    store_one = pltpu.make_async_copy(R.l1, R.layer_one, new_sem())
    store_one.start()
    late.append(store_one.wait)

    R.p1b[:, two.W : two.W + px2, :] = dot(outer(R.l1, C_OUT), R.w_r2[...]).reshape(
        NIM, px2, C_MID
    )
    halo_p = Halo(
        (R.p1b.at[:, pl.ds(px2, two.W)], R.p1b.at[:, pl.ds(0, two.W)]),
        (R.p1b.at[:, pl.ds(two.W, two.W)], R.p1b.at[:, pl.ds(two.hp - two.W, two.W)]),
    )
    exchange = Exchange(tag.n1b)
    put(exchange, stat_pass(R.p1b, two.W, px2, C_MID, R.mk2, two.W))
    exchange.start()
    halo_p.start()
    norm_coef(R.c_n1b, exchange.finish(), 0, C_MID, two, second.reduce)
    halo_p.finish()
    activate(two)
    convolve(two)
    exchange = Exchange(tag.n2b)
    put(exchange, stat_pass(R.p2b, 0, px2, 2 * C_MID, R.mk2, two.W))
    exchange.start()
    norm_coef(R.c_n2b, exchange.finish(), 0, 2 * C_MID, two, second.split)
    attend(two, lambda: None, lambda: None)
    mix(two, R.mix2, 0)
    product_out(R.mix2, C_MID, R.w_o2, R.o2)
    exchange = Exchange(tag.nob)
    put(exchange, stat_pass(R.o2, 0, px2, C_OUT, R.mk2, two.W))
    exchange.start()
    load_cot.wait()
    norm_coef(R.c_o2, exchange.finish(), 0, C_OUT, two, second.output)

    clear_acc(2, C_OUT)

    def body(i, m):
        total, along = R.acc[m, 0], R.acc[m, 1]
        for t in range(0, px2, 16):
            at = slice(t, t + 16)
            mask = widen(R.mk2[i, two.W + t : two.W + t + 16, :], C_OUT)
            raw = R.o2[i, at, :]
            value = R.c_o2[m, 0:1, :] * raw + R.c_o2[m, 1:2, :] + R.l1[i, at, :].astype(FLOAT)
            logistic = sigmoid(value)
            R.dpo[i, at, :] = (value * logistic * mask).astype(BFLOAT)
            grad = R.cot[i, at, :].astype(FLOAT) * mask * (logistic * (1.0 + value * (1.0 - logistic)))
            R.g2[i, at, :] = grad
            total = total + fold(grad)
            along = along + fold(grad * (R.c_o2[m, 2:3, :] * raw + R.c_o2[m, 3:4, :]))
        R.acc[m, 0] = total
        R.acc[m, 1] = along

    over_images(body)
    exchange = Exchange(tag.dnob)
    put(exchange, totals(2, C_OUT))
    exchange.start()
    store_two = pltpu.make_async_copy(R.dpo, R.layer_two, new_sem())
    store_two.start()
    norm_coef_back(R.c_o2, exchange.finish(), ((0, 1), (2, 3)), C_OUT, two, second.output)
    store_two.wait()
    norm_back(px2, R.g2, R.c_o2, R.o2, 0, R.mk2, two.W, R.dpo, 0, C_OUT)
    R.dmixb[...] = dot(outer(R.dpo, C_OUT), R.w_o2[...], NT).reshape(NIM, px2, C_MID)

    def grad_outer(name, source, inner, grad):
        for at in range(0, C_OUT, 256):
            part = grad[:, :, at : at + 256].reshape(NIM * px2, 256)
            emit(name, at, dot(outer(source, inner), part, TN))

    def window_att():
        if inside:
            for gather in gathers:
                gather.sent()
        grad_outer(tag.o2, R.mix2, C_MID, R.dpo)
        if inside:
            sums[tag.o2].step()

    def window_norm():
        if inside:
            sums[tag.o2].step()

    def window_split():
        if inside:
            sums[tag.o2].step()
            small_two.start()

    def window_reduce():
        if inside:
            sums[tag.o2].step()
            sums[tag.s2].step()

    halo_d = Halo(
        (R.dp2b.at[:, pl.ds(px2, two.W)], R.dp2b.at[:, pl.ds(0, two.W)]),
        (R.dp2b.at[:, pl.ds(two.W, two.W)], R.dp2b.at[:, pl.ds(two.hp - two.W, two.W)]),
    )
    splat_back(two, halo_d, window_att, window_norm, window_split, window_reduce)

    clear_acc(3, C_OUT)
    R.o2[...] = dot(outer(R.dp1b, C_MID), R.w_r2[...], NT).reshape(NIM, px2, C_OUT)

    def body(i, m):
        sums_ = [R.acc[m, kind] for kind in range(3)]
        for t in range(0, px2, 16):
            at = slice(t, t + 16)
            mask = widen(R.mk2[i, two.W + t : two.W + t + 16, :], C_OUT)
            value = first_sum(i, m, at, None)
            grad = (R.g2[i, at, :] + R.o2[i, at, :]) * mask * slope_of(value)
            R.g2[i, at, :] = grad
            sums_[0] = sums_[0] + fold(grad)
            sums_[1] = sums_[1] + fold(
                grad * (R.c_o1[m, 2:3, :] * R.o1[i, at, :] + R.c_o1[m, 3:4, :])
            )
            sums_[2] = sums_[2] + fold(
                grad * (R.c_sh[m, 2:3, :] * R.csh[i, at, :] + R.c_sh[m, 3:4, :])
            )
        for kind in range(3):
            R.acc[m, kind] = sums_[kind]

    over_images(body)
    exchange = Exchange(tag.dno)
    put(exchange, totals(3, C_OUT))
    slot = exchange.slot()
    slot[12:16, :] = jnp.zeros((4, C_OUT // 2), FLOAT)
    slot[12:13, :C_MID] = jnp.sum(R.a_sum[...], axis=0, keepdims=True)
    exchange.start()
    if inside:
        sums[tag.o2].step()
        sums[tag.s2].step()
    dp1b = outer(R.dp1b, C_MID)
    for at in range(0, C_MID, 128):
        emit(tag.r2, at, dot(outer(R.l1, C_OUT), dp1b[:, at : at + 128], TN))
    if inside:
        sums[tag.r2].step()
    total = exchange.finish()
    counts = R.counts[0:1, :], R.counts[1:2, :]
    R.centre[0:1, :] = total[12:13, :C_MID] * widen(
        counts[0] * counts[1] / (counts[0] + counts[1]), C_MID
    )
    norm_coef_back(R.c_o1, total, ((0, 1), (3, 4)), C_OUT, two, first.output)
    norm_coef_back(R.c_sh, total, ((0, 2), (3, 5)), C_OUT, two, first.shortcut)
    norm_back(px2, R.g2, R.c_o1, R.o1, 0, R.mk2, two.W, R.dpo, 0, C_OUT)
    R.dq[:, :px2, :] = (
        (dot(outer(R.dpo, C_OUT), R.w_o1[...], NT) * (1.0 / 9.0)).astype(BFLOAT).reshape(NIM, px2, C_MID)
    )
    halo_q = Halo(up=(R.dq.at[:, pl.ds(0, two.W)], R.dq.at[:, pl.ds(px2, two.W)]))
    halo_q.start()
    norm_back(px2, R.g2, R.c_sh, R.csh, 0, R.mk2, two.W, R.cot, 0, C_OUT)
    if inside:
        sums[tag.s2].step()
        sums[tag.r2].step()
    halo_q.finish()

    def body(i, m):
        R.dmix[i] = dot(R.spread3[...], R.dq[i])

    over_images(body)

    def window_att():
        if inside:
            sums[tag.s2].step()
            sums[tag.r2].step()
        grad_outer(tag.o1, R.q1, C_MID, R.dpo)

    def window_norm():
        if inside:
            sums[tag.s2].step()
            sums[tag.r2].step()
        grad_outer(tag.sh, R.t1, C_IN, R.cot)
        if inside:
            sums[tag.mid].step()

    def window_split():
        if inside:
            emit_squeezes()
            small_one.start()
            sums[tag.mid].step()
        R.dt1[...] = dot(outer(R.cot, C_OUT), R.w_sh[...], NT).astype(BFLOAT).reshape(NIM, px2, C_IN)
        if inside:
            sums[tag.r2].step()
            deliver(tag.o2)
            deliver(tag.s2)
            R.d_e2[...] = small_two.finish()

    def window_reduce():
        if inside:
            sums[tag.mid].step()
            sums[tag.s1].step()
            deliver(tag.r2)

    halo_d = Halo(
        (R.dp2.at[:, pl.ds(px1, edge_rows)], R.dp2.at[:, pl.ds(0, edge_rows)]),
        (R.dp2.at[:, pl.ds(edge_rows, edge_rows)], R.dp2.at[:, pl.ds(one.hp - edge_rows, edge_rows)]),
    )
    splat_back(one, halo_d, window_att, window_norm, window_split, window_reduce)

    for at in range(0, C_MID, 128):

        def body(i, m):
            term = dot(R.xh[i, edge_rows : edge_rows + px1, :], R.dp1[i, :, at : at + 128], TN)
            R.grad[:C_IN, :128] = jnp.where(i == 0, 0.0, R.grad[:C_IN, :128]) + term

        over_images(body)
        emit(tag.r1, at, R.grad[:C_IN, :128])
    if inside:
        sums[tag.r1].step()
        sums[tag.s1].step()
        sums[tag.mid].step()

    halo_d.sent()
    store_images = new_sem()
    own = pl.ds(edge_rows, px1)

    def body(i, m):
        value = dot(R.dp1[i], R.w_r1[...], NT) + dot(R.spread2[...], R.dt1[i])
        R.dp2[i, own, :] = value.astype(BFLOAT)
        pltpu.make_async_copy(R.dp2.at[i, own], R.grad_images.at[i], store_images).start()

    over_images(body)
    late.append(lambda: wait_for(R.dp2.at[:, own], store_images))
    if inside:
        sums[tag.r1].step()
        sums[tag.s1].step()
        sums[tag.mid].step()
        sums[tag.r1].step()
        for name in (tag.o1, tag.sh):
            deliver(name)
        sums[tag.s1].step()
        sums[tag.r1].step()
        sums[tag.s1].step()
        deliver(tag.s1)
        R.d_s1[...] = R.d_s1[...] + mean_term()
        total = small_one.finish()
        R.d_q1[...] = total[:8]
        R.d_q2[...] = total[8:16]
        R.d_e1[...] = total[16:]
        sums[tag.r1].step()
        deliver(tag.r1)
        for group in sums.values():
            assert group.phase == 4
    index = d * nh + h
    for full, target, length in (
        (R.all_gains, R.d_gains, GAIN_LEN // (nd * nh)),
        (R.all_shifts, R.d_shifts, SHIFT_LEN // (nd * nh)),
    ):
        start = index * length
        lane = start & (LANES - 1)
        turned = pltpu.roll(full[pl.ds(start >> 7, 8), :], lax.rem(LANES - lane, LANES), 1)
        here = iota((2, LANES), 1) < LANES - lane
        target[...] = jnp.where(here, turned[0:2], turned[1:3])
    for wait in late:
        wait()


def per_device(nd, nh, images, size_group, cotangent, *params):
    weights, (norm_gains, norm_shifts) = params[:11], params[11:]
    devices = nd * nh
    rows = images.shape[1]
    px1 = rows * H
    px2 = px1 // 4
    hp1, hp2 = px1 + 2 * H, px2 + H
    per_rows = {name: weight.shape[0] // LANES for name, weight in zip(SHAPES, weights)}
    inside = (
        nh == 4
        and devices == 32
        and per_rows[tag.q1] == 8
        and all(inner % devices == 0 for inner, _ in SHAPES.values())
    )
    axes = (tag.dp, tag.height)
    index = lax.axis_index(axes)
    cfg = types.SimpleNamespace(nd=nd, nh=nh, inside=inside, rows=rows)

    operands, names, specs = [], [], []
    whole = pl.BlockSpec(memory_space=pltpu.VMEM)

    def operand(name, value, spec=whole):
        operands.append(value)
        names.append(name)
        specs.append(spec)

    operand(tag.groups, size_group, pl.BlockSpec(memory_space=pltpu.SMEM))
    operand(tag.images, images.reshape(NIM, px1, C_IN), pl.BlockSpec(memory_space=pl.ANY))
    operand(tag.cotangent, cotangent.reshape(NIM, px2, C_OUT), pl.BlockSpec(memory_space=pl.ANY))
    if inside:
        pieces = []
        for vector in (norm_gains, norm_shifts):
            lane = lax.rem(index * vector.shape[0], LANES)
            piece = lax.dynamic_update_slice(jnp.zeros((3 * LANES,), BFLOAT), vector, (lane,))
            pieces.append(piece.reshape(3, LANES))
        operand(tag.gs, jnp.pad(jnp.concatenate(pieces, axis=0), ((0, 10), (0, 0))))
        for name, weight in zip(SHAPES, weights):
            operand(tag.a_ + name, weight.reshape(-1, LANES))
        cfg.table, total_rows = row_table(per_rows)
    else:
        for name, weight in zip(SHAPES, weights):
            full = lax.all_gather(weight, axes, axis=0, tiled=True).reshape(SHAPES[name])
            operand(tag.w_ + name, full.astype(FLOAT) if name[0] in "qe" else full)
        for name, vector, length in (
            (tag.gains, norm_gains, GAIN_ROWS),
            (tag.shifts, norm_shifts, SHIFT_ROWS),
        ):
            full = lax.all_gather(vector, axes, axis=0, tiled=True).astype(FLOAT)
            full = jnp.pad(full, (0, length * LANES - full.shape[0]))
            operand(name, full.reshape(length, LANES))

    outs = dict(
        layer_one=((NIM, px2, C_OUT), BFLOAT),
        layer_two=((NIM, px2, C_OUT), BFLOAT),
        grad_images=((NIM, px1, C_IN), BFLOAT),
    )
    for name, shape in SHAPES.items():
        outs["d_" + name] = ((per_rows[name], LANES) if inside else shape, FLOAT)
    outs[tag.d_gains] = ((2, LANES), FLOAT)
    outs[tag.d_shifts] = ((2, LANES), FLOAT)

    scratch = dict(
        xh=((NIM, hp1, C_IN), BFLOAT),
        cot=((NIM, px2, C_OUT), BFLOAT),
        mk1=((NIM, hp1, LANES), FLOAT),
        mk2=((NIM, hp2, LANES), FLOAT),
        edge1=((2, hp1, LANES), FLOAT),
        edge2=((2, MB * px2, LANES), FLOAT),
        counts=((8, LANES), FLOAT),
        all_gains=((GAIN_ROWS, LANES), FLOAT),
        all_shifts=((SHIFT_ROWS, LANES), FLOAT),
        a_sum=((8, C_MID), FLOAT),
        centre=((8, C_MID), FLOAT),
        grad_sum=((8, 2 * C_MID), FLOAT),
        acc=((MICRO, 3, 8, C_OUT), FLOAT),
        image_sums=((NIM, 8, 2 * C_MID), FLOAT),
        p1=((NIM, hp1, C_MID), FLOAT),
        a3=((NIM, hp1, 3 * C_MID), BFLOAT),
        p2=((NIM, px1, 2 * C_MID), FLOAT),
        s=((NIM, px1, 2 * C_MID), FLOAT),
        v1=((NIM, px1 + H, C_MID), BFLOAT),
        q1=((NIM, px2, C_MID), BFLOAT),
        t1=((NIM, px2, C_IN), BFLOAT),
        o1=((NIM, px2, C_OUT), FLOAT),
        csh=((NIM, px2, C_OUT), FLOAT),
        p1b=((NIM, hp2, C_MID), FLOAT),
        a3b=((NIM, hp2, 3 * C_MID), BFLOAT),
        p2b=((NIM, px2, 2 * C_MID), FLOAT),
        sb=((NIM, px2, 2 * C_MID), FLOAT),
        mix2=((NIM, px2, C_MID), BFLOAT),
        l1=((NIM, px2, C_OUT), BFLOAT),
        o2=((NIM, px2, C_OUT), FLOAT),
        g2=((NIM, px2, C_OUT), FLOAT),
        dpo=((NIM, px2, C_OUT), BFLOAT),
        dmixb=((NIM, px2, C_MID), FLOAT),
        dp2b=((NIM, hp2, 2 * C_MID), BFLOAT),
        dp1b=((NIM, px2, C_MID), BFLOAT),
        dq=((NIM, px2 + H // 2, C_MID), BFLOAT),
        dt1=((NIM, px2, C_IN), BFLOAT),
        dmix=((NIM, px1, C_MID), FLOAT),
        dp2=((NIM, hp1, 2 * C_MID), BFLOAT),
        dp1=((NIM, px1, C_MID), BFLOAT),
        grad=((9 * C_MID, C_MID), FLOAT),
        pool3=((px2, px1 + H), BFLOAT),
        pool2=((px2, px1), BFLOAT),
        spread2=((px1, px2), BFLOAT),
        spread3=((px1, px2 + H // 2), BFLOAT),
        keep1=((6, 8, 2 * C_MID), FLOAT),
        keep2=((6, 8, 2 * C_MID), FLOAT),
        att1=((NIM, 8, 2 * C_MID), FLOAT),
        att2=((NIM, 8, 2 * C_MID), FLOAT),
        dgap1=((NIM, 8, C_MID), FLOAT),
        dgap2=((NIM, 8, C_MID), FLOAT),
        c_n1=((MICRO, 8, C_MID), FLOAT),
        c_n2=((MICRO, 8, 2 * C_MID), FLOAT),
        c_o1=((MICRO, 8, C_OUT), FLOAT),
        c_sh=((MICRO, 8, C_OUT), FLOAT),
        c_n1b=((MICRO, 8, C_MID), FLOAT),
        c_n2b=((MICRO, 8, 2 * C_MID), FLOAT),
        c_o2=((MICRO, 8, C_OUT), FLOAT),
    )
    for name, (count, lanes, kind) in SYNCS.items():
        for k, size in enumerate(stage_sizes(kind, nd, nh)):
            scratch["sy_" + name + str(k)] = ((size, count, lanes), FLOAT)
    if inside:
        four = (nd // 2, 2, nh // 2, 2)
        scratch |= dict(
            pack=(four + (total_rows, LANES), BFLOAT),
            rc=(four[:3] + (total_rows, LANES), BFLOAT),
            ry=(four[:2] + (total_rows, LANES), BFLOAT),
            rx=(four[:1] + (total_rows, LANES), BFLOAT),
            rz=(four[:1] + (total_rows, LANES), BFLOAT),
            small=((nd, nh, 48, LANES), FLOAT),
            small_in=((nd, 48, LANES), FLOAT),
            gains=((GAIN_ROWS, LANES), FLOAT),
            shifts=((SHIFT_ROWS, LANES), FLOAT),
            g_q1=((C_MID, C_ATT), FLOAT),
            g_q2=((C_MID, C_ATT), FLOAT),
        )
        for name, shape in SHAPES.items():
            scratch["w_" + name] = (shape, FLOAT if name[0] in "qe" else BFLOAT)

    results = pl.pallas_call(
        functools.partial(
            kernel, cfg, names + list(outs) + list(scratch) + [tag.sem]
        ),
        out_shape=[jax.ShapeDtypeStruct(shape, kind) for shape, kind in outs.values()],
        in_specs=specs,
        out_specs=[pl.BlockSpec(memory_space=pl.ANY)] * 3 + [whole] * (len(outs) - 3),
        scratch_shapes=[pltpu.VMEM(shape, kind) for shape, kind in scratch.values()]
        + [pltpu.SemaphoreType.DMA((SEMAPHORES,))],
        compiler_params=pltpu.CompilerParams(
            collective_id=0, has_side_effects=True, vmem_limit_bytes=62 * 1024 * 1024
        ),
    )(*operands)

    if inside:
        results = deliver_all(results)
    layer_one, layer_two, grad_images = results[:3]
    grads = [grad.reshape(-1) for grad in results[3:14]]
    if not inside:
        grads = [
            lax.psum_scatter(grad, axes, scatter_dimension=0, tiled=True) for grad in grads
        ]
    tails = [
        total.reshape(-1)[: vector.shape[0]] for total, vector in zip(results[14:], (norm_gains, norm_shifts))
    ]
    return (
        layer_one.reshape(cotangent.shape),
        layer_two.reshape(cotangent.shape),
        grad_images.reshape(images.shape),
        *grads,
        *tails,
    )


def copy_all(count, *refs):
    copies = [
        pltpu.make_async_copy(source, target, refs[-1].at[k])
        for k, (source, target) in enumerate(zip(refs[:count], refs[count : 2 * count]))
    ]
    for copy in copies:
        copy.start()
    for copy in copies:
        copy.wait()


def deliver_all(results):
    count = len(results)
    anywhere = pl.BlockSpec(memory_space=pl.ANY)
    return pl.pallas_call(
        functools.partial(copy_all, count),
        out_shape=[jax.ShapeDtypeStruct(value.shape, value.dtype) for value in results],
        in_specs=[pl.BlockSpec(memory_space=pltpu.VMEM)] * count,
        out_specs=[anywhere] * count,
        scratch_shapes=[pltpu.SemaphoreType.DMA((count,))],
    )(*results)


def solution(mesh):
    shard = P(("dp", "height"))
    rows = P("dp", "height", None, None)
    return jax.shard_map(
        functools.partial(per_device, mesh.shape["dp"], mesh.shape["height"]),
        mesh=mesh,
        in_specs=(rows, P("dp"), rows) + (shard,) * 13,
        out_specs=(rows,) * 3 + (shard,) * 13,
        check_vma=False,
    )
```

```python
import functools
import types

import jax
import jax.numpy as jnp
from jax import lax
from jax.experimental import pallas as pl
from jax.experimental.pallas import tpu as pltpu
from jax.sharding import PartitionSpec as P

C_IN = 512
C_MID = 256
C_ATT = 128
C_OUT = 1024
H = 32
STEP = 4
MICRO = 2
MB = 3

EPSILON = 1e-05
HIGHEST = lax.Precision.HIGHEST
FLOAT = jnp.float32
BFLOAT = jnp.bfloat16
MESH = pl.DeviceIdType.MESH
LANES = 128
NIM = MICRO * MB
NN = (((1,), (0,)), ((), ()))
NT = (((1,), (1,)), ((), ()))
TN = (((0,), (0,)), ((), ()))


class Names:
    def __getattr__(self, name):
        return name


tag = Names()

SHAPES = dict(
    r1=(C_IN, C_MID),
    s1=(9 * C_MID, C_MID),
    q1=(C_MID, C_ATT),
    e1=(C_ATT, 2 * C_MID),
    o1=(C_MID, C_OUT),
    sh=(C_IN, C_OUT),
    r2=(C_OUT, C_MID),
    s2=(9 * C_MID, C_MID),
    q2=(C_MID, C_ATT),
    e2=(C_ATT, 2 * C_MID),
    o2=(C_MID, C_OUT),
)

HEIGHT, DP, ONCE, TWICE = range(4)
SYNCS = dict(
    n1=(8, LANES, ONCE),
    n2=(8, LANES, ONCE),
    gap=(8, LANES, HEIGHT),
    na=(8, LANES, DP),
    no=(8, 4 * LANES, TWICE),
    n1b=(8, LANES, ONCE),
    n2b=(8, LANES, ONCE),
    gapb=(8, LANES, HEIGHT),
    nab=(8, LANES, DP),
    nob=(8, 2 * LANES, TWICE),
    dnob=(8, 2 * LANES, TWICE),
    dattb=(8, 2 * LANES, HEIGHT),
    dnab=(8, LANES, DP),
    dn2b=(8, LANES, ONCE),
    dn1b=(8, LANES, ONCE),
    dno=(8, 3 * LANES, TWICE),
    datt=(8, 2 * LANES, HEIGHT),
    dna=(8, LANES, DP),
    dn2=(8, LANES, ONCE),
    dn1=(8, LANES, ONCE),
)
SEMAPHORES = 384
SMALL = dict(e2=0, q=16, e1=32)


def offsets():
    first = types.SimpleNamespace(
        reduce=0,
        split=C_MID,
        attend=3 * C_MID,
        output=3 * C_MID + C_ATT,
        shortcut=3 * C_MID + C_ATT + C_OUT,
    )
    base = 3 * C_MID + C_ATT + 2 * C_OUT
    second = types.SimpleNamespace(
        reduce=base,
        split=base + C_MID,
        attend=base + 3 * C_MID,
        output=base + 3 * C_MID + C_ATT,
    )
    total = base + 3 * C_MID + C_ATT + C_OUT
    first.bias = total
    second.bias = total + 2 * C_MID
    return (first, second)


GAIN_LEN = 6 * C_MID + 2 * C_ATT + 3 * C_OUT
SHIFT_LEN = GAIN_LEN + 4 * C_MID
GAIN_ROWS = 48
SHIFT_ROWS = 56


def stage_sizes(kind, nd, nh):
    deep = nd // 2
    deep = (deep,) if deep <= 8 else (8, deep // 8)
    if kind == HEIGHT:
        return (nh,)
    if kind == DP:
        return (nd,) if nd <= 8 else deep + (2,)
    return (nd * nh,) if kind == ONCE and nd * nh <= 32 else (2 * nh,) + deep


def row_table(per_device):
    table = {}
    at = 0
    parts = dict(
        s1=per_device[tag.s1],
        o1=per_device[tag.o1],
        sh=per_device[tag.sh],
        r2=per_device[tag.r2],
        s2=per_device[tag.s2],
        o2=per_device[tag.o2],
        r1=per_device[tag.r1],
        gs=16,
        q=per_device[tag.q1] + per_device[tag.q2],
        e1=per_device[tag.e1],
        e2=per_device[tag.e2],
    )
    for name, count in parts.items():
        table[name] = (at, count)
        at += count
    return table, at


def dot(left, right, dims=NN):
    return lax.dot_general(left, right, dims, preferred_element_type=FLOAT)


def exact(left, right, dims=NN):
    return lax.dot_general(left, right, dims, preferred_element_type=FLOAT, precision=HIGHEST)


def sigmoid(values):
    return 0.5 * jnp.tanh(0.5 * values) + 0.5


def slope_of(values):
    logistic = sigmoid(values)
    return logistic * (1.0 + values * (1.0 - logistic))


def widen(part, columns):
    return jnp.concatenate([part] * (columns // LANES), axis=1)


def fold(values):
    rows, columns = values.shape
    return jnp.sum(values.reshape(rows // 8, 8, columns), axis=0)


def iota(shape, axis):
    return lax.broadcasted_iota(jnp.int32, shape, axis)


def ones_where(condition, kind=BFLOAT):
    return jnp.where(condition, 1.0, 0.0).astype(FLOAT).astype(kind)


def shuffle(count, rows, blocks, back=False):
    new = iota((count, count), 1 if back else 0)
    old = iota((count, count), 0 if back else 1)
    hit = None
    for block in range(blocks):
        same = old == blocks * new - blocks * block * rows + block
        hit = same if hit is None else hit | same
    return hit


def kernel(cfg, names, *refs):
    R = types.SimpleNamespace(**dict(zip(names, refs)))
    nd, nh, inside = cfg.nd, cfg.nh, cfg.inside
    d, h = lax.axis_index(tag.dp), lax.axis_index(tag.height)
    first, second = offsets()
    used = [0]
    late = []
    share = 1.0 if inside else 1.0 / nh

    def new_sem():
        used[0] += 1
        assert used[0] <= SEMAPHORES
        return R.sem.at[used[0] - 1]

    def remote(source, target, send, receive, device):
        return pltpu.make_async_remote_copy(
            src_ref=source,
            dst_ref=target,
            send_sem=send,
            recv_sem=receive,
            device_id=device,
            device_id_type=MESH,
        )

    def wait_for(ref, sem):
        pltpu.make_async_copy(ref, ref, sem).wait()

    x, z = lax.rem(d, 2), lax.div(d, 2)
    plane = (2 * nh, 2 * h + x, lambda q: (2 * z + lax.rem(q, 2), lax.div(q, 2)))
    if nd <= 16:
        depth = [(nd // 2, z, lambda q: (2 * q + x, h))]
    else:
        high = nd // 16
        z_low, z_high = lax.div(z, high), lax.rem(z, high)
        depth = [
            (8, z_low, lambda q: (2 * (q * high + z_high) + x, h)),
            (high, z_high, lambda q: (2 * (z_low * high + q) + x, h)),
        ]
    along_dp = [(nd, d, lambda q: (q, h))] if nd <= 8 else depth + [(2, x, lambda q: (2 * z + q, h))]
    along_height = (nh, h, lambda q: (d, q))
    every = (nd * nh, d * nh + h, lambda q: (lax.div(q, nh), lax.rem(q, nh)))
    small_mesh = nd * nh <= 32
    stages_of = {
        HEIGHT: [along_height],
        DP: along_dp,
        ONCE: [every] if small_mesh else [plane] + depth,
        TWICE: [plane] + depth,
    }

    class Exchange:
        def __init__(self, name, m):
            self.stages = stages_of[SYNCS[name][2]]
            self.bufs = [
                getattr(R, "sy_" + name + str(m) + str(k)) for k in range(len(self.stages))
            ]

        def put(self, vectors, at=0, fill=True):
            slot = self.bufs[0].at[self.stages[0][1]]
            rows, lanes = slot.shape
            for vector in vectors:
                for k in range(vector.shape[1] // LANES):
                    column = at // rows * LANES
                    slot[at % rows : at % rows + 1, column : column + LANES] = vector[
                        :, k * LANES : (k + 1) * LANES
                    ]
                    at += 1
            while fill and at < rows * lanes // LANES:
                column = at // rows * LANES
                stop = min(rows, at % rows + rows * lanes // LANES - at)
                slot[at % rows : stop, column : column + LANES] = jnp.zeros(
                    (stop - at % rows, LANES), FLOAT
                )
                at += stop - at % rows

        def send(self, stage):
            count, me, peer = self.stages[stage]
            buf = self.bufs[stage]
            send, self.receive = new_sem(), new_sem()
            for step in range(1, count):
                to = lax.rem(me + step, count)
                remote(buf.at[me], buf.at[me], send, self.receive, peer(to)).start()
            late.append(lambda: wait_for(buf.at[pl.ds(0, count - 1)], send))

        def start(self, vectors):
            self.put(vectors)
            self.send(0)

        def finish(self):
            for stage, (count, me, _) in enumerate(self.stages):
                buf = self.bufs[stage]
                if stage > 0:
                    buf[me] = total
                    self.send(stage)
                yield
                wait_for(buf.at[pl.ds(0, count - 1)], self.receive)
                total = jnp.sum(buf[...], axis=0)
            return total

    def take(total, at, length):
        rows = total.shape[0]
        parts = []
        for k in range(at, at + length // LANES):
            column = k // rows * LANES
            parts.append(total[k % rows : k % rows + 1, column : column + LANES])
        return jnp.concatenate(parts, axis=1)

    if inside:
        Z, X, Y, C = nd // 2, 2, nh // 2, 2
        y, c = lax.div(h, 2), lax.rem(h, 2)
        table = cfg.table
        G = R.pack

        def in_plane(step):
            to = lax.rem(x * Y + y + step, X * Y)
            return lax.div(to, Y), lax.rem(to, Y)

        class Gather:
            def __init__(self, start, stop, direct=False):
                self.rows = pl.ds(start, stop - start)
                self.direct = direct
                self.phase = -1
                self.sends = []
                self.waits = []

            def send(self, part, to):
                send, receive = new_sem(), new_sem()
                remote(part, part, send, receive, to).start()
                self.sends.append(lambda: wait_for(part, send))
                self.waits.append(lambda: wait_for(part, receive))

            def step(self):
                for wait in self.waits:
                    wait()
                self.waits = []
                self.phase += 1
                if self.phase == 0:
                    own = G.at[z, x, y, c, self.rows]
                    if self.direct:
                        count = Z * X * Y
                        for step in range(1, count):
                            to = lax.rem(d * Y + y + step, count)
                            self.send(own, (lax.div(to, Y), lax.rem(to, Y) * 2 + c))
                        self.phase = 1
                    else:
                        for step in range(1, Z):
                            self.send(own, (lax.rem(z + step, Z) * 2 + x, h))
                elif self.phase == 1:
                    for step in range(1, X * Y):
                        xx, yy = in_plane(step)
                        self.send(G.at[:, x, y, c, self.rows], (z * 2 + xx, yy * 2 + c))
                elif self.phase == 2:
                    self.send(G.at[:, :, :, c, self.rows], (d, y * 2 + 1 - c))

            def finish(self):
                while self.phase < 3:
                    self.step()

            def sent(self):
                for wait in self.sends:
                    wait()

        class Scatter:
            def __init__(self, start, stop):
                self.rows = pl.ds(start, stop - start)
                self.phase = -1
                self.waits = []

            def begin(self, source, target, to):
                send, receive = new_sem(), new_sem()
                remote(source, target, send, receive, to).start()
                late.append(lambda: wait_for(source, send))
                self.waits.append(lambda: wait_for(target, receive))

            def step(self):
                rows = self.rows
                for wait in self.waits:
                    wait()
                self.waits = []
                self.phase += 1
                if self.phase == 0:
                    self.begin(G.at[:, :, :, 1 - c, rows], R.rc.at[:, :, :, rows], (d, y * 2 + 1 - c))
                elif self.phase == 1:

                    def add(zz, _):
                        for xx in range(X):
                            for yy in range(Y):
                                mine = G[zz, xx, yy, c, rows].astype(FLOAT)
                                G[zz, xx, yy, c, rows] = (
                                    mine + R.rc[zz, xx, yy, rows].astype(FLOAT)
                                ).astype(BFLOAT)
                        return 0

                    lax.fori_loop(0, Z, add, 0)
                    for step in range(1, X * Y):
                        xx, yy = in_plane(step)
                        self.begin(
                            G.at[:, xx, yy, c, rows],
                            R.rp.at[step - 1, :, rows],
                            (z * 2 + xx, yy * 2 + c),
                        )
                elif self.phase == 2:

                    def add(zz, _):
                        total = G[zz, x, y, c, rows].astype(FLOAT)
                        for k in range(X * Y - 1):
                            total = total + R.rp[k, zz, rows].astype(FLOAT)
                        G[zz, x, y, c, rows] = total.astype(BFLOAT)
                        return 0

                    lax.fori_loop(0, Z, add, 0)
                    for step in range(1, Z):
                        to = lax.rem(z + step, Z)
                        self.begin(
                            G.at[to, x, y, c, rows], R.rz.at[step - 1, rows], (to * 2 + x, h)
                        )

            def finish(self):
                while self.phase < 3:
                    self.step()

        def scattered(name):
            start, count = table[name]
            rows = pl.ds(start, count)
            total = G[z, x, y, c, rows].astype(FLOAT)
            for k in range(Z - 1):
                total = total + R.rz[k, rows].astype(FLOAT)
            return total

        def own_rows(name, values):
            start, count = table[name]
            G[z, x, y, c, start : start + count] = values.astype(BFLOAT)

        def per_dev(name):
            return SHAPES[name][0] // (nd * nh)

        def pack_shards(*parts):
            for name in parts:
                rows, blocks = per_dev(name), SHAPES[name][1] // LANES
                order = ones_where(shuffle(rows * blocks, rows, blocks))
                own_rows(name, dot(order, getattr(R, "a_" + name)[...]))

        def pack_small():
            own_rows(
                "q", jnp.concatenate([R.a_q1[...].astype(FLOAT), R.a_q2[...].astype(FLOAT)], axis=0)
            )
            own_rows(tag.e1, R.a_e1[...])
            own_rows(tag.e2, R.a_e2[...])

        def unpack_rows(name):
            rows, blocks = per_dev(name), SHAPES[name][1] // LANES
            start = table[name][0]
            full = getattr(R, "w_" + name)
            for block in range(blocks):
                at = start + block * rows
                full[:, block * LANES : (block + 1) * LANES] = G[
                    :, :, :, :, at : at + rows, :
                ].reshape(nd * nh * rows, LANES)

        def unpack_pairs(name):
            blocks = SHAPES[name][1] // LANES
            start = table[name][0]
            full = getattr(R, "w_" + name)
            for pair in range(blocks // 2):
                at = start + 16 * pair
                both = G[:, :, :, :, at : at + 16, :].astype(FLOAT).reshape(nd * nh, 2, 8, LANES)
                for one in range(2):
                    block = 2 * pair + one
                    full[:, block * LANES : (block + 1) * LANES] = (
                        both[:, one].reshape(nd * nh * 8, LANES).astype(BFLOAT)
                    )

        def unpack_split(name):
            start, count = table[name]
            full = getattr(R, "w_" + name)
            rows = per_dev(name)
            group = nh * rows

            def body(j, _):
                zz, xx = lax.div(j, 2), lax.rem(j, 2)
                part = G[zz, xx, :, :, start : start + count, :].astype(FLOAT)
                part = part.reshape(nh, 2, rows, LANES)
                at = pl.ds(pl.multiple_of(j * group, group), group)
                for block in range(2):
                    full[at, block * LANES : (block + 1) * LANES] = (
                        part[:, block].reshape(group, LANES).astype(BFLOAT)
                    )
                return 0

            lax.fori_loop(0, nd, body, 0)

        def unpack_attention():
            at = table[tag.q][0]
            both = G[:, :, :, :, at : at + 16, :].astype(FLOAT).reshape(nd * nh, 2, 8, LANES)
            R.w_q1[...] = both[:, 0].reshape(C_MID, C_ATT)
            R.w_q2[...] = both[:, 1].reshape(C_MID, C_ATT)
            for name in (tag.e1, tag.e2):
                at = table[name][0]
                part = G[:, :, :, :, at : at + 16, :].reshape(4 * C_ATT, LANES)
                for block in range(4):
                    pick = ones_where(
                        iota((C_ATT, 4 * C_ATT), 1) == 4 * iota((C_ATT, 4 * C_ATT), 0) + block
                    )
                    getattr(R, "w_" + name)[:, block * LANES : (block + 1) * LANES] = dot(pick, part)

        def unpack_gains():
            at = table[tag.gs][0]
            part = G[:, :, :, :, at : at + 16, :].reshape(16 * nd * nh, LANES)
            for full, rows, first_row, length in (
                (R.gains, GAIN_ROWS, 0, GAIN_LEN // (nd * nh)),
                (R.shifts, SHIFT_ROWS, 3, SHIFT_LEN // (nd * nh)),
            ):
                shape = (rows, 16 * nd * nh)
                source = iota(shape, 1)
                row = (source & 15) - first_row
                target = (((source >> 4) * length) >> 7) + row
                hit = (row >= 0) & (row < 3) & (target == iota(shape, 0))
                full[...] = dot(ones_where(hit), part)

        def emit(name, at, values):
            start = table[name][0] if name[0] != "q" else 0
            rows = per_dev(name)
            if rows % 16 == 0:
                for block in range(values.shape[1] // LANES):
                    to = start + (at // LANES + block) * rows
                    part = values[:, block * LANES : (block + 1) * LANES].astype(BFLOAT)
                    G[:, :, :, :, to : to + rows, :] = part.reshape(Z, X, Y, C, rows, LANES)
            elif name[0] == "o":
                for pair in range(values.shape[1] // (2 * LANES)):
                    to = start + (at // LANES + 2 * pair) * 8
                    both = [
                        values[:, (2 * pair + one) * LANES : (2 * pair + one + 1) * LANES].reshape(
                            nd * nh, 8, LANES
                        )
                        for one in range(2)
                    ]
                    part = jnp.concatenate(both, axis=1).astype(BFLOAT)
                    G[:, :, :, :, to : to + 16, :] = part.reshape(Z, X, Y, C, 16, LANES)
            elif name[0] == "e":
                part = None
                for block in range(4):
                    place = ones_where(
                        iota((4 * C_ATT, C_ATT), 0) == 4 * iota((4 * C_ATT, C_ATT), 1) + block, FLOAT
                    )
                    term = exact(place, values[:, block * LANES : (block + 1) * LANES])
                    part = term if part is None else part + term
                at = SMALL[name]
                R.small[:, :, at : at + 16, :] = part.reshape(nd, nh, 16, LANES)
            elif name[0] == "q":
                getattr(R, "g_" + name)[...] = values

        def emit_squeezes():
            both = [part[...].reshape(nd * nh, 8, LANES) for part in (R.g_q1, R.g_q2)]
            part = jnp.concatenate(both, axis=1)
            at = SMALL[tag.q]
            R.small[:, :, at : at + 16, :] = part.reshape(nd, nh, 16, LANES)

        class SmallScatter:
            def __init__(self, start, count):
                self.rows = pl.ds(start, count)

            def start(self):
                send, self.receive = new_sem(), new_sem()
                rows = self.rows
                for step in range(1, nd):
                    to = lax.rem(d + step, nd)
                    source, target = R.small.at[to, h, rows], R.small_in.at[d, rows]
                    remote(source, target, send, self.receive, (to, h)).start()
                late.append(lambda: wait_for(R.small_in.at[pl.ds(0, nd - 1), rows], send))

            def finish(self):
                wait_for(R.small_in.at[pl.ds(0, nd - 1), self.rows], self.receive)
                total = R.small[d, h, self.rows]
                for step in range(1, nd):
                    total = total + R.small_in[lax.rem(d + step, nd), self.rows]
                return total

        def emit_split(name, g):
            start, count = table[name]
            rows = per_dev(name)
            group = nh * rows

            def body(j, _):
                zz, xx = lax.div(j, 2) + g * (Z // 2), lax.rem(j, 2)
                at = pl.ds(pl.multiple_of(j * group, group), group)
                both = [
                    R.grad[at, block * LANES : (block + 1) * LANES].reshape(nh, rows, LANES)
                    for block in range(2)
                ]
                part = jnp.concatenate(both, axis=1).astype(BFLOAT)
                G[zz, xx, :, :, start : start + count, :] = part.reshape(Y, C, count, LANES)
                return 0

            lax.fori_loop(0, nd // 2, body, 0)

        def deliver(name):
            rows, blocks = per_dev(name), SHAPES[name][1] // LANES
            order = ones_where(shuffle(rows * blocks, rows, blocks, back=True), FLOAT)
            getattr(R, "d_" + name)[...] = exact(order, scattered(name))

        def range_of(*parts):
            return (table[parts[0]][0], table[parts[-1]][0] + table[parts[-1]][1])

        gather_first = Gather(*range_of(tag.r1, tag.gs), direct=True)
        gather_split = Gather(*range_of(tag.s1))
        gather_small = Gather(*range_of(tag.q, tag.e2), direct=True)
        gather_outer = Gather(*range_of(tag.o1, tag.sh))
        gather_last = Gather(*range_of(tag.r2, tag.o2))
        sums = dict(
            o2=Scatter(*range_of(tag.o2)),
            s2=Scatter(*range_of(tag.s2)),
            r2=Scatter(*range_of(tag.r2)),
            mid=Scatter(*range_of(tag.o1, tag.sh)),
            s1=Scatter(*range_of(tag.s1)),
            r1=Scatter(*range_of(tag.r1)),
        )
        small_two, small_one = SmallScatter(0, 16), SmallScatter(16, 32)
    else:

        def emit(name, at, values):
            getattr(R, "d_" + name)[:, at : at + values.shape[1]] = values

        def emit_split(name, g):
            half = R.grad.shape[0]
            getattr(R, "d_" + name)[g * half : (g + 1) * half, :] = R.grad[...]

    def vector(ref, at, length):
        row = at // LANES
        return jnp.concatenate([ref[row + k : row + k + 1, :] for k in range(length // LANES)], axis=1)

    def store_vector(m, ref, at, values):
        row = at // LANES
        for k in range(values.shape[1] // LANES):
            part = values[:, k * LANES : (k + 1) * LANES]
            ref[row + k : row + k + 1, :] = part if m == 0 else ref[row + k : row + k + 1, :] + part

    def over_images(m, body):
        def step(i, _):
            body(m * MB + i)
            return 0

        lax.fori_loop(0, MB, step, 0)

    one = types.SimpleNamespace(
        suffix="", W=H, px=cfg.rows * H, hp=(cfg.rows + 2) * H, place=first, mk=R.mk1, edge=R.edge1, p1=R.p1,
        a3=R.a3, p2=R.p2, s=R.s, dp2=R.dp2, dmix=R.dmix, dy1=R.dmix, dp1=R.dp1, c1=R.c_n1, c2=R.c_n2, group=1,
        split=R.w_s1, squeeze=R.w_q1, expand=R.w_e1, att=R.att1, dgap=R.dgap1, count=0, keep=R.keep1, k="1",
    )
    two = types.SimpleNamespace(
        suffix="b", W=H // 2, px=cfg.rows * H // 4, hp=(cfg.rows // 2 + 2) * H // 2, place=second, mk=R.mk2,
        edge=R.edge2, p1=R.p1b, a3=R.a3b, p2=R.p2b, s=R.sb, dp2=R.dp2b, dmix=R.dmixb, dy1=R.dmixb, dp1=R.dp1b,
        c1=R.c_n1b, c2=R.c_n2b, group=MB, split=R.w_s2, squeeze=R.w_q2, expand=R.w_e2, att=R.att2,
        dgap=R.dgap2, count=2, keep=R.keep2, k="2",
    )
    px1, px2 = one.px, two.px
    edge_rows = H

    def images_of(m):
        return pl.ds(m * MB, MB)

    def build_masks(block):
        bits = block.W.bit_length() - 1
        shape = (block.hp, LANES)
        pixel = iota(shape, 0)
        column = pixel & (block.W - 1)
        place = iota(block.edge.shape[1:], 0) & (block.W - 1)
        block.edge[0] = ones_where(place != 0, FLOAT)
        block.edge[1] = ones_where(place != block.W - 1, FLOAT)
        row = (pixel >> bits) - 1 + h * (block.px // block.W)
        for i in range(NIM):
            limit = (H - STEP * (2 - R.groups[i])) // (1 if block is one else 2)
            inside_grid = (row >= 0) & (row < limit) & (column < limit)
            block.mk[i] = ones_where(inside_grid, FLOAT)

    def clear(ref):
        ref[...] = jnp.zeros(ref.shape, ref.dtype)

    def totals(m, kinds, columns):
        return [
            jnp.sum(R.acc[m, kind, :, :columns], axis=0, keepdims=True) for kind in range(kinds)
        ]

    def clear_acc(m, kinds, columns):
        for kind in range(kinds):
            R.acc[m, kind, :, :columns] = jnp.zeros((8, columns), FLOAT)

    def chunk_of(columns):
        return 32 if columns <= 512 else 16

    def stat_pass(m, source, start, px, columns, mk, mask_start):
        chunk = chunk_of(columns)
        clear_acc(m, 2, columns)

        def body(i):
            total, square = R.acc[m, 0, :, :columns], R.acc[m, 1, :, :columns]
            for t in range(0, px, chunk):
                v = source[i, start + t : start + t + chunk, :]
                vm = v * widen(mk[i, mask_start + t : mask_start + t + chunk, :], columns)
                total = total + fold(vm)
                square = square + fold(vm * v)
            R.acc[m, 0, :, :columns] = total
            R.acc[m, 1, :, :columns] = square

        over_images(m, body)
        return totals(m, 2, columns)

    def inverse_count(block, m, columns):
        return widen(R.counts[block.count + m : block.count + m + 1, :], columns)

    def norm_coef(m, coef, total, at, columns, block, offset):
        gain, shift = vector(R.gains, offset, columns), vector(R.shifts, offset, columns)
        inverse = inverse_count(block, m, columns)
        step = columns // LANES
        centre = take(total, at, columns) * inverse
        scaled = lax.rsqrt(take(total, at + step, columns) * inverse - centre * centre + EPSILON)
        coef[m, 0:1, :] = gain * scaled
        coef[m, 1:2, :] = shift - centre * (gain * scaled)
        coef[m, 2:3, :] = scaled
        coef[m, 3:4, :] = -centre * scaled

    def norm_coef_back(m, coef, total, at_sum, at_along, columns, block, offset):
        inverse = inverse_count(block, m, columns)
        summed, along = take(total, at_sum, columns), take(total, at_along, columns)
        scale = -coef[m, 0:1, :] * inverse
        coef[m, 4:5, :] = scale * (summed + along * coef[m, 3:4, :])
        coef[m, 5:6, :] = scale * along * coef[m, 2:3, :]
        store_vector(m, R.all_shifts, offset, summed)
        store_vector(m, R.all_gains, offset, along)

    class Halo:
        def __init__(self, down=None, up=None):
            self.ways = []
            for pair, step in ((down, 1), (up, -1)):
                if pair is not None:
                    sends = h < nh - 1 if step == 1 else h > 0
                    gets = h > 0 if step == 1 else h < nh - 1
                    copy = remote(pair[0], pair[1], new_sem(), new_sem(), (d, h + step))
                    self.ways.append((sends, gets, copy))

        def start(self):
            for sends, _, copy in self.ways:
                pl.when(sends)(copy.start)
            late.append(self.sent)

        def finish(self):
            for _, gets, copy in self.ways:
                pl.when(gets)(copy.wait_recv)

        def sent(self):
            for sends, _, copy in self.ways:
                pl.when(sends)(copy.wait_send)
            self.ways = []

    def rims(m, block, ref):
        image, width = images_of(m), block.W
        return Halo(
            (ref.at[image, pl.ds(block.px, width)], ref.at[image, pl.ds(0, width)]),
            (ref.at[image, pl.ds(width, width)], ref.at[image, pl.ds(block.hp - width, width)]),
        )

    def clear_rim(block, ref):
        shape = (NIM, block.W, ref.shape[-1])

        @pl.when(h == 0)
        def _():
            ref[:, : block.W, :] = jnp.zeros(shape, ref.dtype)

        @pl.when(h == nh - 1)
        def _():
            ref[:, block.hp - block.W :, :] = jnp.zeros(shape, ref.dtype)

    def activate(m, block):
        half = C_MID // 2

        def body(i):
            mask = block.mk[i]
            for g in range(2):
                cols = slice(g * half, (g + 1) * half)
                value = block.c1[m, 0:1, cols] * block.p1[i, :, cols] + block.c1[m, 1:2, cols]
                value = value * sigmoid(value) * mask
                if block is one:
                    R.a_sum[m, :, cols] = R.a_sum[m, :, cols] + fold(
                        value[block.W : block.W + block.px]
                    )
                at = 3 * g * half
                left = pltpu.roll(value, 1, 0) * block.edge[0, : block.hp]
                right = pltpu.roll(value, block.hp - 1, 0) * block.edge[1, : block.hp]
                block.a3[i, :, at : at + half] = left.astype(BFLOAT)
                block.a3[i, :, at + half : at + 2 * half] = value.astype(BFLOAT)
                block.a3[i, :, at + 2 * half : at + 3 * half] = right.astype(BFLOAT)

        over_images(m, body)

    def rows_of(ref, i, count, start, rows, cols):
        part = ref[pl.ds(i, count), start : start + rows, cols]
        return part.reshape(count * rows, part.shape[-1])

    def convolve(m, block):
        half = C_MID // 2
        for g in range(2):
            cols = slice(3 * g * half, 3 * (g + 1) * half)
            taps = [
                rows_of(block.a3, m * MB, MB, dy * block.W, block.px, cols) for dy in range(3)
            ]
            matrix = block.split[9 * g * half : 9 * (g + 1) * half, :]
            result = dot(jnp.concatenate(taps, axis=1), matrix)
            block.p2[images_of(m), :, g * C_MID : (g + 1) * C_MID] = result.reshape(
                MB, block.px, C_MID
            )

    def split_activate(m, block):
        columns = 2 * C_MID

        def body(i):
            gap = jnp.zeros((8, C_MID), FLOAT)
            for t in range(0, block.px, 32):
                at = slice(t, t + 32)
                mask = widen(block.mk[i, block.W + t : block.W + t + 32, :], columns)
                value = block.c2[m, 0:1, :] * block.p2[i, at, :] + block.c2[m, 1:2, :]
                value = value * sigmoid(value) * mask
                block.s[i, at, :] = value
                gap = gap + fold(value[:, :C_MID] + value[:, C_MID:])
            R.image_sums[i, :, :C_MID] = gap

        over_images(m, body)

    def image_rows(m, columns):
        return [
            jnp.sum(R.image_sums[i, :, :columns], axis=0, keepdims=True)
            for i in range(m * MB, (m + 1) * MB)
        ]

    def inverse_area(block, i):
        limit = (H - STEP * (2 - R.groups[i])) // (1 if block is one else 2)
        side = jnp.full((1, C_MID), limit.astype(FLOAT))
        return 1.0 / (side * side)

    def attend(m, block, window_gap, window_norm):
        suffix = block.suffix
        gap, norm = Exchange(tag.gap + suffix, m), Exchange(tag.na + suffix, m)
        split_activate(m, block)
        gap.start(image_rows(m, C_MID))
        window_gap()
        total = yield from gap.finish()
        keep = block.keep.at[m]
        for k in range(MB):
            keep[0, k : k + 1, :C_MID] = take(total, 2 * k, C_MID) * inverse_area(block, m * MB + k)
        before = exact(keep[0, :, :C_MID], block.squeeze[...])
        norm.start(
            [
                jnp.sum(before, axis=0, keepdims=True),
                jnp.sum(before * before, axis=0, keepdims=True),
            ]
        )
        window_norm()
        total = yield from norm.finish()
        count = MB * nd
        centre = total[0:1] / count
        scaled = lax.rsqrt(total[1:2] / count - centre * centre + EPSILON)
        normal = (before - centre) * scaled
        gain = vector(R.gains, block.place.attend, C_ATT)
        shift = vector(R.shifts, block.place.attend, C_ATT)
        normed = gain * normal + shift
        hidden = normed * sigmoid(normed)
        keep[1, :, :C_ATT] = normal
        keep[2, :, :C_ATT] = normed
        keep[3, :, :C_ATT] = hidden
        keep[4, 0:1, :C_ATT] = gain * scaled
        logits = exact(hidden, block.expand[...]) + vector(R.shifts, block.place.bias, 2 * C_MID)
        gap_logit = logits[:, :C_MID] - logits[:, C_MID:]
        keep[5, :, :] = jnp.concatenate([sigmoid(gap_logit), sigmoid(-gap_logit)], axis=1)
        for k in range(MB):
            block.att[m * MB + k] = jnp.broadcast_to(keep[5, k : k + 1, :], (8, 2 * C_MID))

    def mix(m, block, target, start):
        def body(i):
            for t in range(0, block.px, 32):
                at = slice(t, t + 32)
                value = (
                    block.att[i, 0:1, :C_MID] * block.s[i, at, :C_MID]
                    + block.att[i, 0:1, C_MID:] * block.s[i, at, C_MID:]
                )
                target[i, start + t : start + t + 32, :] = value.astype(BFLOAT)

        over_images(m, body)

    def attend_back(m, block, window_att, window_norm):
        suffix = block.suffix

        def body(i):
            parts = [jnp.zeros((8, C_MID), FLOAT)] * 2
            for t in range(0, block.px, 32):
                at = slice(t, t + 32)
                grad = block.dmix[i, at, :]
                for j in range(2):
                    parts[j] = parts[j] + fold(grad * block.s[i, at, j * C_MID : (j + 1) * C_MID])
            R.image_sums[i] = jnp.concatenate(parts, axis=1)

        over_images(m, body)
        heights, norm = Exchange(tag.datt + suffix, m), Exchange(tag.dna + suffix, m)
        heights.start(image_rows(m, 2 * C_MID))
        window_att()
        total = yield from heights.finish()
        keep = block.keep.at[m]
        for k in range(MB):
            keep[6, k : k + 1, :] = take(total, 4 * k, 2 * C_MID)
        att = keep[5]
        weighted = att * keep[6]
        both = weighted[:, :C_MID] + weighted[:, C_MID:]
        grad_logits = weighted - att * jnp.concatenate([both, both], axis=1)
        keep[6] = grad_logits
        grad_hidden = exact(grad_logits, block.expand[...], NT)
        grad_normed = grad_hidden * slope_of(keep[2, :, :C_ATT])
        normal = keep[1, :, :C_ATT]
        norm.start(
            [
                jnp.sum(grad_normed, axis=0, keepdims=True),
                jnp.sum(grad_normed * normal, axis=0, keepdims=True),
                jnp.sum(grad_logits, axis=0, keepdims=True),
            ]
        )
        window_norm()
        total = yield from norm.finish()
        count = MB * nd
        store_vector(m, R.all_shifts, block.place.attend, total[0:1])
        store_vector(m, R.all_gains, block.place.attend, total[1:2])
        store_vector(m, R.all_shifts, block.place.bias, take(total, 2, 2 * C_MID))
        grad_before = keep[4, 0:1, :C_ATT] * (grad_normed - (total[0:1] + normal * total[1:2]) / count)
        keep[7, :, :C_ATT] = grad_before
        grad_gap = exact(grad_before, block.squeeze[...], NT)
        for k in range(MB):
            row = grad_gap[k : k + 1, :] * inverse_area(block, m * MB + k)
            block.dgap[m * MB + k] = jnp.broadcast_to(row, (8, C_MID))

    def small_grads(block, squeeze):
        left, right, wide = (0, 7, C_ATT) if squeeze else (3, 6, 2 * C_MID)
        tall = C_MID if squeeze else C_ATT
        total = None
        for m in range(MICRO):
            term = exact(block.keep[m, left, :, :tall], block.keep[m, right, :, :wide], TN)
            total = term if total is None else total + term
        emit((tag.q if squeeze else tag.e) + block.k, 0, total * share)

    def split_back(m, block):
        clear_acc(m, 2, 2 * C_MID)

        def body(i):
            for j in range(2):
                cols = slice(j * C_MID, (j + 1) * C_MID)
                total, along = R.acc[m, 0, :, cols], R.acc[m, 1, :, cols]
                for t in range(0, block.px, 32):
                    at = slice(t, t + 32)
                    mask = widen(block.mk[i, block.W + t : block.W + t + 32, :], C_MID)
                    raw = block.p2[i, at, cols]
                    value = block.c2[m, 0:1, cols] * raw + block.c2[m, 1:2, cols]
                    grad = block.att[i, 0:1, cols] * block.dmix[i, at, :] + block.dgap[i, 0:1, :]
                    grad = grad * slope_of(value) * mask
                    block.s[i, at, cols] = grad
                    total = total + fold(grad)
                    along = along + fold(
                        grad * (block.c2[m, 2:3, cols] * raw + block.c2[m, 3:4, cols])
                    )
                R.acc[m, 0, :, cols] = total
                R.acc[m, 1, :, cols] = along

        over_images(m, body)

    def norm_back(m, block_px, grad, coef, raw, raw_start, mk, mask_start, target, start, columns, sums_=False):
        chunk = chunk_of(columns)
        if sums_:
            R.acc[m, 2, :, :columns] = jnp.zeros((8, columns), FLOAT)

        def body(i):
            for t in range(0, block_px, chunk):
                mask = widen(mk[i, mask_start + t : mask_start + t + chunk, :], columns)
                value = (
                    coef[m, 0:1, :] * grad[i, t : t + chunk, :]
                    + coef[m, 4:5, :]
                    + coef[m, 5:6, :] * raw[i, raw_start + t : raw_start + t + chunk, :]
                )
                value = (value * mask).astype(BFLOAT)
                target[i, start + t : start + t + chunk, :] = value
                if sums_:
                    R.acc[m, 2, :, :columns] = R.acc[m, 2, :, :columns] + fold(value.astype(FLOAT))

        over_images(m, body)

    def mean_activation():
        return 0.5 * (R.centre[0:1, :] + R.centre[1:2, :])

    def product_of_means(g):
        half = C_MID // 2
        cols = slice(g * C_MID, (g + 1) * C_MID)
        eye = iota((half, half), 0) == iota((half, half), 1)
        row = jnp.broadcast_to(mean_activation()[:, g * half : (g + 1) * half], (half, half))
        column = jnp.sum(jnp.where(eye, row, 0.0), axis=1, keepdims=True)
        return column * (R.grad_sum[0:1, cols] + R.grad_sum[1:2, cols])

    def mean_term():
        half = C_MID // 2
        rows = SHAPES[tag.s1][0] // (nd * nh)
        index = d * nh + h
        low = index * rows < 9 * half
        mean = mean_activation()
        centre = jnp.where(low, mean[:, :half], mean[:, half:])
        sums_ = R.grad_sum[2:3, :] + R.grad_sum[3:4, :]
        sums_ = jnp.where(low, sums_[:, :C_MID], sums_[:, C_MID:])
        shape = (2 * rows, LANES)
        row = iota(shape, 0)
        hit = iota(shape, 1) == ((index * rows + (row >> 1)) & (half - 1))
        column = jnp.sum(
            jnp.where(hit, jnp.broadcast_to(centre, shape), 0.0), axis=1, keepdims=True
        )
        odd = (row & 1) == 1
        return column * jnp.where(
            odd, jnp.broadcast_to(sums_[:, LANES:], shape), jnp.broadcast_to(sums_[:, :LANES], shape)
        )

    def kernel_grad(block, g):
        half = C_MID // 2
        images = MB if block.group == 1 else NIM
        for dy in range(3):
            at = slice(3 * dy * half, 3 * (dy + 1) * half)
            total = None
            for i in range(0, NIM, images):
                taps = rows_of(
                    block.a3, i, images, dy * block.W, block.px, slice(3 * g * half, 3 * (g + 1) * half)
                )
                grad = rows_of(
                    block.dp2, i, images, block.W, block.px, slice(g * C_MID, (g + 1) * C_MID)
                )
                term = dot(taps, grad, TN)
                total = term if total is None else total + term
            if inside and block is one:
                total = total - jnp.concatenate([product_of_means(g)] * 3, axis=0)
            R.grad[at, :] = total

    def convolve_back(m, block):
        half = C_MID // 2
        clear_acc(m, 2, C_MID)

        def body(i, count):
            rows = count * block.px
            for g in range(2):
                cols = slice(g * half, (g + 1) * half)
                total = None
                for dy in range(3):
                    grad = rows_of(
                        block.dp2, i, count, (2 - dy) * block.W, block.px, slice(g * C_MID, (g + 1) * C_MID)
                    )
                    at = 9 * g * half + 3 * dy * half
                    term = dot(grad, block.split[at : at + 3 * half, :], NT)
                    total = term if total is None else total + term
                value = (
                    total[:, half : 2 * half]
                    + pltpu.roll(total[:, :half], rows - 1, 0) * block.edge[1, :rows]
                    + pltpu.roll(total[:, 2 * half :], 1, 0) * block.edge[0, :rows]
                )
                raw = rows_of(block.p1, i, count, block.W, block.px, cols)
                mask = rows_of(block.mk, i, count, block.W, block.px, slice(0, LANES))
                before = block.c1[m, 0:1, cols] * raw + block.c1[m, 1:2, cols]
                value = value * slope_of(before) * mask
                block.dy1[pl.ds(i, count), :, cols] = value.reshape(count, block.px, half)
                normal = block.c1[m, 2:3, cols] * raw + block.c1[m, 3:4, cols]
                R.acc[m, 0, :, cols] = R.acc[m, 0, :, cols] + fold(value)
                R.acc[m, 1, :, cols] = R.acc[m, 1, :, cols] + fold(value * normal)

        if block.group == 1:
            over_images(m, lambda i: body(i, 1))
        else:
            body(m * MB, MB)

    def splat_back(m, block, window_att, window_norm, window_split, window_halo, window_reduce):
        suffix = block.suffix
        yield from attend_back(m, block, window_att, window_norm)
        split_back(m, block)
        exchange = Exchange(tag.dn2 + suffix, m)
        exchange.start(totals(m, 2, 2 * C_MID))
        window_split()
        total = yield from exchange.finish()
        norm_coef_back(m, block.c2, total, 0, 4, 2 * C_MID, block, block.place.split)
        norm_back(
            m, block.px, block.s, block.c2, block.p2, 0, block.mk, block.W, block.dp2, block.W, 2 * C_MID,
            sums_=block is one,
        )
        block.halo[m] = rims(m, block, block.dp2)
        block.halo[m].start()
        if block is one:
            R.grad_sum[m : m + 1, :] = jnp.sum(R.acc[m, 2, :, : 2 * C_MID], axis=0, keepdims=True)
        window_halo()
        yield
        block.halo[m].finish()
        convolve_back(m, block)
        exchange = Exchange(tag.dn1 + suffix, m)
        sums_ = totals(m, 2, C_MID)
        if block is one:
            sums_.append(R.grad_sum[m : m + 1, :])
        exchange.start(sums_)
        window_reduce()
        total = yield from exchange.finish()
        if block is one:
            R.grad_sum[2 + m : 3 + m, :] = take(total, 4, 2 * C_MID)
        norm_coef_back(m, block.c1, total, 0, 2, C_MID, block, block.place.reduce)
        norm_back(
            m, block.px, block.dy1, block.c1, block.p1, block.W, block.mk, block.W, block.dp1, 0, C_MID
        )

    def nothing():
        pass

    def when_last(m, *steps):
        def window():
            if m == MICRO - 1:
                for step in steps:
                    step()

        return window

    def step_of(name):
        return sums[name].step if inside else nothing

    def hand_out(*parts):
        def step():
            if inside:
                for name in parts:
                    deliver(name)

        return step

    def outer(m, ref, columns):
        return ref[images_of(m)].reshape(MB * px2, columns)

    def product_out(m, source, inner, matrix, target):
        for at in range(0, C_OUT, 256):
            target[images_of(m), :, at : at + 256] = dot(
                outer(m, source, inner), matrix[:, at : at + 256]
            ).reshape(MB, px2, 256)

    def grad_outer(name, source, inner, grad):
        def step():
            left = source[...].reshape(NIM * px2, inner)
            for at in range(0, C_OUT, 256):
                part = grad[:, :, at : at + 256].reshape(NIM * px2, 256)
                emit(name, at, dot(left, part, TN))

        return step

    def grad_reduce_two():
        left = R.l1[...].reshape(NIM * px2, C_OUT)
        right = R.dp1b[...].reshape(NIM * px2, C_MID)
        for at in range(0, C_MID, LANES):
            emit(tag.r2, at, dot(left, right[:, at : at + LANES], TN))

    def grad_split(block):
        def step():
            for g in range(2):
                kernel_grad(block, g)
                emit_split(tag.s + block.k, g)

        return step

    def gradients_sent():
        if inside:
            for gather in (gather_first, gather_split, gather_small, gather_outer, gather_last):
                gather.sent()

    halo_x = Halo(
        (R.images.at[:, pl.ds(px1 - edge_rows, edge_rows)], R.xh.at[:, pl.ds(0, edge_rows)]),
        (R.images.at[:, pl.ds(0, edge_rows)], R.xh.at[:, pl.ds(one.hp - edge_rows, edge_rows)]),
    )
    barrier = pltpu.get_barrier_semaphore()
    partners = 0
    groups = [every] if small_mesh else [along_height, plane] + along_dp + depth
    for count, me, peer in groups:
        for step in range(1, count):
            to = peer(lax.rem(me + step, count))
            pl.semaphore_signal(barrier, inc=1, device_id=to, device_id_type=MESH)
        partners += count - 1
    load_x = pltpu.make_async_copy(R.images, R.xh.at[:, pl.ds(edge_rows, px1)], new_sem())
    load_cot = pltpu.make_async_copy(R.cotangent, R.cot, new_sem())
    load_x.start()
    load_cot.start()
    if inside:
        pack_shards(tag.r1)
        own_rows(tag.gs, R.gs[...])
    pl.semaphore_wait(barrier, partners)
    if inside:
        gather_first.step()
    halo_x.start()
    if inside:
        pack_shards(tag.s1)
        gather_split.step()
        pack_small()
    build_masks(one)

    def pool_matrices():
        out_shape = (px2, px1 + edge_rows)
        out_pixel, in_pixel = iota(out_shape, 0), iota(out_shape, 1)
        down = (in_pixel >> 5) - 2 * (out_pixel >> 4)
        along = (in_pixel & 31) - 2 * (out_pixel & 15) + 1
        R.pool3[...] = ones_where((down >= 0) & (down < 3) & (along >= 0) & (along < 3))
        out_shape = (px2, px1)
        out_pixel, in_pixel = iota(out_shape, 0), iota(out_shape, 1)
        cell = ((in_pixel >> 6) == (out_pixel >> 4)) & (((in_pixel & 31) >> 1) == (out_pixel & 15))
        R.pool2[...] = jnp.where(cell, 0.25, 0.0).astype(FLOAT).astype(BFLOAT)

    def spread_matrices():
        back_shape = (px1, px2)
        in_pixel, out_pixel = iota(back_shape, 0), iota(back_shape, 1)
        cell = ((in_pixel >> 6) == (out_pixel >> 4)) & (((in_pixel & 31) >> 1) == (out_pixel & 15))
        R.spread2[...] = jnp.where(cell, 0.25, 0.0).astype(FLOAT).astype(BFLOAT)
        back_shape = (px1, px2 + two.W)
        in_pixel, out_pixel = iota(back_shape, 0), iota(back_shape, 1)
        down = (in_pixel >> 5) + 1 - 2 * (out_pixel >> 4)
        along = (in_pixel & 31) + 1 - 2 * (out_pixel & 15)
        R.spread3[...] = ones_where((down >= 0) & (down < 3) & (along >= 0) & (along < 3))

    pool_matrices()
    clear_rim(one, R.xh)
    if inside:
        gather_first.step()
    clear(R.a_sum)
    clear(R.keep1)
    clear(R.keep2)
    load_x.wait()
    halo_x.finish()
    if inside:
        gather_first.finish()
        unpack_rows(tag.r1)
        unpack_gains()
        gather_split.step()

    def prepare_rest():
        if inside:
            gather_small.step()
            pack_shards(tag.o1, tag.sh)
            gather_outer.step()
            pack_shards(tag.r2, tag.s2, tag.o2)
        build_masks(two)
        clear_rim(two, R.p1b)

    def window_split_sums():
        if inside:
            gather_outer.step()
        spread_matrices()
        clear_rim(one, R.dp2)
        clear_rim(two, R.dp2b)

        @pl.when(h == 0)
        def _():
            R.v1[:, :edge_rows, :] = jnp.zeros((NIM, edge_rows, C_MID), BFLOAT)

        @pl.when(h == nh - 1)
        def _():
            R.dq[:, px2:, :] = jnp.zeros((NIM, two.W, C_MID), BFLOAT)

    def window_gap():
        if inside:
            gather_small.finish()
            unpack_attention()
            gather_last.step()

    def window_mix():
        if inside:
            gather_outer.finish()
            unpack_rows(tag.sh)
            unpack_pairs(tag.o1)
            gather_last.step()

    def window_output():
        if inside:
            gather_last.step()
            gather_last.finish()
            unpack_rows(tag.r2)
            unpack_split(tag.s2)
            unpack_pairs(tag.o2)

    def first_sum(m, i, at):
        return (
            R.c_o1[m, 0:1, :] * R.o1[i, at, :]
            + R.c_sh[m, 0:1, :] * R.csh[i, at, :]
            + (R.c_o1[m, 1:2, :] + R.c_sh[m, 1:2, :])
        )

    one.halo, two.halo = {}, {}

    def chain(m):
        mine = images_of(m)

        def body(i):
            R.p1[i] = dot(R.xh[i], R.w_r1[...])

        over_images(m, body)
        exchange = Exchange(tag.n1, m)
        cells = jnp.zeros((8, LANES), FLOAT)
        for i in range(m * MB, (m + 1) * MB):
            cells = cells + fold(R.mk1[i, one.W : one.W + px1, :])
        exchange.start(
            stat_pass(m, R.p1, one.W, px1, C_MID, R.mk1, one.W)
            + [jnp.sum(cells, axis=0, keepdims=True)]
        )

        def body(i):
            R.t1[i] = dot(R.pool2[...], R.xh[i, edge_rows : edge_rows + px1, :]).astype(BFLOAT)

        over_images(m, body)
        when_last(m, prepare_rest)()
        total = yield from exchange.finish()
        R.counts[m : m + 1, :] = 1.0 / total[4:5, :]
        R.counts[2 + m : 3 + m, :] = 4.0 / total[4:5, :]
        norm_coef(m, R.c_n1, total, 0, C_MID, one, first.reduce)
        if inside and m == 0:
            gather_split.step()
        activate(m, one)
        if inside and m == 0:
            gather_split.finish()
            unpack_split(tag.s1)
        convolve(m, one)
        exchange = Exchange(tag.n2, m)
        exchange.start(stat_pass(m, R.p2, 0, px1, 2 * C_MID, R.mk1, one.W))
        when_last(m, window_split_sums)()
        total = yield from exchange.finish()
        norm_coef(m, R.c_n2, total, 0, 2 * C_MID, one, first.split)
        if inside and m == 0:
            gather_small.step()
        yield from attend(m, one, when_last(m, window_gap), nothing)
        mix(m, one, R.v1, edge_rows)
        halo = Halo((R.v1.at[mine, pl.ds(px1, edge_rows)], R.v1.at[mine, pl.ds(0, edge_rows)]))
        halo.start()
        when_last(m, window_mix)()
        yield
        product_out(m, R.t1, C_IN, R.w_sh, R.csh)
        exchange = Exchange(tag.no, m)
        exchange.put(stat_pass(m, R.csh, 0, px2, C_OUT, R.mk2, two.W), 16)
        halo.finish()

        def body(i):
            R.q1[i] = (dot(R.pool3[...], R.v1[i]) * (1.0 / 9.0)).astype(BFLOAT)

        over_images(m, body)
        product_out(m, R.q1, C_MID, R.w_o1, R.o1)
        exchange.put(stat_pass(m, R.o1, 0, px2, C_OUT, R.mk2, two.W), fill=False)
        exchange.send(0)
        when_last(m, window_output)()
        total = yield from exchange.finish()
        norm_coef(m, R.c_o1, total, 0, C_OUT, two, first.output)
        norm_coef(m, R.c_sh, total, 16, C_OUT, two, first.shortcut)

        def body(i):
            for t in range(0, px2, 16):
                at = slice(t, t + 16)
                value = first_sum(m, i, at)
                mask = widen(R.mk2[i, two.W + t : two.W + t + 16, :], C_OUT)
                R.l1[i, at, :] = (value * sigmoid(value) * mask).astype(BFLOAT)

        over_images(m, body)
        store_one = pltpu.make_async_copy(R.l1.at[mine], R.layer_one.at[mine], new_sem())
        store_one.start()
        late.append(store_one.wait)

        R.p1b[mine, two.W : two.W + px2, :] = dot(outer(m, R.l1, C_OUT), R.w_r2[...]).reshape(
            MB, px2, C_MID
        )
        exchange = Exchange(tag.n1b, m)
        exchange.start(
            stat_pass(m, R.p1b, two.W, px2, C_MID, R.mk2, two.W)
            + [jnp.sum(R.a_sum[m], axis=0, keepdims=True)]
        )
        halo = rims(m, two, R.p1b)
        halo.start()
        total = yield from exchange.finish()
        R.centre[m : m + 1, :] = take(total, 4, C_MID) * widen(R.counts[m : m + 1, :], C_MID)
        norm_coef(m, R.c_n1b, total, 0, C_MID, two, second.reduce)
        halo.finish()
        activate(m, two)
        convolve(m, two)
        exchange = Exchange(tag.n2b, m)
        exchange.start(stat_pass(m, R.p2b, 0, px2, 2 * C_MID, R.mk2, two.W))
        total = yield from exchange.finish()
        norm_coef(m, R.c_n2b, total, 0, 2 * C_MID, two, second.split)
        yield from attend(m, two, nothing, nothing)
        mix(m, two, R.mix2, 0)
        product_out(m, R.mix2, C_MID, R.w_o2, R.o2)
        exchange = Exchange(tag.nob, m)
        exchange.start(stat_pass(m, R.o2, 0, px2, C_OUT, R.mk2, two.W))
        if m == 0:
            load_cot.wait()
        total = yield from exchange.finish()
        norm_coef(m, R.c_o2, total, 0, C_OUT, two, second.output)

        clear_acc(m, 2, C_OUT)

        def body(i):
            total, along = R.acc[m, 0], R.acc[m, 1]
            for t in range(0, px2, 16):
                at = slice(t, t + 16)
                mask = widen(R.mk2[i, two.W + t : two.W + t + 16, :], C_OUT)
                raw = R.o2[i, at, :]
                value = R.c_o2[m, 0:1, :] * raw + R.c_o2[m, 1:2, :] + R.l1[i, at, :].astype(FLOAT)
                logistic = sigmoid(value)
                R.dpo[i, at, :] = (value * logistic * mask).astype(BFLOAT)
                grad = (
                    R.cot[i, at, :].astype(FLOAT) * mask * (logistic * (1.0 + value * (1.0 - logistic)))
                )
                R.g2[i, at, :] = grad
                total = total + fold(grad)
                along = along + fold(grad * (R.c_o2[m, 2:3, :] * raw + R.c_o2[m, 3:4, :]))
            R.acc[m, 0] = total
            R.acc[m, 1] = along

        over_images(m, body)
        exchange = Exchange(tag.dnob, m)
        exchange.start(totals(m, 2, C_OUT))
        store_two = pltpu.make_async_copy(R.dpo.at[mine], R.layer_two.at[mine], new_sem())
        store_two.start()
        total = yield from exchange.finish()
        norm_coef_back(m, R.c_o2, total, 0, 8, C_OUT, two, second.output)
        store_two.wait()
        norm_back(m, px2, R.g2, R.c_o2, R.o2, 0, R.mk2, two.W, R.dpo, 0, C_OUT)
        R.dmixb[mine] = dot(outer(m, R.dpo, C_OUT), R.w_o2[...], NT).reshape(MB, px2, C_MID)
        yield from splat_back(
            m,
            two,
            when_last(
                m, gradients_sent, grad_outer(tag.o2, R.mix2, C_MID, R.dpo), step_of(tag.o2)
            ),
            when_last(m, lambda: small_grads(two, False), step_of(tag.o2)),
            when_last(
                m,
                lambda: small_grads(two, True),
                step_of(tag.o2),
                small_two.start if inside else nothing,
            ),
            when_last(m, grad_split(two), step_of(tag.s2), step_of(tag.o2)),
            when_last(m, step_of(tag.s2)),
        )

        clear_acc(m, 3, C_OUT)
        R.o2[mine] = dot(outer(m, R.dp1b, C_MID), R.w_r2[...], NT).reshape(MB, px2, C_OUT)

        def body(i):
            sums_ = [R.acc[m, kind] for kind in range(3)]
            for t in range(0, px2, 16):
                at = slice(t, t + 16)
                mask = widen(R.mk2[i, two.W + t : two.W + t + 16, :], C_OUT)
                value = first_sum(m, i, at)
                grad = (R.g2[i, at, :] + R.o2[i, at, :]) * mask * slope_of(value)
                R.g2[i, at, :] = grad
                sums_[0] = sums_[0] + fold(grad)
                sums_[1] = sums_[1] + fold(
                    grad * (R.c_o1[m, 2:3, :] * R.o1[i, at, :] + R.c_o1[m, 3:4, :])
                )
                sums_[2] = sums_[2] + fold(
                    grad * (R.c_sh[m, 2:3, :] * R.csh[i, at, :] + R.c_sh[m, 3:4, :])
                )
            for kind in range(3):
                R.acc[m, kind] = sums_[kind]

        over_images(m, body)
        exchange = Exchange(tag.dno, m)
        exchange.start(totals(m, 3, C_OUT))
        when_last(m, grad_reduce_two, step_of(tag.r2), step_of(tag.s2))()
        total = yield from exchange.finish()
        norm_coef_back(m, R.c_o1, total, 0, 8, C_OUT, two, first.output)
        norm_coef_back(m, R.c_sh, total, 0, 16, C_OUT, two, first.shortcut)
        norm_back(m, px2, R.g2, R.c_o1, R.o1, 0, R.mk2, two.W, R.dpo, 0, C_OUT)
        R.dq[mine, :px2, :] = (
            (dot(outer(m, R.dpo, C_OUT), R.w_o1[...], NT) * (1.0 / 9.0))
            .astype(BFLOAT)
            .reshape(MB, px2, C_MID)
        )
        halo = Halo(up=(R.dq.at[mine, pl.ds(0, two.W)], R.dq.at[mine, pl.ds(px2, two.W)]))
        halo.start()
        norm_back(m, px2, R.g2, R.c_sh, R.csh, 0, R.mk2, two.W, R.cot, 0, C_OUT)
        when_last(m, step_of(tag.r2), step_of(tag.s2))()
        yield
        halo.finish()

        def body(i):
            R.dmix[i] = dot(R.spread3[...], R.dq[i])

        over_images(m, body)

        def window_split():
            R.t1[...] = (
                dot(R.cot[...].reshape(NIM * px2, C_OUT), R.w_sh[...], NT)
                .astype(BFLOAT)
                .reshape(NIM, px2, C_IN)
            )
            small_grads(one, True)
            if inside:
                emit_squeezes()
                small_one.start()

        def finish_two():
            if inside:
                R.d_e2[...] = small_two.finish()

        yield from splat_back(
            m,
            one,
            when_last(
                m,
                grad_outer(tag.o1, R.q1, C_MID, R.dpo),
                grad_outer(tag.sh, R.t1, C_IN, R.cot),
                step_of(tag.mid),
                step_of(tag.r2),
            ),
            when_last(m, lambda: small_grads(one, False), step_of(tag.mid), hand_out(tag.o2, tag.s2)),
            when_last(m, window_split, step_of(tag.mid), step_of(tag.r2)),
            when_last(m, grad_split(one), step_of(tag.s1)),
            when_last(m, step_of(tag.s1), step_of(tag.mid), hand_out(tag.r2, tag.o1, tag.sh), finish_two),
        )
        term = dot(rows_of(R.xh, m * MB, MB, edge_rows, px1, slice(0, C_IN)), rows_of(R.dp1, m * MB, MB, 0, px1, slice(0, C_MID)), TN)
        if m == 0:
            R.grad[:C_IN, :] = term
        else:
            emit(tag.r1, 0, R.grad[:C_IN, :] + term)

    chains = [chain(m) for m in range(MICRO)]
    while chains:
        for one_chain in list(chains):
            if next(one_chain, tag) is tag:
                chains.remove(one_chain)

    if inside:
        sums[tag.r1].step()
        sums[tag.s1].step()
    store_images = new_sem()
    own = pl.ds(edge_rows, px1)

    def image_grads(m):
        one.halo[m].sent()

        def body(i):
            value = dot(R.dp1[i], R.w_r1[...], NT) + dot(R.spread2[...], R.t1[i])
            R.dp2[i, own, :] = value.astype(BFLOAT)
            pltpu.make_async_copy(R.dp2.at[i, own], R.grad_images.at[i], store_images).start()

        over_images(m, body)

    image_grads(0)
    if inside:
        sums[tag.r1].step()
    image_grads(1)
    if inside:
        sums[tag.r1].step()
        sums[tag.s1].step()
        deliver(tag.s1)
        R.d_s1[...] = R.d_s1[...] + mean_term()
        total = small_one.finish()
        R.d_q1[...] = total[:8]
        R.d_q2[...] = total[8:16]
        R.d_e1[...] = total[16:]
    index = d * nh + h
    for full, target, length in (
        (R.all_gains, R.d_gains, GAIN_LEN // (nd * nh)),
        (R.all_shifts, R.d_shifts, SHIFT_LEN // (nd * nh)),
    ):
        start = index * length
        lane = start & (LANES - 1)
        turned = pltpu.roll(full[pl.ds(start >> 7, 8), :], lax.rem(LANES - lane, LANES), 1)
        here = iota((2, LANES), 1) < LANES - lane
        target[...] = jnp.where(here, turned[0:2], turned[1:3])
    if inside:
        sums[tag.r1].step()
        deliver(tag.r1)
        for group in sums.values():
            assert group.phase == 3
    wait_for(R.dp2.at[:, own], store_images)
    for wait in late:
        wait()


def per_device(nd, nh, images, size_group, cotangent, *params):
    weights, (norm_gains, norm_shifts) = params[:11], params[11:]
    devices = nd * nh
    rows = images.shape[1]
    px1 = rows * H
    px2 = px1 // 4
    hp1, hp2 = px1 + 2 * H, px2 + H
    per_rows = {name: weight.shape[0] // LANES for name, weight in zip(SHAPES, weights)}
    inside = (
        nh == 4
        and devices == 32
        and per_rows[tag.q1] == 8
        and all(inner % devices == 0 for inner, _ in SHAPES.values())
    )
    axes = (tag.dp, tag.height)
    index = lax.axis_index(axes)
    cfg = types.SimpleNamespace(nd=nd, nh=nh, inside=inside, rows=rows)

    operands, names, specs = [], [], []
    whole = pl.BlockSpec(memory_space=pltpu.VMEM)

    def operand(name, value, spec=whole):
        operands.append(value)
        names.append(name)
        specs.append(spec)

    operand(tag.groups, size_group, pl.BlockSpec(memory_space=pltpu.SMEM))
    operand(tag.images, images.reshape(NIM, px1, C_IN), pl.BlockSpec(memory_space=pl.ANY))
    operand(tag.cotangent, cotangent.reshape(NIM, px2, C_OUT), pl.BlockSpec(memory_space=pl.ANY))
    if inside:
        pieces = []
        for vector in (norm_gains, norm_shifts):
            lane = lax.rem(index * vector.shape[0], LANES)
            piece = lax.dynamic_update_slice(jnp.zeros((3 * LANES,), BFLOAT), vector, (lane,))
            pieces.append(piece.reshape(3, LANES))
        operand(tag.gs, jnp.pad(jnp.concatenate(pieces, axis=0), ((0, 10), (0, 0))))
        for name, weight in zip(SHAPES, weights):
            operand(tag.a_ + name, weight.reshape(-1, LANES))
        cfg.table, total_rows = row_table(per_rows)
        summed_rows = sum(cfg.table[tag.r1])
    else:
        for name, weight in zip(SHAPES, weights):
            full = lax.all_gather(weight, axes, axis=0, tiled=True).reshape(SHAPES[name])
            operand(tag.w_ + name, full.astype(FLOAT) if name[0] in "qe" else full)
        for name, vector, length in (
            (tag.gains, norm_gains, GAIN_ROWS),
            (tag.shifts, norm_shifts, SHIFT_ROWS),
        ):
            full = lax.all_gather(vector, axes, axis=0, tiled=True).astype(FLOAT)
            full = jnp.pad(full, (0, length * LANES - full.shape[0]))
            operand(name, full.reshape(length, LANES))

    outs = dict(
        layer_one=((NIM, px2, C_OUT), BFLOAT),
        layer_two=((NIM, px2, C_OUT), BFLOAT),
        grad_images=((NIM, px1, C_IN), BFLOAT),
    )
    for name, shape in SHAPES.items():
        outs["d_" + name] = ((per_rows[name], LANES) if inside else shape, FLOAT)
    outs[tag.d_gains] = ((2, LANES), FLOAT)
    outs[tag.d_shifts] = ((2, LANES), FLOAT)

    scratch = dict(
        xh=((NIM, hp1, C_IN), BFLOAT),
        cot=((NIM, px2, C_OUT), BFLOAT),
        mk1=((NIM, hp1, LANES), FLOAT),
        mk2=((NIM, hp2, LANES), FLOAT),
        edge1=((2, hp1, LANES), FLOAT),
        edge2=((2, MB * px2, LANES), FLOAT),
        counts=((8, LANES), FLOAT),
        all_gains=((GAIN_ROWS, LANES), FLOAT),
        all_shifts=((SHIFT_ROWS, LANES), FLOAT),
        a_sum=((MICRO, 8, C_MID), FLOAT),
        centre=((8, C_MID), FLOAT),
        grad_sum=((8, 2 * C_MID), FLOAT),
        acc=((MICRO, 3, 8, C_OUT), FLOAT),
        image_sums=((NIM, 8, 2 * C_MID), FLOAT),
        p1=((NIM, hp1, C_MID), FLOAT),
        a3=((NIM, hp1, 3 * C_MID), BFLOAT),
        p2=((NIM, px1, 2 * C_MID), FLOAT),
        s=((NIM, px1, 2 * C_MID), FLOAT),
        v1=((NIM, px1 + H, C_MID), BFLOAT),
        q1=((NIM, px2, C_MID), BFLOAT),
        t1=((NIM, px2, C_IN), BFLOAT),
        o1=((NIM, px2, C_OUT), FLOAT),
        csh=((NIM, px2, C_OUT), FLOAT),
        p1b=((NIM, hp2, C_MID), FLOAT),
        a3b=((NIM, hp2, 3 * C_MID), BFLOAT),
        p2b=((NIM, px2, 2 * C_MID), FLOAT),
        sb=((NIM, px2, 2 * C_MID), FLOAT),
        mix2=((NIM, px2, C_MID), BFLOAT),
        l1=((NIM, px2, C_OUT), BFLOAT),
        o2=((NIM, px2, C_OUT), FLOAT),
        g2=((NIM, px2, C_OUT), FLOAT),
        dpo=((NIM, px2, C_OUT), BFLOAT),
        dmixb=((NIM, px2, C_MID), FLOAT),
        dp2b=((NIM, hp2, 2 * C_MID), BFLOAT),
        dp1b=((NIM, px2, C_MID), BFLOAT),
        dq=((NIM, px2 + H // 2, C_MID), BFLOAT),
        dmix=((NIM, px1, C_MID), FLOAT),
        dp2=((NIM, hp1, 2 * C_MID), BFLOAT),
        dp1=((NIM, px1, C_MID), BFLOAT),
        grad=((9 * C_MID // 2, C_MID), FLOAT),
        pool3=((px2, px1 + H), BFLOAT),
        pool2=((px2, px1), BFLOAT),
        spread2=((px1, px2), BFLOAT),
        spread3=((px1, px2 + H // 2), BFLOAT),
        keep1=((MICRO, 8, 8, 2 * C_MID), FLOAT),
        keep2=((MICRO, 8, 8, 2 * C_MID), FLOAT),
        att1=((NIM, 8, 2 * C_MID), FLOAT),
        att2=((NIM, 8, 2 * C_MID), FLOAT),
        dgap1=((NIM, 8, C_MID), FLOAT),
        dgap2=((NIM, 8, C_MID), FLOAT),
        c_n1=((MICRO, 8, C_MID), FLOAT),
        c_n2=((MICRO, 8, 2 * C_MID), FLOAT),
        c_o1=((MICRO, 8, C_OUT), FLOAT),
        c_sh=((MICRO, 8, C_OUT), FLOAT),
        c_n1b=((MICRO, 8, C_MID), FLOAT),
        c_n2b=((MICRO, 8, 2 * C_MID), FLOAT),
        c_o2=((MICRO, 8, C_OUT), FLOAT),
    )
    for name, (count, lanes, kind) in SYNCS.items():
        for k, size in enumerate(stage_sizes(kind, nd, nh)):
            for m in range(MICRO):
                scratch["sy_" + name + str(m) + str(k)] = ((size, count, lanes), FLOAT)
    if inside:
        four = (nd // 2, 2, nh // 2, 2)
        scratch |= dict(
            pack=(four + (total_rows, LANES), BFLOAT),
            rc=(four[:3] + (summed_rows, LANES), BFLOAT),
            rp=((3,) + four[:1] + (summed_rows, LANES), BFLOAT),
            rz=((four[0] - 1, summed_rows, LANES), BFLOAT),
            small=((nd, nh, 48, LANES), FLOAT),
            small_in=((nd, 48, LANES), FLOAT),
            gains=((GAIN_ROWS, LANES), FLOAT),
            shifts=((SHIFT_ROWS, LANES), FLOAT),
            g_q1=((C_MID, C_ATT), FLOAT),
            g_q2=((C_MID, C_ATT), FLOAT),
        )
        for name, shape in SHAPES.items():
            scratch["w_" + name] = (shape, FLOAT if name[0] in "qe" else BFLOAT)

    results = pl.pallas_call(
        functools.partial(
            kernel, cfg, names + list(outs) + list(scratch) + [tag.sem]
        ),
        out_shape=[jax.ShapeDtypeStruct(shape, kind) for shape, kind in outs.values()],
        in_specs=specs,
        out_specs=[pl.BlockSpec(memory_space=pl.ANY)] * 3 + [whole] * (len(outs) - 3),
        scratch_shapes=[pltpu.VMEM(shape, kind) for shape, kind in scratch.values()]
        + [pltpu.SemaphoreType.DMA((SEMAPHORES,))],
        compiler_params=pltpu.CompilerParams(
            collective_id=0, has_side_effects=True, vmem_limit_bytes=62 * 1024 * 1024
        ),
    )(*operands)

    if inside:
        results = deliver_all(results)
    layer_one, layer_two, grad_images = results[:3]
    grads = [grad.reshape(-1) for grad in results[3:14]]
    if not inside:
        grads = [
            lax.psum_scatter(grad, axes, scatter_dimension=0, tiled=True) for grad in grads
        ]
    tails = [
        total.reshape(-1)[: vector.shape[0]] for total, vector in zip(results[14:], (norm_gains, norm_shifts))
    ]
    return (
        layer_one.reshape(cotangent.shape),
        layer_two.reshape(cotangent.shape),
        grad_images.reshape(images.shape),
        *grads,
        *tails,
    )


def copy_all(count, *refs):
    copies = [
        pltpu.make_async_copy(source, target, refs[-1].at[k])
        for k, (source, target) in enumerate(zip(refs[:count], refs[count : 2 * count]))
    ]
    for copy in copies:
        copy.start()
    for copy in copies:
        copy.wait()


def deliver_all(results):
    count = len(results)
    anywhere = pl.BlockSpec(memory_space=pl.ANY)
    return pl.pallas_call(
        functools.partial(copy_all, count),
        out_shape=[jax.ShapeDtypeStruct(value.shape, value.dtype) for value in results],
        in_specs=[pl.BlockSpec(memory_space=pltpu.VMEM)] * count,
        out_specs=[anywhere] * count,
        scratch_shapes=[pltpu.SemaphoreType.DMA((count,))],
    )(*results)


def solution(mesh):
    shard = P(("dp", "height"))
    rows = P("dp", "height", None, None)
    return jax.shard_map(
        functools.partial(per_device, mesh.shape["dp"], mesh.shape["height"]),
        mesh=mesh,
        in_specs=(rows, P("dp"), rows) + (shard,) * 13,
        out_specs=(rows,) * 3 + (shard,) * 13,
        check_vma=False,
    )
```

```python
import functools
import types

import jax
import jax.numpy as jnp
from jax import lax
from jax.experimental import pallas as pl
from jax.experimental.pallas import tpu as pltpu
from jax.sharding import PartitionSpec as P

C_IN = 512
C_MID = 256
C_ATT = 128
C_OUT = 1024
H = 32
STEP = 4
MICRO = 2
MB = 3

EPSILON = 1e-05
HIGHEST = lax.Precision.HIGHEST
FLOAT = jnp.float32
BFLOAT = jnp.bfloat16
MESH = pl.DeviceIdType.MESH
LANES = 128
NIM = MICRO * MB
NN = (((1,), (0,)), ((), ()))
NT = (((1,), (1,)), ((), ()))
TN = (((0,), (0,)), ((), ()))


class Names:
    def __getattr__(self, name):
        return name


tag = Names()

SHAPES = dict(
    r1=(C_IN, C_MID),
    s1=(9 * C_MID, C_MID),
    q1=(C_MID, C_ATT),
    e1=(C_ATT, 2 * C_MID),
    o1=(C_MID, C_OUT),
    sh=(C_IN, C_OUT),
    r2=(C_OUT, C_MID),
    s2=(9 * C_MID, C_MID),
    q2=(C_MID, C_ATT),
    e2=(C_ATT, 2 * C_MID),
    o2=(C_MID, C_OUT),
)

HEIGHT, DP, ONCE, TWICE = range(4)
SYNCS = dict(
    n1=(8, LANES, ONCE),
    n2=(8, LANES, ONCE),
    gap=(8, LANES, HEIGHT),
    na=(8, LANES, DP),
    no=(8, 4 * LANES, TWICE),
    n1b=(8, LANES, ONCE),
    n2b=(8, LANES, ONCE),
    gapb=(8, LANES, HEIGHT),
    nab=(8, LANES, DP),
    nob=(8, 2 * LANES, TWICE),
    dnob=(8, 2 * LANES, TWICE),
    dattb=(8, 2 * LANES, HEIGHT),
    dnab=(8, LANES, DP),
    dn2b=(8, LANES, ONCE),
    dn1b=(8, LANES, ONCE),
    dno=(8, 3 * LANES, TWICE),
    datt=(8, 2 * LANES, HEIGHT),
    dna=(8, LANES, DP),
    dn2=(8, LANES, ONCE),
    dn1=(8, LANES, ONCE),
)
SEMAPHORES = 640
SMALL = dict(e2=0, q=16, e1=32)


def offsets():
    first = types.SimpleNamespace(
        reduce=0,
        split=C_MID,
        attend=3 * C_MID,
        output=3 * C_MID + C_ATT,
        shortcut=3 * C_MID + C_ATT + C_OUT,
    )
    base = 3 * C_MID + C_ATT + 2 * C_OUT
    second = types.SimpleNamespace(
        reduce=base,
        split=base + C_MID,
        attend=base + 3 * C_MID,
        output=base + 3 * C_MID + C_ATT,
    )
    total = base + 3 * C_MID + C_ATT + C_OUT
    first.bias = total
    second.bias = total + 2 * C_MID
    return (first, second)


GAIN_LEN = 6 * C_MID + 2 * C_ATT + 3 * C_OUT
SHIFT_LEN = GAIN_LEN + 4 * C_MID
GAIN_ROWS = 48
SHIFT_ROWS = 56


def stage_sizes(kind, nd, nh):
    deep = nd // 2
    deep = (deep,) if deep <= 8 else (8, deep // 8)
    if kind == HEIGHT:
        return (nh,)
    if kind == DP:
        return (nd,) if nd <= 8 else deep + (2,)
    return (nd * nh,) if kind == ONCE and nd * nh <= 32 else (2 * nh,) + deep


def row_table(per_device):
    table = {}
    at = 0
    parts = dict(
        s1=per_device[tag.s1],
        o1=per_device[tag.o1],
        sh=per_device[tag.sh],
        r2=per_device[tag.r2],
        s2=per_device[tag.s2],
        o2=per_device[tag.o2],
        r1=per_device[tag.r1],
        gs=16,
        q=per_device[tag.q1] + per_device[tag.q2],
        e1=per_device[tag.e1],
        e2=per_device[tag.e2],
    )
    for name, count in parts.items():
        table[name] = (at, count)
        at += count
    return table, at


def dot(left, right, dims=NN):
    return lax.dot_general(left, right, dims, preferred_element_type=FLOAT)


def exact(left, right, dims=NN):
    return lax.dot_general(left, right, dims, preferred_element_type=FLOAT, precision=HIGHEST)


def sigmoid(values):
    return 0.5 * jnp.tanh(0.5 * values) + 0.5


def slope_of(values):
    logistic = sigmoid(values)
    return logistic * (1.0 + values * (1.0 - logistic))


def widen(part, columns):
    return jnp.concatenate([part] * (columns // LANES), axis=1)


def fold(values):
    rows, columns = values.shape
    return jnp.sum(values.reshape(rows // 8, 8, columns), axis=0)


def iota(shape, axis):
    return lax.broadcasted_iota(jnp.int32, shape, axis)


def ones_where(condition, kind=BFLOAT):
    return jnp.where(condition, 1.0, 0.0).astype(FLOAT).astype(kind)


def shuffle(count, rows, blocks, back=False):
    new = iota((count, count), 1 if back else 0)
    old = iota((count, count), 0 if back else 1)
    hit = None
    for block in range(blocks):
        same = old == blocks * new - blocks * block * rows + block
        hit = same if hit is None else hit | same
    return hit


def kernel(cfg, names, *refs):
    R = types.SimpleNamespace(**dict(zip(names, refs)))
    nd, nh, inside = cfg.nd, cfg.nh, cfg.inside
    d, h = lax.axis_index(tag.dp), lax.axis_index(tag.height)
    first, second = offsets()
    used = [0]
    late = []
    share = 1.0 if inside else 1.0 / nh

    def new_sem():
        used[0] += 1
        assert used[0] <= SEMAPHORES
        return R.sem.at[used[0] - 1]

    def remote(source, target, send, receive, device):
        return pltpu.make_async_remote_copy(
            src_ref=source,
            dst_ref=target,
            send_sem=send,
            recv_sem=receive,
            device_id=device,
            device_id_type=MESH,
        )

    def wait_for(ref, sem):
        pltpu.make_async_copy(ref, ref, sem).wait()

    x, z = lax.rem(d, 2), lax.div(d, 2)
    plane = (2 * nh, 2 * h + x, lambda q: (2 * z + lax.rem(q, 2), lax.div(q, 2)))
    if nd <= 16:
        depth = [(nd // 2, z, lambda q: (2 * q + x, h))]
    else:
        high = nd // 16
        z_low, z_high = lax.div(z, high), lax.rem(z, high)
        depth = [
            (8, z_low, lambda q: (2 * (q * high + z_high) + x, h)),
            (high, z_high, lambda q: (2 * (z_low * high + q) + x, h)),
        ]
    along_dp = [(nd, d, lambda q: (q, h))] if nd <= 8 else depth + [(2, x, lambda q: (2 * z + q, h))]
    along_height = (nh, h, lambda q: (d, q))
    every = (nd * nh, d * nh + h, lambda q: (lax.div(q, nh), lax.rem(q, nh)))
    small_mesh = nd * nh <= 32
    stages_of = {
        HEIGHT: [along_height],
        DP: along_dp,
        ONCE: [every] if small_mesh else [plane] + depth,
        TWICE: [plane] + depth,
    }

    class Exchange:
        def __init__(self, name, m):
            self.stages = stages_of[SYNCS[name][2]]
            self.bufs = [
                getattr(R, "sy_" + name + str(m) + str(k)) for k in range(len(self.stages))
            ]

        def put(self, vectors, at=0, fill=True):
            slot = self.bufs[0].at[self.stages[0][1]]
            rows, lanes = slot.shape
            for vector in vectors:
                for k in range(vector.shape[1] // LANES):
                    column = at // rows * LANES
                    slot[at % rows : at % rows + 1, column : column + LANES] = vector[
                        :, k * LANES : (k + 1) * LANES
                    ]
                    at += 1
            while fill and at < rows * lanes // LANES:
                column = at // rows * LANES
                stop = min(rows, at % rows + rows * lanes // LANES - at)
                slot[at % rows : stop, column : column + LANES] = jnp.zeros(
                    (stop - at % rows, LANES), FLOAT
                )
                at += stop - at % rows

        def send(self, stage):
            count, me, peer = self.stages[stage]
            buf = self.bufs[stage]
            send, self.receive = new_sem(), new_sem()
            for step in range(1, count):
                to = lax.rem(me + step, count)
                remote(buf.at[me], buf.at[me], send, self.receive, peer(to)).start()
            late.append(lambda: wait_for(buf.at[pl.ds(0, count - 1)], send))

        def start(self, vectors):
            self.put(vectors)
            self.send(0)

        def finish(self, between=None):
            for stage, (count, me, _) in enumerate(self.stages):
                buf = self.bufs[stage]
                if stage > 0:
                    buf[me] = total
                    self.send(stage)
                    if between is not None and stage == 1:
                        between()
                yield
                wait_for(buf.at[pl.ds(0, count - 1)], self.receive)
                total = jnp.sum(buf[...], axis=0)
            return total

    def take(total, at, length):
        rows = total.shape[0]
        parts = []
        for k in range(at, at + length // LANES):
            column = k // rows * LANES
            parts.append(total[k % rows : k % rows + 1, column : column + LANES])
        return jnp.concatenate(parts, axis=1)

    if inside:
        Z, X, Y, C = nd // 2, 2, nh // 2, 2
        y, c = lax.div(h, 2), lax.rem(h, 2)
        table = cfg.table
        G = R.pack

        def in_plane(step):
            to = lax.rem(x * Y + y + step, X * Y)
            return lax.div(to, Y), lax.rem(to, Y)

        class Gather:
            def __init__(self, start, stop, direct=False):
                self.rows = pl.ds(start, stop - start)
                self.direct = direct
                self.phase = -1
                self.sends = []
                self.waits = []

            def send(self, part, to):
                send, receive = new_sem(), new_sem()
                remote(part, part, send, receive, to).start()
                self.sends.append(lambda: wait_for(part, send))
                self.waits.append(lambda: wait_for(part, receive))

            def step(self):
                for wait in self.waits:
                    wait()
                self.waits = []
                self.phase += 1
                if self.phase == 0:
                    own = G.at[z, x, y, c, self.rows]
                    if self.direct:
                        count = Z * X * Y
                        for step in range(1, count):
                            to = lax.rem(d * Y + y + step, count)
                            self.send(own, (lax.div(to, Y), lax.rem(to, Y) * 2 + c))
                        self.phase = 1
                    else:
                        for step in range(1, Z):
                            self.send(own, (lax.rem(z + step, Z) * 2 + x, h))
                elif self.phase == 1:
                    for step in range(1, X * Y):
                        xx, yy = in_plane(step)
                        self.send(G.at[:, x, y, c, self.rows], (z * 2 + xx, yy * 2 + c))
                elif self.phase == 2:
                    self.send(G.at[:, :, :, c, self.rows], (d, y * 2 + 1 - c))

            def finish(self):
                while self.phase < 3:
                    self.step()

            def sent(self):
                for wait in self.sends:
                    wait()

        class Scatter:
            def __init__(self, start, stop, direct=False):
                self.rows = pl.ds(start, stop - start)
                self.direct = direct
                self.phase = -1
                self.waits = []

            def begin(self, source, target, to):
                send, receive = new_sem(), new_sem()
                remote(source, target, send, receive, to).start()
                late.append(lambda: wait_for(source, send))
                self.waits.append(lambda: wait_for(target, receive))

            def step(self):
                rows = self.rows
                for wait in self.waits:
                    wait()
                self.waits = []
                self.phase += 1
                if self.phase == 0:
                    self.begin(G.at[:, :, :, 1 - c, rows], R.rc.at[:, :, :, rows], (d, y * 2 + 1 - c))
                elif self.phase == 1:

                    def add(zz, _):
                        for xx in range(X):
                            for yy in range(Y):
                                mine = G[zz, xx, yy, c, rows].astype(FLOAT)
                                G[zz, xx, yy, c, rows] = (
                                    mine + R.rc[zz, xx, yy, rows].astype(FLOAT)
                                ).astype(BFLOAT)
                        return 0

                    lax.fori_loop(0, Z, add, 0)
                    if self.direct:
                        count = Z * X * Y
                        for step in range(1, count):
                            to = lax.rem(d * Y + y + step, count)
                            dd, yy = lax.div(to, Y), lax.rem(to, Y)
                            self.begin(
                                G.at[lax.div(dd, X), lax.rem(dd, X), yy, c, rows],
                                R.rd.at[step - 1],
                                (dd, yy * 2 + c),
                            )
                        self.phase = 2
                        return
                    for step in range(1, X * Y):
                        xx, yy = in_plane(step)
                        self.begin(
                            G.at[:, xx, yy, c, rows],
                            R.rp.at[step - 1, :, rows],
                            (z * 2 + xx, yy * 2 + c),
                        )
                elif self.phase == 2:

                    def add(zz, _):
                        total = G[zz, x, y, c, rows].astype(FLOAT)
                        for k in range(X * Y - 1):
                            total = total + R.rp[k, zz, rows].astype(FLOAT)
                        G[zz, x, y, c, rows] = total.astype(BFLOAT)
                        return 0

                    lax.fori_loop(0, Z, add, 0)
                    for step in range(1, Z):
                        to = lax.rem(z + step, Z)
                        self.begin(
                            G.at[to, x, y, c, rows], R.rz.at[step - 1, rows], (to * 2 + x, h)
                        )

            def finish(self):
                while self.phase < 3:
                    self.step()

        def scattered(name):
            start, count = table[name]
            rows = pl.ds(start, count)
            total = G[z, x, y, c, rows].astype(FLOAT)
            if name == tag.r1:
                for k in range(Z * X * Y - 1):
                    total = total + R.rd[k].astype(FLOAT)
                return total
            for k in range(Z - 1):
                total = total + R.rz[k, rows].astype(FLOAT)
            return total

        def own_rows(name, values):
            start, count = table[name]
            G[z, x, y, c, start : start + count] = values.astype(BFLOAT)

        def per_dev(name):
            return SHAPES[name][0] // (nd * nh)

        def pack_shards(*parts):
            for name in parts:
                rows, blocks = per_dev(name), SHAPES[name][1] // LANES
                order = ones_where(shuffle(rows * blocks, rows, blocks))
                own_rows(name, dot(order, getattr(R, "a_" + name)[...]))

        def pack_gains():
            clear(R.piece)
            lane_of = iota((1, LANES), 1)
            for k, length in enumerate((GAIN_LEN // (nd * nh), SHIFT_LEN // (nd * nh))):
                lane = lax.rem((d * nh + h) * length, LANES)
                turned = pltpu.roll(R.gs[...].astype(FLOAT), lane, 1)
                upper, lower = turned[2 * k : 2 * k + 1], turned[2 * k + 1 : 2 * k + 2]
                R.piece[3 * k : 3 * k + 1, :] = jnp.where(lane_of >= lane, upper, 0.0)
                R.piece[3 * k + 1 : 3 * k + 2, :] = jnp.where(lane_of < lane, upper, lower)
                R.piece[3 * k + 2 : 3 * k + 3, :] = jnp.where(lane_of < lane, lower, 0.0)
            own_rows(tag.gs, R.piece[...])

        def pack_small():
            own_rows(
                "q", jnp.concatenate([R.a_q1[...].astype(FLOAT), R.a_q2[...].astype(FLOAT)], axis=0)
            )
            own_rows(tag.e1, R.a_e1[...])
            own_rows(tag.e2, R.a_e2[...])

        def unpack_rows(name):
            rows, blocks = per_dev(name), SHAPES[name][1] // LANES
            start = table[name][0]
            full = getattr(R, "w_" + name)
            for block in range(blocks):
                at = start + block * rows
                full[:, block * LANES : (block + 1) * LANES] = G[
                    :, :, :, :, at : at + rows, :
                ].reshape(nd * nh * rows, LANES)

        def unpack_pairs(name):
            blocks = SHAPES[name][1] // LANES
            start = table[name][0]
            full = getattr(R, "w_" + name)
            for pair in range(blocks // 2):
                at = start + 16 * pair
                both = G[:, :, :, :, at : at + 16, :].astype(FLOAT).reshape(nd * nh, 2, 8, LANES)
                for one in range(2):
                    block = 2 * pair + one
                    full[:, block * LANES : (block + 1) * LANES] = (
                        both[:, one].reshape(nd * nh * 8, LANES).astype(BFLOAT)
                    )

        def unpack_split(name):
            start, count = table[name]
            full = getattr(R, "w_" + name)
            rows = per_dev(name)
            group = nh * rows

            def body(j, _):
                zz, xx = lax.div(j, 2), lax.rem(j, 2)
                part = G[zz, xx, :, :, start : start + count, :].astype(FLOAT)
                part = part.reshape(nh, 2, rows, LANES)
                at = pl.ds(pl.multiple_of(j * group, group), group)
                for block in range(2):
                    full[at, block * LANES : (block + 1) * LANES] = (
                        part[:, block].reshape(group, LANES).astype(BFLOAT)
                    )
                return 0

            lax.fori_loop(0, nd, body, 0)

        def unpack_attention():
            at = table[tag.q][0]
            both = G[:, :, :, :, at : at + 16, :].astype(FLOAT).reshape(nd * nh, 2, 8, LANES)
            R.w_q1[...] = both[:, 0].reshape(C_MID, C_ATT)
            R.w_q2[...] = both[:, 1].reshape(C_MID, C_ATT)
            for name in (tag.e1, tag.e2):
                at = table[name][0]
                part = G[:, :, :, :, at : at + 16, :].reshape(4 * C_ATT, LANES)
                for block in range(4):
                    pick = ones_where(
                        iota((C_ATT, 4 * C_ATT), 1) == 4 * iota((C_ATT, 4 * C_ATT), 0) + block
                    )
                    getattr(R, "w_" + name)[:, block * LANES : (block + 1) * LANES] = dot(pick, part)

        def unpack_gains():
            at = table[tag.gs][0]
            part = G[:, :, :, :, at : at + 16, :].reshape(16 * nd * nh, LANES)
            for full, rows, first_row, length in (
                (R.gains, GAIN_ROWS, 0, GAIN_LEN // (nd * nh)),
                (R.shifts, SHIFT_ROWS, 3, SHIFT_LEN // (nd * nh)),
            ):
                shape = (rows, 16 * nd * nh)
                source = iota(shape, 1)
                row = (source & 15) - first_row
                target = (((source >> 4) * length) >> 7) + row
                hit = (row >= 0) & (row < 3) & (target == iota(shape, 0))
                full[...] = dot(ones_where(hit), part)

        def emit(name, at, values):
            start = table[name][0] if name[0] != "q" else 0
            rows = per_dev(name)
            if rows % 16 == 0:
                for block in range(values.shape[1] // LANES):
                    to = start + (at // LANES + block) * rows
                    part = values[:, block * LANES : (block + 1) * LANES].astype(BFLOAT)
                    G[:, :, :, :, to : to + rows, :] = part.reshape(Z, X, Y, C, rows, LANES)
            elif name[0] == "o":
                for pair in range(values.shape[1] // (2 * LANES)):
                    to = start + (at // LANES + 2 * pair) * 8
                    both = [
                        values[:, (2 * pair + one) * LANES : (2 * pair + one + 1) * LANES].reshape(
                            nd * nh, 8, LANES
                        )
                        for one in range(2)
                    ]
                    part = jnp.concatenate(both, axis=1).astype(BFLOAT)
                    G[:, :, :, :, to : to + 16, :] = part.reshape(Z, X, Y, C, 16, LANES)
            elif name[0] == "e":
                part = None
                for block in range(4):
                    place = ones_where(
                        iota((4 * C_ATT, C_ATT), 0) == 4 * iota((4 * C_ATT, C_ATT), 1) + block, FLOAT
                    )
                    term = exact(place, values[:, block * LANES : (block + 1) * LANES])
                    part = term if part is None else part + term
                at = SMALL[name]
                R.small[:, :, at : at + 16, :] = part.reshape(nd, nh, 16, LANES)
            elif name[0] == "q":
                getattr(R, "g_" + name)[...] = values

        def emit_squeezes():
            both = [part[...].reshape(nd * nh, 8, LANES) for part in (R.g_q1, R.g_q2)]
            part = jnp.concatenate(both, axis=1)
            at = SMALL[tag.q]
            R.small[:, :, at : at + 16, :] = part.reshape(nd, nh, 16, LANES)

        class SmallScatter:
            def __init__(self, start, count):
                self.rows = pl.ds(start, count)

            def start(self):
                send, self.receive = new_sem(), new_sem()
                rows = self.rows
                for step in range(1, nd):
                    to = lax.rem(d + step, nd)
                    source, target = R.small.at[to, h, rows], R.small_in.at[d, rows]
                    remote(source, target, send, self.receive, (to, h)).start()
                late.append(lambda: wait_for(R.small_in.at[pl.ds(0, nd - 1), rows], send))

            def finish(self):
                wait_for(R.small_in.at[pl.ds(0, nd - 1), self.rows], self.receive)
                total = R.small[d, h, self.rows]
                for step in range(1, nd):
                    total = total + R.small_in[lax.rem(d + step, nd), self.rows]
                return total

        def emit_split(name, g):
            start, count = table[name]
            rows = per_dev(name)
            group = nh * rows

            def body(j, _):
                zz, xx = lax.div(j, 2) + g * (Z // 2), lax.rem(j, 2)
                at = pl.ds(pl.multiple_of(j * group, group), group)
                both = [
                    R.grad[at, block * LANES : (block + 1) * LANES].reshape(nh, rows, LANES)
                    for block in range(2)
                ]
                part = jnp.concatenate(both, axis=1).astype(BFLOAT)
                G[zz, xx, :, :, start : start + count, :] = part.reshape(Y, C, count, LANES)
                return 0

            lax.fori_loop(0, nd // 2, body, 0)

        def deliver(name):
            rows, blocks = per_dev(name), SHAPES[name][1] // LANES
            order = ones_where(shuffle(rows * blocks, rows, blocks, back=True), FLOAT)
            getattr(R, "d_" + name)[...] = exact(order, scattered(name))

        def range_of(*parts):
            return (table[parts[0]][0], table[parts[-1]][0] + table[parts[-1]][1])

        gather_first = Gather(*range_of(tag.r1, tag.gs), direct=True)
        def pieces(kind):
            def halves(name):
                start, stop = range_of(name)
                middle = start + -(-(stop - start) // 32) * 16
                return kind(start, middle), kind(middle, stop)

            parts = types.SimpleNamespace(
                s1=kind(*range_of(tag.s1)),
                o1=kind(*range_of(tag.o1)),
                r1=kind(*range_of(tag.r1)),
                r2=kind(*range_of(tag.r2)),
                o2=kind(*range_of(tag.o2)),
            )
            parts.sha, parts.shb = halves(tag.sh)
            parts.s2a, parts.s2b = halves(tag.s2)
            parts.s1a, parts.s1b = halves(tag.s1)
            return parts

        got = pieces(Gather)
        got.small = Gather(*range_of(tag.q, tag.e2))
        sums = pieces(Scatter)
        sums.r1 = Scatter(*range_of(tag.r1), direct=True)
        small_two, small_one = SmallScatter(0, 16), SmallScatter(16, 32)
    else:

        def emit(name, at, values):
            getattr(R, "d_" + name)[:, at : at + values.shape[1]] = values

        def emit_split(name, g):
            half = R.grad.shape[0]
            getattr(R, "d_" + name)[g * half : (g + 1) * half, :] = R.grad[...]

    def vector(ref, at, length):
        row = at // LANES
        return jnp.concatenate([ref[row + k : row + k + 1, :] for k in range(length // LANES)], axis=1)

    def store_vector(m, ref, at, values):
        row = at // LANES
        for k in range(values.shape[1] // LANES):
            part = values[:, k * LANES : (k + 1) * LANES]
            ref[row + k : row + k + 1, :] = part if m == 0 else ref[row + k : row + k + 1, :] + part

    def over_images(m, body):
        def step(i, _):
            body(m * MB + i)
            return 0

        lax.fori_loop(0, MB, step, 0)

    one = types.SimpleNamespace(
        suffix="", W=H, px=cfg.rows * H, hp=(cfg.rows + 2) * H, place=first, mk=R.mk1, edge=R.edge1, p1=R.p1,
        a3=R.a3, p2=R.p2, s=R.s, dp2=R.dp2, dmix=R.dmix, dy1=R.dmix, dp1=R.dp1, c1=R.c_n1, c2=R.c_n2, group=1,
        split=R.w_s1, squeeze=R.w_q1, expand=R.w_e1, att=R.att1, dgap=R.dgap1, count=0, keep=R.keep1, k="1",
    )
    two = types.SimpleNamespace(
        suffix="b", W=H // 2, px=cfg.rows * H // 4, hp=(cfg.rows // 2 + 2) * H // 2, place=second, mk=R.mk2,
        edge=R.edge2, p1=R.p1b, a3=R.a3b, p2=R.p2b, s=R.sb, dp2=R.dp2b, dmix=R.dmixb, dy1=R.dmixb, dp1=R.dp1b,
        c1=R.c_n1b, c2=R.c_n2b, group=MB, split=R.w_s2, squeeze=R.w_q2, expand=R.w_e2, att=R.att2,
        dgap=R.dgap2, count=2, keep=R.keep2, k="2",
    )
    px1, px2 = one.px, two.px
    edge_rows = H

    def images_of(m):
        return pl.ds(m * MB, MB)

    def build_masks(block):
        bits = block.W.bit_length() - 1
        shape = (block.hp, LANES)
        pixel = iota(shape, 0)
        column = pixel & (block.W - 1)
        place = iota(block.edge.shape[1:], 0) & (block.W - 1)
        block.edge[0] = ones_where(place != 0, FLOAT)
        block.edge[1] = ones_where(place != block.W - 1, FLOAT)
        row = (pixel >> bits) - 1 + h * (block.px // block.W)
        for i in range(NIM):
            limit = (H - STEP * (2 - R.groups[i])) // (1 if block is one else 2)
            inside_grid = (row >= 0) & (row < limit) & (column < limit)
            block.mk[i] = ones_where(inside_grid, FLOAT)

    def clear(ref):
        ref[...] = jnp.zeros(ref.shape, ref.dtype)

    def totals(m, kinds, columns):
        return [
            jnp.sum(R.acc[m, kind, :, :columns], axis=0, keepdims=True) for kind in range(kinds)
        ]

    def clear_acc(m, kinds, columns):
        for kind in range(kinds):
            R.acc[m, kind, :, :columns] = jnp.zeros((8, columns), FLOAT)

    def chunk_of(columns):
        return 32 if columns <= 512 else 16

    def stat_pass(m, source, start, px, columns, mk, mask_start):
        chunk = chunk_of(columns)
        clear_acc(m, 2, columns)

        def body(i):
            total, square = R.acc[m, 0, :, :columns], R.acc[m, 1, :, :columns]
            for t in range(0, px, chunk):
                v = source[i, start + t : start + t + chunk, :]
                vm = v * widen(mk[i, mask_start + t : mask_start + t + chunk, :], columns)
                total = total + fold(vm)
                square = square + fold(vm * v)
            R.acc[m, 0, :, :columns] = total
            R.acc[m, 1, :, :columns] = square

        over_images(m, body)
        return totals(m, 2, columns)

    def inverse_count(block, m, columns):
        return widen(R.counts[block.count + m : block.count + m + 1, :], columns)

    def norm_coef(m, coef, total, at, columns, block, offset):
        gain, shift = vector(R.gains, offset, columns), vector(R.shifts, offset, columns)
        inverse = inverse_count(block, m, columns)
        step = columns // LANES
        centre = take(total, at, columns) * inverse
        scaled = lax.rsqrt(take(total, at + step, columns) * inverse - centre * centre + EPSILON)
        coef[m, 0:1, :] = gain * scaled
        coef[m, 1:2, :] = shift - centre * (gain * scaled)
        coef[m, 2:3, :] = scaled
        coef[m, 3:4, :] = -centre * scaled

    def norm_coef_back(m, coef, total, at_sum, at_along, columns, block, offset):
        inverse = inverse_count(block, m, columns)
        summed, along = take(total, at_sum, columns), take(total, at_along, columns)
        scale = -coef[m, 0:1, :] * inverse
        coef[m, 4:5, :] = scale * (summed + along * coef[m, 3:4, :])
        coef[m, 5:6, :] = scale * along * coef[m, 2:3, :]
        store_vector(m, R.all_shifts, offset, summed)
        store_vector(m, R.all_gains, offset, along)

    class Halo:
        def __init__(self, down=None, up=None):
            self.ways = []
            for pair, step in ((down, 1), (up, -1)):
                if pair is not None:
                    sends = h < nh - 1 if step == 1 else h > 0
                    gets = h > 0 if step == 1 else h < nh - 1
                    copy = remote(pair[0], pair[1], new_sem(), new_sem(), (d, h + step))
                    self.ways.append((sends, gets, copy))

        def start(self):
            for sends, _, copy in self.ways:
                pl.when(sends)(copy.start)
            late.append(self.sent)

        def finish(self):
            for _, gets, copy in self.ways:
                pl.when(gets)(copy.wait_recv)

        def sent(self):
            for sends, _, copy in self.ways:
                pl.when(sends)(copy.wait_send)
            self.ways = []

    def rims(m, block, ref):
        image, width = images_of(m), block.W
        return Halo(
            (ref.at[image, pl.ds(block.px, width)], ref.at[image, pl.ds(0, width)]),
            (ref.at[image, pl.ds(width, width)], ref.at[image, pl.ds(block.hp - width, width)]),
        )

    def clear_rim(block, ref):
        shape = (NIM, block.W, ref.shape[-1])

        @pl.when(h == 0)
        def _():
            ref[:, : block.W, :] = jnp.zeros(shape, ref.dtype)

        @pl.when(h == nh - 1)
        def _():
            ref[:, block.hp - block.W :, :] = jnp.zeros(shape, ref.dtype)

    def activate(m, block):
        half = C_MID // 2

        def body(i):
            mask = block.mk[i]
            for g in range(2):
                cols = slice(g * half, (g + 1) * half)
                value = block.c1[m, 0:1, cols] * block.p1[i, :, cols] + block.c1[m, 1:2, cols]
                value = value * sigmoid(value) * mask
                if block is one:
                    R.a_sum[m, :, cols] = R.a_sum[m, :, cols] + fold(
                        value[block.W : block.W + block.px]
                    )
                at = 3 * g * half
                left = pltpu.roll(value, 1, 0) * block.edge[0, : block.hp]
                right = pltpu.roll(value, block.hp - 1, 0) * block.edge[1, : block.hp]
                block.a3[i, :, at : at + half] = left.astype(BFLOAT)
                block.a3[i, :, at + half : at + 2 * half] = value.astype(BFLOAT)
                block.a3[i, :, at + 2 * half : at + 3 * half] = right.astype(BFLOAT)

        over_images(m, body)

    def rows_of(ref, i, count, start, rows, cols):
        part = ref[pl.ds(i, count), start : start + rows, cols]
        return part.reshape(count * rows, part.shape[-1])

    def convolve(m, block):
        half = C_MID // 2
        for g in range(2):
            cols = slice(3 * g * half, 3 * (g + 1) * half)
            taps = [
                rows_of(block.a3, m * MB, MB, dy * block.W, block.px, cols) for dy in range(3)
            ]
            matrix = block.split[9 * g * half : 9 * (g + 1) * half, :]
            result = dot(jnp.concatenate(taps, axis=1), matrix)
            block.p2[images_of(m), :, g * C_MID : (g + 1) * C_MID] = result.reshape(
                MB, block.px, C_MID
            )

    def split_activate(m, block):
        columns = 2 * C_MID

        def body(i):
            gap = jnp.zeros((8, C_MID), FLOAT)
            for t in range(0, block.px, 32):
                at = slice(t, t + 32)
                mask = widen(block.mk[i, block.W + t : block.W + t + 32, :], columns)
                value = block.c2[m, 0:1, :] * block.p2[i, at, :] + block.c2[m, 1:2, :]
                value = value * sigmoid(value) * mask
                block.s[i, at, :] = value
                gap = gap + fold(value[:, :C_MID] + value[:, C_MID:])
            R.image_sums[i, :, :C_MID] = gap

        over_images(m, body)

    def image_rows(m, columns):
        return [
            jnp.sum(R.image_sums[i, :, :columns], axis=0, keepdims=True)
            for i in range(m * MB, (m + 1) * MB)
        ]

    def inverse_area(block, i):
        limit = (H - STEP * (2 - R.groups[i])) // (1 if block is one else 2)
        side = jnp.full((1, C_MID), limit.astype(FLOAT))
        return 1.0 / (side * side)

    def attend(m, block, window_gap, window_norm):
        suffix = block.suffix
        gap, norm = Exchange(tag.gap + suffix, m), Exchange(tag.na + suffix, m)
        split_activate(m, block)
        gap.start(image_rows(m, C_MID))
        window_gap()
        total = yield from gap.finish()
        keep = block.keep.at[m]
        for k in range(MB):
            keep[0, k : k + 1, :C_MID] = take(total, 2 * k, C_MID) * inverse_area(block, m * MB + k)
        before = exact(keep[0, :, :C_MID], block.squeeze[...])
        norm.start(
            [
                jnp.sum(before, axis=0, keepdims=True),
                jnp.sum(before * before, axis=0, keepdims=True),
            ]
        )
        window_norm()
        total = yield from norm.finish()
        count = MB * nd
        centre = total[0:1] / count
        scaled = lax.rsqrt(total[1:2] / count - centre * centre + EPSILON)
        normal = (before - centre) * scaled
        gain = vector(R.gains, block.place.attend, C_ATT)
        shift = vector(R.shifts, block.place.attend, C_ATT)
        normed = gain * normal + shift
        hidden = normed * sigmoid(normed)
        keep[1, :, :C_ATT] = normal
        keep[2, :, :C_ATT] = normed
        keep[3, :, :C_ATT] = hidden
        keep[4, 0:1, :C_ATT] = gain * scaled
        logits = exact(hidden, block.expand[...]) + vector(R.shifts, block.place.bias, 2 * C_MID)
        gap_logit = logits[:, :C_MID] - logits[:, C_MID:]
        keep[5, :, :] = jnp.concatenate([sigmoid(gap_logit), sigmoid(-gap_logit)], axis=1)
        for k in range(MB):
            block.att[m * MB + k] = jnp.broadcast_to(keep[5, k : k + 1, :], (8, 2 * C_MID))

    def mix(m, block, target, start):
        def body(i):
            for t in range(0, block.px, 32):
                at = slice(t, t + 32)
                value = (
                    block.att[i, 0:1, :C_MID] * block.s[i, at, :C_MID]
                    + block.att[i, 0:1, C_MID:] * block.s[i, at, C_MID:]
                )
                target[i, start + t : start + t + 32, :] = value.astype(BFLOAT)

        over_images(m, body)

    def attend_back(m, block, window_att, window_norm):
        suffix = block.suffix

        def body(i):
            parts = [jnp.zeros((8, C_MID), FLOAT)] * 2
            for t in range(0, block.px, 32):
                at = slice(t, t + 32)
                grad = block.dmix[i, at, :]
                for j in range(2):
                    parts[j] = parts[j] + fold(grad * block.s[i, at, j * C_MID : (j + 1) * C_MID])
            R.image_sums[i] = jnp.concatenate(parts, axis=1)

        over_images(m, body)
        heights, norm = Exchange(tag.datt + suffix, m), Exchange(tag.dna + suffix, m)
        heights.start(image_rows(m, 2 * C_MID))
        window_att()
        total = yield from heights.finish()
        keep = block.keep.at[m]
        for k in range(MB):
            keep[6, k : k + 1, :] = take(total, 4 * k, 2 * C_MID)
        att = keep[5]
        weighted = att * keep[6]
        both = weighted[:, :C_MID] + weighted[:, C_MID:]
        grad_logits = weighted - att * jnp.concatenate([both, both], axis=1)
        keep[6] = grad_logits
        grad_hidden = exact(grad_logits, block.expand[...], NT)
        grad_normed = grad_hidden * slope_of(keep[2, :, :C_ATT])
        normal = keep[1, :, :C_ATT]
        norm.start(
            [
                jnp.sum(grad_normed, axis=0, keepdims=True),
                jnp.sum(grad_normed * normal, axis=0, keepdims=True),
                jnp.sum(grad_logits, axis=0, keepdims=True),
            ]
        )
        window_norm()
        total = yield from norm.finish()
        count = MB * nd
        store_vector(m, R.all_shifts, block.place.attend, total[0:1])
        store_vector(m, R.all_gains, block.place.attend, total[1:2])
        store_vector(m, R.all_shifts, block.place.bias, take(total, 2, 2 * C_MID))
        grad_before = keep[4, 0:1, :C_ATT] * (grad_normed - (total[0:1] + normal * total[1:2]) / count)
        keep[7, :, :C_ATT] = grad_before
        grad_gap = exact(grad_before, block.squeeze[...], NT)
        for k in range(MB):
            row = grad_gap[k : k + 1, :] * inverse_area(block, m * MB + k)
            block.dgap[m * MB + k] = jnp.broadcast_to(row, (8, C_MID))

    def small_grads(block, squeeze):
        left, right, wide = (0, 7, C_ATT) if squeeze else (3, 6, 2 * C_MID)
        tall = C_MID if squeeze else C_ATT
        total = None
        for m in range(MICRO):
            term = exact(block.keep[m, left, :, :tall], block.keep[m, right, :, :wide], TN)
            total = term if total is None else total + term
        emit((tag.q if squeeze else tag.e) + block.k, 0, total * share)

    def split_back(m, block):
        clear_acc(m, 2, 2 * C_MID)

        def body(i):
            for j in range(2):
                cols = slice(j * C_MID, (j + 1) * C_MID)
                total, along = R.acc[m, 0, :, cols], R.acc[m, 1, :, cols]
                for t in range(0, block.px, 32):
                    at = slice(t, t + 32)
                    mask = widen(block.mk[i, block.W + t : block.W + t + 32, :], C_MID)
                    raw = block.p2[i, at, cols]
                    value = block.c2[m, 0:1, cols] * raw + block.c2[m, 1:2, cols]
                    grad = block.att[i, 0:1, cols] * block.dmix[i, at, :] + block.dgap[i, 0:1, :]
                    grad = grad * slope_of(value) * mask
                    block.s[i, at, cols] = grad
                    total = total + fold(grad)
                    along = along + fold(
                        grad * (block.c2[m, 2:3, cols] * raw + block.c2[m, 3:4, cols])
                    )
                R.acc[m, 0, :, cols] = total
                R.acc[m, 1, :, cols] = along

        over_images(m, body)

    def norm_back(m, block_px, grad, coef, raw, raw_start, mk, mask_start, target, start, columns, sums_=False):
        chunk = chunk_of(columns)
        if sums_:
            R.acc[m, 2, :, :columns] = jnp.zeros((8, columns), FLOAT)

        def body(i):
            for t in range(0, block_px, chunk):
                mask = widen(mk[i, mask_start + t : mask_start + t + chunk, :], columns)
                value = (
                    coef[m, 0:1, :] * grad[i, t : t + chunk, :]
                    + coef[m, 4:5, :]
                    + coef[m, 5:6, :] * raw[i, raw_start + t : raw_start + t + chunk, :]
                )
                value = (value * mask).astype(BFLOAT)
                target[i, start + t : start + t + chunk, :] = value
                if sums_:
                    R.acc[m, 2, :, :columns] = R.acc[m, 2, :, :columns] + fold(value.astype(FLOAT))

        over_images(m, body)

    def mean_activation():
        return 0.5 * (R.centre[0:1, :] + R.centre[1:2, :])

    def product_of_means(g):
        half = C_MID // 2
        cols = slice(g * C_MID, (g + 1) * C_MID)
        eye = iota((half, half), 0) == iota((half, half), 1)
        row = jnp.broadcast_to(mean_activation()[:, g * half : (g + 1) * half], (half, half))
        column = jnp.sum(jnp.where(eye, row, 0.0), axis=1, keepdims=True)
        return column * (R.grad_sum[0:1, cols] + R.grad_sum[1:2, cols])

    def mean_term():
        half = C_MID // 2
        rows = SHAPES[tag.s1][0] // (nd * nh)
        index = d * nh + h
        low = index * rows < 9 * half
        mean = mean_activation()
        centre = jnp.where(low, mean[:, :half], mean[:, half:])
        sums_ = R.grad_sum[2:3, :] + R.grad_sum[3:4, :]
        sums_ = jnp.where(low, sums_[:, :C_MID], sums_[:, C_MID:])
        shape = (2 * rows, LANES)
        row = iota(shape, 0)
        hit = iota(shape, 1) == ((index * rows + (row >> 1)) & (half - 1))
        column = jnp.sum(
            jnp.where(hit, jnp.broadcast_to(centre, shape), 0.0), axis=1, keepdims=True
        )
        odd = (row & 1) == 1
        return column * jnp.where(
            odd, jnp.broadcast_to(sums_[:, LANES:], shape), jnp.broadcast_to(sums_[:, :LANES], shape)
        )

    def kernel_grad(block, g):
        half = C_MID // 2
        images = MB if block.group == 1 else NIM
        for dy in range(3):
            at = slice(3 * dy * half, 3 * (dy + 1) * half)
            total = None
            for i in range(0, NIM, images):
                taps = rows_of(
                    block.a3, i, images, dy * block.W, block.px, slice(3 * g * half, 3 * (g + 1) * half)
                )
                grad = rows_of(
                    block.dp2, i, images, block.W, block.px, slice(g * C_MID, (g + 1) * C_MID)
                )
                term = dot(taps, grad, TN)
                total = term if total is None else total + term
            if inside and block is one:
                total = total - jnp.concatenate([product_of_means(g)] * 3, axis=0)
            R.grad[at, :] = total

    def convolve_back(m, block):
        half = C_MID // 2
        clear_acc(m, 2, C_MID)

        def body(i, count):
            rows = count * block.px
            for g in range(2):
                cols = slice(g * half, (g + 1) * half)
                total = None
                for dy in range(3):
                    grad = rows_of(
                        block.dp2, i, count, (2 - dy) * block.W, block.px, slice(g * C_MID, (g + 1) * C_MID)
                    )
                    at = 9 * g * half + 3 * dy * half
                    term = dot(grad, block.split[at : at + 3 * half, :], NT)
                    total = term if total is None else total + term
                value = (
                    total[:, half : 2 * half]
                    + pltpu.roll(total[:, :half], rows - 1, 0) * block.edge[1, :rows]
                    + pltpu.roll(total[:, 2 * half :], 1, 0) * block.edge[0, :rows]
                )
                raw = rows_of(block.p1, i, count, block.W, block.px, cols)
                mask = rows_of(block.mk, i, count, block.W, block.px, slice(0, LANES))
                before = block.c1[m, 0:1, cols] * raw + block.c1[m, 1:2, cols]
                value = value * slope_of(before) * mask
                block.dy1[pl.ds(i, count), :, cols] = value.reshape(count, block.px, half)
                normal = block.c1[m, 2:3, cols] * raw + block.c1[m, 3:4, cols]
                R.acc[m, 0, :, cols] = R.acc[m, 0, :, cols] + fold(value)
                R.acc[m, 1, :, cols] = R.acc[m, 1, :, cols] + fold(value * normal)

        if block.group == 1:
            over_images(m, lambda i: body(i, 1))
        else:
            body(m * MB, MB)

    def splat_back(m, block, window_att, window_norm, window_split, window_halo, window_reduce):
        suffix = block.suffix
        yield from attend_back(m, block, window_att, window_norm)
        split_back(m, block)
        exchange = Exchange(tag.dn2 + suffix, m)
        exchange.start(totals(m, 2, 2 * C_MID))
        window_split()
        total = yield from exchange.finish()
        norm_coef_back(m, block.c2, total, 0, 4, 2 * C_MID, block, block.place.split)
        norm_back(
            m, block.px, block.s, block.c2, block.p2, 0, block.mk, block.W, block.dp2, block.W, 2 * C_MID,
            sums_=block is one,
        )
        block.halo[m] = rims(m, block, block.dp2)
        block.halo[m].start()
        if block is one:
            R.grad_sum[m : m + 1, :] = jnp.sum(R.acc[m, 2, :, : 2 * C_MID], axis=0, keepdims=True)
        window_halo()
        yield
        block.halo[m].finish()
        convolve_back(m, block)
        exchange = Exchange(tag.dn1 + suffix, m)
        sums_ = totals(m, 2, C_MID)
        if block is one:
            sums_.append(R.grad_sum[m : m + 1, :])
        exchange.start(sums_)
        window_reduce()
        total = yield from exchange.finish()
        if block is one:
            R.grad_sum[2 + m : 3 + m, :] = take(total, 4, 2 * C_MID)
        norm_coef_back(m, block.c1, total, 0, 2, C_MID, block, block.place.reduce)
        norm_back(
            m, block.px, block.dy1, block.c1, block.p1, block.W, block.mk, block.W, block.dp1, 0, C_MID
        )

    def nothing():
        pass

    def when_last(m, *steps):
        def window():
            if m == MICRO - 1:
                for step in steps:
                    step()

        return window

    def step_of(*parts):
        def step():
            if inside:
                for name in parts:
                    getattr(sums, name).step()

        return step

    def fetch(*parts):
        def step():
            if inside:
                for name in parts:
                    getattr(got, name).step()

        return step

    def run(*steps):
        for step in steps:
            step()

    def unpack(how, *parts):
        def step():
            if inside:
                for name in parts:
                    how(name)

        return step

    def hand_out(*parts):
        def step():
            if inside:
                for name in parts:
                    deliver(name)

        return step

    def outer(m, ref, columns):
        return ref[images_of(m)].reshape(MB * px2, columns)

    def product_out(m, source, inner, matrix, target):
        for at in range(0, C_OUT, 256):
            target[images_of(m), :, at : at + 256] = dot(
                outer(m, source, inner), matrix[:, at : at + 256]
            ).reshape(MB, px2, 256)

    def grad_outer(name, source, inner, grad):
        def step():
            left = source[...].reshape(NIM * px2, inner)
            for at in range(0, C_OUT, 256):
                part = grad[:, :, at : at + 256].reshape(NIM * px2, 256)
                emit(name, at, dot(left, part, TN))

        return step

    def grad_reduce_two():
        left = R.l1[...].reshape(NIM * px2, C_OUT)
        right = R.dp1b[...].reshape(NIM * px2, C_MID)
        for at in range(0, C_MID, LANES):
            emit(tag.r2, at, dot(left, right[:, at : at + LANES], TN))

    def grad_split(block):
        def step():
            for g in range(2):
                kernel_grad(block, g)
                emit_split(tag.s + block.k, g)

        return step

    def gradients_sent():
        if inside:
            gather_first.sent()
            for gather in vars(got).values():
                gather.sent()

    halo_x = Halo(
        (R.images.at[:, pl.ds(px1 - edge_rows, edge_rows)], R.xh.at[:, pl.ds(0, edge_rows)]),
        (R.images.at[:, pl.ds(0, edge_rows)], R.xh.at[:, pl.ds(one.hp - edge_rows, edge_rows)]),
    )
    barrier = pltpu.get_barrier_semaphore()
    partners = 0
    groups = [every] if small_mesh else [along_height, plane] + along_dp + depth
    for count, me, peer in groups:
        for step in range(1, count):
            to = peer(lax.rem(me + step, count))
            pl.semaphore_signal(barrier, inc=1, device_id=to, device_id_type=MESH)
        partners += count - 1
    load_x = pltpu.make_async_copy(R.images, R.xh.at[:, pl.ds(edge_rows, px1)], new_sem())
    load_cot = pltpu.make_async_copy(R.cotangent, R.cot, new_sem())
    load_x.start()
    load_cot.start()
    if inside:
        pack_shards(tag.r1)
        pack_gains()
    pl.semaphore_wait(barrier, partners)
    if inside:
        gather_first.step()
    halo_x.start()
    if inside:
        pack_shards(tag.s1)
        got.s1.step()
        pack_small()
        got.small.step()
    build_masks(one)

    def pool_matrices():
        out_shape = (px2, px1 + edge_rows)
        out_pixel, in_pixel = iota(out_shape, 0), iota(out_shape, 1)
        down = (in_pixel >> 5) - 2 * (out_pixel >> 4)
        along = (in_pixel & 31) - 2 * (out_pixel & 15) + 1
        R.pool3[...] = ones_where((down >= 0) & (down < 3) & (along >= 0) & (along < 3))
        out_shape = (px2, px1)
        out_pixel, in_pixel = iota(out_shape, 0), iota(out_shape, 1)
        cell = ((in_pixel >> 6) == (out_pixel >> 4)) & (((in_pixel & 31) >> 1) == (out_pixel & 15))
        R.pool2[...] = jnp.where(cell, 0.25, 0.0).astype(FLOAT).astype(BFLOAT)

    def spread_matrices():
        back_shape = (px1, px2)
        in_pixel, out_pixel = iota(back_shape, 0), iota(back_shape, 1)
        cell = ((in_pixel >> 6) == (out_pixel >> 4)) & (((in_pixel & 31) >> 1) == (out_pixel & 15))
        R.spread2[...] = jnp.where(cell, 0.25, 0.0).astype(FLOAT).astype(BFLOAT)
        back_shape = (px1, px2 + two.W)
        in_pixel, out_pixel = iota(back_shape, 0), iota(back_shape, 1)
        down = (in_pixel >> 5) + 1 - 2 * (out_pixel >> 4)
        along = (in_pixel & 31) + 1 - 2 * (out_pixel & 15)
        R.spread3[...] = ones_where((down >= 0) & (down < 3) & (along >= 0) & (along < 3))

    pool_matrices()
    clear_rim(one, R.xh)
    if inside:
        gather_first.step()
    clear(R.a_sum)
    clear(R.keep1)
    clear(R.keep2)
    load_x.wait()
    halo_x.finish()
    if inside:
        gather_first.finish()
        unpack_rows(tag.r1)
        unpack_gains()

    def window_start():
        if inside:
            got.s1.step()
            got.small.step()
            pack_shards(tag.o1, tag.sh)
            got.o1.step()
            pack_shards(tag.r2, tag.s2, tag.o2)
        build_masks(two)
        clear_rim(two, R.p1b)

    def window_split_sums():
        fetch(tag.o1, tag.small, tag.sha)()
        spread_matrices()
        clear_rim(one, R.dp2)
        clear_rim(two, R.dp2b)

        @pl.when(h == 0)
        def _():
            R.v1[:, :edge_rows, :] = jnp.zeros((NIM, edge_rows, C_MID), BFLOAT)

        @pl.when(h == nh - 1)
        def _():
            R.dq[:, px2:, :] = jnp.zeros((NIM, two.W, C_MID), BFLOAT)

    def window_gap():
        fetch(tag.sha, tag.shb, tag.o1)()
        if inside:
            got.small.finish()
            unpack_attention()

    def window_mix():
        fetch(tag.shb, tag.r2, tag.s2a, tag.o1, tag.sha)()
        if inside:
            unpack_pairs(tag.o1)
        fetch(tag.shb)()
        if inside:
            unpack_rows(tag.sh)

    def window_second_conv():
        fetch(tag.s2b, tag.o2, tag.s2a, tag.s2b)()
        if inside:
            unpack_split(tag.s2)

    def first_sum(m, i, at):
        return (
            R.c_o1[m, 0:1, :] * R.o1[i, at, :]
            + R.c_sh[m, 0:1, :] * R.csh[i, at, :]
            + (R.c_o1[m, 1:2, :] + R.c_sh[m, 1:2, :])
        )

    one.halo, two.halo = {}, {}

    def chain(m):
        mine = images_of(m)

        def body(i):
            R.p1[i] = dot(R.xh[i], R.w_r1[...])

        over_images(m, body)
        exchange = Exchange(tag.n1, m)
        cells = jnp.zeros((8, LANES), FLOAT)
        for i in range(m * MB, (m + 1) * MB):
            cells = cells + fold(R.mk1[i, one.W : one.W + px1, :])
        exchange.start(
            stat_pass(m, R.p1, one.W, px1, C_MID, R.mk1, one.W)
            + [jnp.sum(cells, axis=0, keepdims=True)]
        )

        def body(i):
            R.t1[i] = dot(R.pool2[...], R.xh[i, edge_rows : edge_rows + px1, :]).astype(BFLOAT)

        over_images(m, body)
        when_last(m, window_start)()
        total = yield from exchange.finish()
        R.counts[m : m + 1, :] = 1.0 / total[4:5, :]
        R.counts[2 + m : 3 + m, :] = 4.0 / total[4:5, :]
        norm_coef(m, R.c_n1, total, 0, C_MID, one, first.reduce)
        if inside and m == 0:
            got.s1.step()
        activate(m, one)
        if inside and m == 0:
            got.s1.finish()
            unpack_split(tag.s1)
        convolve(m, one)
        exchange = Exchange(tag.n2, m)
        exchange.start(stat_pass(m, R.p2, 0, px1, 2 * C_MID, R.mk1, one.W))
        when_last(m, window_split_sums)()
        total = yield from exchange.finish()
        norm_coef(m, R.c_n2, total, 0, 2 * C_MID, one, first.split)
        yield from attend(
            m, one, when_last(m, window_gap), when_last(m, fetch(tag.shb, tag.r2, tag.sha))
        )
        mix(m, one, R.v1, edge_rows)
        halo = Halo((R.v1.at[mine, pl.ds(px1, edge_rows)], R.v1.at[mine, pl.ds(0, edge_rows)]))
        halo.start()
        when_last(m, window_mix)()
        yield
        product_out(m, R.t1, C_IN, R.w_sh, R.csh)
        exchange = Exchange(tag.no, m)
        exchange.put(stat_pass(m, R.csh, 0, px2, C_OUT, R.mk2, two.W), 16)
        halo.finish()

        def body(i):
            R.q1[i] = (dot(R.pool3[...], R.v1[i]) * (1.0 / 9.0)).astype(BFLOAT)

        over_images(m, body)
        product_out(m, R.q1, C_MID, R.w_o1, R.o1)
        exchange.put(stat_pass(m, R.o1, 0, px2, C_OUT, R.mk2, two.W), fill=False)
        exchange.send(0)
        when_last(m, fetch(tag.r2, tag.s2a, tag.s2b))()
        total = yield from exchange.finish(
            when_last(
                m, fetch(tag.s2a, tag.s2b, tag.o2, tag.r2), unpack(unpack_rows, tag.r2) if inside else nothing
            )
        )
        norm_coef(m, R.c_o1, total, 0, C_OUT, two, first.output)
        norm_coef(m, R.c_sh, total, 16, C_OUT, two, first.shortcut)

        def body(i):
            for t in range(0, px2, 16):
                at = slice(t, t + 16)
                value = first_sum(m, i, at)
                mask = widen(R.mk2[i, two.W + t : two.W + t + 16, :], C_OUT)
                R.l1[i, at, :] = (value * sigmoid(value) * mask).astype(BFLOAT)

        over_images(m, body)
        store_one = pltpu.make_async_copy(R.l1.at[mine], R.layer_one.at[mine], new_sem())
        store_one.start()
        late.append(store_one.wait)

        R.p1b[mine, two.W : two.W + px2, :] = dot(outer(m, R.l1, C_OUT), R.w_r2[...]).reshape(
            MB, px2, C_MID
        )
        exchange = Exchange(tag.n1b, m)
        exchange.start(
            stat_pass(m, R.p1b, two.W, px2, C_MID, R.mk2, two.W)
            + [jnp.sum(R.a_sum[m], axis=0, keepdims=True)]
        )
        halo = rims(m, two, R.p1b)
        halo.start()
        when_last(m, window_second_conv)()
        total = yield from exchange.finish()
        R.centre[m : m + 1, :] = take(total, 4, C_MID) * widen(R.counts[m : m + 1, :], C_MID)
        norm_coef(m, R.c_n1b, total, 0, C_MID, two, second.reduce)
        halo.finish()
        activate(m, two)
        convolve(m, two)
        exchange = Exchange(tag.n2b, m)
        exchange.start(stat_pass(m, R.p2b, 0, px2, 2 * C_MID, R.mk2, two.W))
        when_last(m, fetch(tag.o2))()
        total = yield from exchange.finish()
        norm_coef(m, R.c_n2b, total, 0, 2 * C_MID, two, second.split)
        yield from attend(
            m,
            two,
            when_last(m, fetch(tag.o2), unpack(unpack_pairs, tag.o2) if inside else nothing),
            nothing,
        )
        mix(m, two, R.mix2, 0)
        product_out(m, R.mix2, C_MID, R.w_o2, R.o2)
        exchange = Exchange(tag.nob, m)
        exchange.start(stat_pass(m, R.o2, 0, px2, C_OUT, R.mk2, two.W))
        if m == 0:
            load_cot.wait()
        total = yield from exchange.finish()
        norm_coef(m, R.c_o2, total, 0, C_OUT, two, second.output)

        clear_acc(m, 2, C_OUT)

        def body(i):
            total, along = R.acc[m, 0], R.acc[m, 1]
            for t in range(0, px2, 16):
                at = slice(t, t + 16)
                mask = widen(R.mk2[i, two.W + t : two.W + t + 16, :], C_OUT)
                raw = R.o2[i, at, :]
                value = R.c_o2[m, 0:1, :] * raw + R.c_o2[m, 1:2, :] + R.l1[i, at, :].astype(FLOAT)
                logistic = sigmoid(value)
                R.dpo[i, at, :] = (value * logistic * mask).astype(BFLOAT)
                grad = (
                    R.cot[i, at, :].astype(FLOAT) * mask * (logistic * (1.0 + value * (1.0 - logistic)))
                )
                R.g2[i, at, :] = grad
                total = total + fold(grad)
                along = along + fold(grad * (R.c_o2[m, 2:3, :] * raw + R.c_o2[m, 3:4, :]))
            R.acc[m, 0] = total
            R.acc[m, 1] = along

        over_images(m, body)
        exchange = Exchange(tag.dnob, m)
        exchange.start(totals(m, 2, C_OUT))
        store_two = pltpu.make_async_copy(R.dpo.at[mine], R.layer_two.at[mine], new_sem())
        store_two.start()
        total = yield from exchange.finish()
        norm_coef_back(m, R.c_o2, total, 0, 8, C_OUT, two, second.output)
        store_two.wait()
        norm_back(m, px2, R.g2, R.c_o2, R.o2, 0, R.mk2, two.W, R.dpo, 0, C_OUT)
        R.dmixb[mine] = dot(outer(m, R.dpo, C_OUT), R.w_o2[...], NT).reshape(MB, px2, C_MID)
        yield from splat_back(
            m,
            two,
            when_last(
                m, gradients_sent, grad_outer(tag.o2, R.mix2, C_MID, R.dpo), step_of(tag.o2)
            ),
            when_last(m, step_of(tag.o2), lambda: small_grads(two, False)),
            when_last(
                m,
                step_of(tag.o2),
                small_two.start if inside else nothing,
                lambda: small_grads(two, True),
            ),
            when_last(m, grad_split(two), step_of(tag.s2a, tag.s2b, tag.o2)),
            when_last(m, step_of(tag.s2a), hand_out(tag.o2)),
        )

        clear_acc(m, 3, C_OUT)
        R.o2[mine] = dot(outer(m, R.dp1b, C_MID), R.w_r2[...], NT).reshape(MB, px2, C_OUT)

        def body(i):
            sums_ = [R.acc[m, kind] for kind in range(3)]
            for t in range(0, px2, 16):
                at = slice(t, t + 16)
                mask = widen(R.mk2[i, two.W + t : two.W + t + 16, :], C_OUT)
                value = first_sum(m, i, at)
                grad = (R.g2[i, at, :] + R.o2[i, at, :]) * mask * slope_of(value)
                R.g2[i, at, :] = grad
                sums_[0] = sums_[0] + fold(grad)
                sums_[1] = sums_[1] + fold(
                    grad * (R.c_o1[m, 2:3, :] * R.o1[i, at, :] + R.c_o1[m, 3:4, :])
                )
                sums_[2] = sums_[2] + fold(
                    grad * (R.c_sh[m, 2:3, :] * R.csh[i, at, :] + R.c_sh[m, 3:4, :])
                )
            for kind in range(3):
                R.acc[m, kind] = sums_[kind]

        over_images(m, body)
        exchange = Exchange(tag.dno, m)
        exchange.start(totals(m, 3, C_OUT))
        when_last(m, step_of(tag.s2b, tag.s2a), grad_reduce_two, step_of(tag.r2))()
        total = yield from exchange.finish(when_last(m, step_of(tag.r2, tag.s2b)))
        norm_coef_back(m, R.c_o1, total, 0, 8, C_OUT, two, first.output)
        norm_coef_back(m, R.c_sh, total, 0, 16, C_OUT, two, first.shortcut)
        norm_back(m, px2, R.g2, R.c_o1, R.o1, 0, R.mk2, two.W, R.dpo, 0, C_OUT)
        R.dq[mine, :px2, :] = (
            (dot(outer(m, R.dpo, C_OUT), R.w_o1[...], NT) * (1.0 / 9.0))
            .astype(BFLOAT)
            .reshape(MB, px2, C_MID)
        )
        halo = Halo(up=(R.dq.at[mine, pl.ds(0, two.W)], R.dq.at[mine, pl.ds(px2, two.W)]))
        halo.start()
        norm_back(m, px2, R.g2, R.c_sh, R.csh, 0, R.mk2, two.W, R.cot, 0, C_OUT)
        when_last(m, step_of(tag.r2, tag.s2a))()
        yield
        halo.finish()

        def body(i):
            R.dmix[i] = dot(R.spread3[...], R.dq[i])

        over_images(m, body)

        def window_split():
            R.t1[...] = (
                dot(R.cot[...].reshape(NIM * px2, C_OUT), R.w_sh[...], NT)
                .astype(BFLOAT)
                .reshape(NIM, px2, C_IN)
            )
            small_grads(one, True)
            if inside:
                emit_squeezes()
                small_one.start()

        def finish_two():
            if inside:
                R.d_e2[...] = small_two.finish()

        yield from splat_back(
            m,
            one,
            when_last(
                m,
                grad_outer(tag.o1, R.q1, C_MID, R.dpo),
                step_of(tag.o1, tag.s2b, tag.r2),
                hand_out(tag.s2),
            ),
            when_last(
                m,
                step_of(tag.o1),
                lambda: small_grads(one, False),
                grad_outer(tag.sh, R.t1, C_IN, R.cot),
                step_of(tag.sha, tag.shb),
            ),
            when_last(m, step_of(tag.o1, tag.sha), window_split, hand_out(tag.r2)),
            when_last(m, step_of(tag.shb), grad_split(one), step_of(tag.s1a, tag.s1b, tag.sha, tag.o1)),
            when_last(m, step_of(tag.s1a, tag.shb, tag.sha), hand_out(tag.o1), finish_two),
        )
        term = dot(rows_of(R.xh, m * MB, MB, edge_rows, px1, slice(0, C_IN)), rows_of(R.dp1, m * MB, MB, 0, px1, slice(0, C_MID)), TN)
        if m == 0:
            step_of(tag.s1b)()
            R.grad[:C_IN, :] = term
        else:
            emit(tag.r1, 0, R.grad[:C_IN, :] + term)

    chains = [chain(m) for m in range(MICRO)]
    while chains:
        for one_chain in list(chains):
            if next(one_chain, tag) is tag:
                chains.remove(one_chain)

    step_of(tag.r1, tag.s1a)()
    store_images = new_sem()
    own = pl.ds(edge_rows, px1)

    def image_grads(m):
        one.halo[m].sent()

        def body(i):
            value = dot(R.dp1[i], R.w_r1[...], NT) + dot(R.spread2[...], R.t1[i])
            R.dp2[i, own, :] = value.astype(BFLOAT)
            pltpu.make_async_copy(R.dp2.at[i, own], R.grad_images.at[i], store_images).start()

        over_images(m, body)

    image_grads(0)
    step_of(tag.r1, tag.s1b)()
    image_grads(1)
    step_of(tag.shb, tag.s1a)()
    hand_out(tag.sh)()
    if inside:
        sums.s1b.step()
        deliver(tag.s1)
        R.d_s1[...] = R.d_s1[...] + mean_term()
        total = small_one.finish()
        R.d_q1[...] = total[:8]
        R.d_q2[...] = total[8:16]
        R.d_e1[...] = total[16:]
    index = d * nh + h
    for full, target, length in (
        (R.all_gains, R.d_gains, GAIN_LEN // (nd * nh)),
        (R.all_shifts, R.d_shifts, SHIFT_LEN // (nd * nh)),
    ):
        start = index * length
        lane = start & (LANES - 1)
        turned = pltpu.roll(full[pl.ds(start >> 7, 8), :], lax.rem(LANES - lane, LANES), 1)
        here = iota((2, LANES), 1) < LANES - lane
        target[...] = jnp.where(here, turned[0:2], turned[1:3])
    if inside:
        sums.r1.step()
        deliver(tag.r1)
        for name, group in list(vars(sums).items()) + list(vars(got).items()):
            assert group.phase in (-1, 3), name
    wait_for(R.dp2.at[:, own], store_images)
    for wait in late:
        wait()


def per_device(nd, nh, images, size_group, cotangent, *params):
    weights, (norm_gains, norm_shifts) = params[:11], params[11:]
    devices = nd * nh
    rows = images.shape[1]
    px1 = rows * H
    px2 = px1 // 4
    hp1, hp2 = px1 + 2 * H, px2 + H
    per_rows = {name: weight.shape[0] // LANES for name, weight in zip(SHAPES, weights)}
    inside = (
        nh == 4
        and devices == 32
        and per_rows[tag.q1] == 8
        and all(inner % devices == 0 for inner, _ in SHAPES.values())
    )
    axes = (tag.dp, tag.height)
    index = lax.axis_index(axes)
    cfg = types.SimpleNamespace(nd=nd, nh=nh, inside=inside, rows=rows)

    operands, names, specs = [], [], []
    whole = pl.BlockSpec(memory_space=pltpu.VMEM)

    def operand(name, value, spec=whole):
        operands.append(value)
        names.append(name)
        specs.append(spec)

    operand(tag.groups, size_group, pl.BlockSpec(memory_space=pltpu.SMEM))
    operand(tag.images, images.reshape(NIM, px1, C_IN), pl.BlockSpec(memory_space=pl.ANY))
    operand(tag.cotangent, cotangent.reshape(NIM, px2, C_OUT), pl.BlockSpec(memory_space=pl.ANY))
    if inside:
        pieces = [
            jnp.pad(vector, (0, 2 * LANES - vector.shape[0])).reshape(2, LANES)
            for vector in (norm_gains, norm_shifts)
        ]
        operand(tag.gs, jnp.pad(jnp.concatenate(pieces, axis=0), ((0, 12), (0, 0))))
        for name, weight in zip(SHAPES, weights):
            operand(tag.a_ + name, weight.reshape(-1, LANES))
        cfg.table, total_rows = row_table(per_rows)
        summed_rows, phased_rows = sum(cfg.table[tag.r1]), cfg.table[tag.r1][0]
    else:
        for name, weight in zip(SHAPES, weights):
            full = lax.all_gather(weight, axes, axis=0, tiled=True).reshape(SHAPES[name])
            operand(tag.w_ + name, full.astype(FLOAT) if name[0] in "qe" else full)
        for name, vector, length in (
            (tag.gains, norm_gains, GAIN_ROWS),
            (tag.shifts, norm_shifts, SHIFT_ROWS),
        ):
            full = lax.all_gather(vector, axes, axis=0, tiled=True).astype(FLOAT)
            full = jnp.pad(full, (0, length * LANES - full.shape[0]))
            operand(name, full.reshape(length, LANES))

    outs = dict(
        layer_one=((NIM, px2, C_OUT), BFLOAT),
        layer_two=((NIM, px2, C_OUT), BFLOAT),
        grad_images=((NIM, px1, C_IN), BFLOAT),
    )
    for name, shape in SHAPES.items():
        outs["d_" + name] = ((per_rows[name], LANES) if inside else shape, FLOAT)
    outs[tag.d_gains] = ((2, LANES), FLOAT)
    outs[tag.d_shifts] = ((2, LANES), FLOAT)

    scratch = dict(
        xh=((NIM, hp1, C_IN), BFLOAT),
        cot=((NIM, px2, C_OUT), BFLOAT),
        mk1=((NIM, hp1, LANES), FLOAT),
        mk2=((NIM, hp2, LANES), FLOAT),
        edge1=((2, hp1, LANES), FLOAT),
        edge2=((2, MB * px2, LANES), FLOAT),
        counts=((8, LANES), FLOAT),
        all_gains=((GAIN_ROWS, LANES), FLOAT),
        all_shifts=((SHIFT_ROWS, LANES), FLOAT),
        a_sum=((MICRO, 8, C_MID), FLOAT),
        centre=((8, C_MID), FLOAT),
        grad_sum=((8, 2 * C_MID), FLOAT),
        acc=((MICRO, 3, 8, C_OUT), FLOAT),
        image_sums=((NIM, 8, 2 * C_MID), FLOAT),
        p1=((NIM, hp1, C_MID), FLOAT),
        a3=((NIM, hp1, 3 * C_MID), BFLOAT),
        p2=((NIM, px1, 2 * C_MID), FLOAT),
        s=((NIM, px1, 2 * C_MID), FLOAT),
        v1=((NIM, px1 + H, C_MID), BFLOAT),
        q1=((NIM, px2, C_MID), BFLOAT),
        t1=((NIM, px2, C_IN), BFLOAT),
        o1=((NIM, px2, C_OUT), FLOAT),
        csh=((NIM, px2, C_OUT), FLOAT),
        p1b=((NIM, hp2, C_MID), FLOAT),
        a3b=((NIM, hp2, 3 * C_MID), BFLOAT),
        p2b=((NIM, px2, 2 * C_MID), FLOAT),
        sb=((NIM, px2, 2 * C_MID), FLOAT),
        mix2=((NIM, px2, C_MID), BFLOAT),
        l1=((NIM, px2, C_OUT), BFLOAT),
        o2=((NIM, px2, C_OUT), FLOAT),
        g2=((NIM, px2, C_OUT), FLOAT),
        dpo=((NIM, px2, C_OUT), BFLOAT),
        dmixb=((NIM, px2, C_MID), FLOAT),
        dp2b=((NIM, hp2, 2 * C_MID), BFLOAT),
        dp1b=((NIM, px2, C_MID), BFLOAT),
        dq=((NIM, px2 + H // 2, C_MID), BFLOAT),
        dmix=((NIM, px1, C_MID), FLOAT),
        dp2=((NIM, hp1, 2 * C_MID), BFLOAT),
        dp1=((NIM, px1, C_MID), BFLOAT),
        grad=((9 * C_MID // 2, C_MID), FLOAT),
        pool3=((px2, px1 + H), BFLOAT),
        pool2=((px2, px1), BFLOAT),
        spread2=((px1, px2), BFLOAT),
        spread3=((px1, px2 + H // 2), BFLOAT),
        keep1=((MICRO, 8, 8, 2 * C_MID), FLOAT),
        keep2=((MICRO, 8, 8, 2 * C_MID), FLOAT),
        att1=((NIM, 8, 2 * C_MID), FLOAT),
        att2=((NIM, 8, 2 * C_MID), FLOAT),
        dgap1=((NIM, 8, C_MID), FLOAT),
        dgap2=((NIM, 8, C_MID), FLOAT),
        c_n1=((MICRO, 8, C_MID), FLOAT),
        c_n2=((MICRO, 8, 2 * C_MID), FLOAT),
        c_o1=((MICRO, 8, C_OUT), FLOAT),
        c_sh=((MICRO, 8, C_OUT), FLOAT),
        c_n1b=((MICRO, 8, C_MID), FLOAT),
        c_n2b=((MICRO, 8, 2 * C_MID), FLOAT),
        c_o2=((MICRO, 8, C_OUT), FLOAT),
    )
    for name, (count, lanes, kind) in SYNCS.items():
        for k, size in enumerate(stage_sizes(kind, nd, nh)):
            for m in range(MICRO):
                scratch["sy_" + name + str(m) + str(k)] = ((size, count, lanes), FLOAT)
    if inside:
        four = (nd // 2, 2, nh // 2, 2)
        scratch |= dict(
            pack=(four + (total_rows, LANES), BFLOAT),
            rc=(four[:3] + (summed_rows, LANES), BFLOAT),
            rp=((3,) + four[:1] + (phased_rows, LANES), BFLOAT),
            rz=((four[0] - 1, phased_rows, LANES), BFLOAT),
            rd=((devices // 2 - 1, per_rows[tag.r1], LANES), BFLOAT),
            piece=((16, LANES), FLOAT),
            small=((nd, nh, 48, LANES), FLOAT),
            small_in=((nd, 48, LANES), FLOAT),
            gains=((GAIN_ROWS, LANES), FLOAT),
            shifts=((SHIFT_ROWS, LANES), FLOAT),
            g_q1=((C_MID, C_ATT), FLOAT),
            g_q2=((C_MID, C_ATT), FLOAT),
        )
        for name, shape in SHAPES.items():
            scratch["w_" + name] = (shape, FLOAT if name[0] in "qe" else BFLOAT)

    results = pl.pallas_call(
        functools.partial(
            kernel, cfg, names + list(outs) + list(scratch) + [tag.sem]
        ),
        out_shape=[jax.ShapeDtypeStruct(shape, kind) for shape, kind in outs.values()],
        in_specs=specs,
        out_specs=[pl.BlockSpec(memory_space=pl.ANY)] * 3 + [whole] * (len(outs) - 3),
        scratch_shapes=[pltpu.VMEM(shape, kind) for shape, kind in scratch.values()]
        + [pltpu.SemaphoreType.DMA((SEMAPHORES,))],
        compiler_params=pltpu.CompilerParams(
            collective_id=0, has_side_effects=True, vmem_limit_bytes=62 * 1024 * 1024
        ),
    )(*operands)

    if inside:
        results = deliver_all(results)
    layer_one, layer_two, grad_images = results[:3]
    grads = [grad.reshape(-1) for grad in results[3:14]]
    if not inside:
        grads = [
            lax.psum_scatter(grad, axes, scatter_dimension=0, tiled=True) for grad in grads
        ]
    tails = [
        total.reshape(-1)[: vector.shape[0]] for total, vector in zip(results[14:], (norm_gains, norm_shifts))
    ]
    return (
        layer_one.reshape(cotangent.shape),
        layer_two.reshape(cotangent.shape),
        grad_images.reshape(images.shape),
        *grads,
        *tails,
    )


def copy_all(count, *refs):
    sources, targets, held, sem = refs[:count], refs[count : 2 * count], refs[2 * count : -1], refs[-1]
    loads = [pltpu.make_async_copy(sources[k], held[k], sem.at[0, k]) for k in range(count)]
    stores = [pltpu.make_async_copy(held[k], targets[k], sem.at[1, k]) for k in range(count)]
    for load in loads:
        load.start()
    for load, store in zip(loads, stores):
        load.wait()
        store.start()
    for store in stores:
        store.wait()


def deliver_all(results):
    count = len(results)
    anywhere = pl.BlockSpec(memory_space=pl.ANY)
    return pl.pallas_call(
        functools.partial(copy_all, count),
        out_shape=[jax.ShapeDtypeStruct(value.shape, value.dtype) for value in results],
        in_specs=[anywhere] * count,
        out_specs=[anywhere] * count,
        scratch_shapes=[pltpu.VMEM(value.shape, value.dtype) for value in results]
        + [pltpu.SemaphoreType.DMA((2, count))],
    )(*results)


def solution(mesh):
    shard = P(("dp", "height"))
    rows = P("dp", "height", None, None)
    return jax.shard_map(
        functools.partial(per_device, mesh.shape["dp"], mesh.shape["height"]),
        mesh=mesh,
        in_specs=(rows, P("dp"), rows) + (shard,) * 13,
        out_specs=(rows,) * 3 + (shard,) * 13,
        check_vma=False,
    )
```
